32 devices in a mesh: grp: 4 (over x, core), blk: 4 (over z), head: 2 (over y).
Axes of the slice: x: 2, y: 2, z: 4, core: 2. Of those that a mesh axis runs over, the one named last changes fastest.
Arguments:
- prompt: bfloat16 [4096, 1024], P(('grp', 'blk', 'head')), parts along dimension 0, may hold values from -6 to 6
- continued: bfloat16 [8192, 1024], P(('grp', 'blk', 'head')), parts along dimension 0, may hold values from -6 to 6
- encoded: bfloat16 [2048, 1024], P(('grp', 'blk', 'head')), parts along dimension 0, may hold values from -6 to 6
- cont_lengths: int32 [8], P('grp'), parts along dimension 0, may hold values from 1 to 1536, 2048 in all
- self_gain: bfloat16 [1024], P(('blk', 'head')), may hold values from 0.099609375 to 1.8984375
- self_shift: bfloat16 [1024], P(('blk', 'head')), may hold values from -1.75 to 1.75
- query_weight: bfloat16 [1024, 1024], P(('blk', 'head')), may hold values from -0.1875 to 0.1875
- query_bias: bfloat16 [1024], P(('blk', 'head')), may hold values from -1.75 to 1.75
- key_weight: bfloat16 [1024, 1024], P(('blk', 'head')), may hold values from -0.1875 to 0.1875
- value_weight: bfloat16 [1024, 1024], P(('blk', 'head')), may hold values from -0.1875 to 0.1875
- value_bias: bfloat16 [1024], P(('blk', 'head')), may hold values from -1.75 to 1.75
- output_weight: bfloat16 [1024, 1024], P(('blk', 'head')), may hold values from -1.5 to 1.5
- output_bias: bfloat16 [1024], P(('blk', 'head')), may hold values from -3 to 3
- cross_gain: bfloat16 [1024], P(('blk', 'head')), may hold values from 0.099609375 to 1.8984375
- cross_shift: bfloat16 [1024], P(('blk', 'head')), may hold values from -1.75 to 1.75
- probe_weight: bfloat16 [1024, 1024], P(('blk', 'head')), may hold values from -0.1875 to 0.1875
- probe_bias: bfloat16 [1024], P(('blk', 'head')), may hold values from -1.75 to 1.75
- lookup_weight: bfloat16 [1024, 1024], P(('blk', 'head')), may hold values from -0.1875 to 0.1875
- content_weight: bfloat16 [1024, 1024], P(('blk', 'head')), may hold values from -0.1875 to 0.1875
- content_bias: bfloat16 [1024], P(('blk', 'head')), may hold values from -1.75 to 1.75
- merged_weight: bfloat16 [1024, 1024], P(('blk', 'head')), may hold values from -1.5 to 1.5
- merged_bias: bfloat16 [1024], P(('blk', 'head')), may hold values from -3 to 3
- feed_gain: bfloat16 [1024], P(('blk', 'head')), may hold values from 0.099609375 to 1.8984375
- feed_shift: bfloat16 [1024], P(('blk', 'head')), may hold values from -1.75 to 1.75
- up_weight: bfloat16 [1024, 8192], P(('blk', 'head')), may hold values from -0.1875 to 0.1875
- up_bias: bfloat16 [8192], P(('blk', 'head')), may hold values from -1.75 to 1.75
- down_weight: bfloat16 [8192, 1024], P(('blk', 'head')), may hold values from -0.0625 to 0.0625
- down_bias: bfloat16 [1024], P(('blk', 'head')), may hold values from -3 to 3
- cot_prompt: bfloat16 [4096, 1024], P(('grp', 'blk', 'head')), parts along dimension 0, may hold values from -6 to 6
- cot_cont: bfloat16 [8192, 1024], P(('grp', 'blk', 'head')), parts along dimension 0, may hold values from -6 to 6
Outputs:
- out_prompt: bfloat16 [4096, 1024], P(('grp', 'blk', 'head')), parts along dimension 0
- out_cont: bfloat16 [8192, 1024], P(('grp', 'blk', 'head')), parts along dimension 0
- prompt_gradient: float32 [4096, 1024], P(('grp', 'blk', 'head')), parts along dimension 0
- cont_gradient: float32 [8192, 1024], P(('grp', 'blk', 'head')), parts along dimension 0
- encoded_gradient: float32 [2048, 1024], P(('grp', 'blk', 'head')), parts along dimension 0
- self_gain_gradient: float32 [4096], P(('grp', 'blk', 'head')), parts along dimension 0
- self_shift_gradient: float32 [4096], P(('grp', 'blk', 'head')), parts along dimension 0
- query_weight_gradient: float32 [4096, 1024], P(('grp', 'blk', 'head')), parts along dimension 0
- query_bias_gradient: float32 [4096], P(('grp', 'blk', 'head')), parts along dimension 0
- key_weight_gradient: float32 [4096, 1024], P(('grp', 'blk', 'head')), parts along dimension 0
- value_weight_gradient: float32 [4096, 1024], P(('grp', 'blk', 'head')), parts along dimension 0
- value_bias_gradient: float32 [4096], P(('grp', 'blk', 'head')), parts along dimension 0
- output_weight_gradient: float32 [4096, 1024], P(('grp', 'blk', 'head')), parts along dimension 0
- output_bias_gradient: float32 [4096], P(('grp', 'blk', 'head')), parts along dimension 0
- cross_gain_gradient: float32 [4096], P(('grp', 'blk', 'head')), parts along dimension 0
- cross_shift_gradient: float32 [4096], P(('grp', 'blk', 'head')), parts along dimension 0
- probe_weight_gradient: float32 [4096, 1024], P(('grp', 'blk', 'head')), parts along dimension 0
- probe_bias_gradient: float32 [4096], P(('grp', 'blk', 'head')), parts along dimension 0
- lookup_weight_gradient: float32 [4096, 1024], P(('grp', 'blk', 'head')), parts along dimension 0
- content_weight_gradient: float32 [4096, 1024], P(('grp', 'blk', 'head')), parts along dimension 0
- content_bias_gradient: float32 [4096], P(('grp', 'blk', 'head')), parts along dimension 0
- merged_weight_gradient: float32 [4096, 1024], P(('grp', 'blk', 'head')), parts along dimension 0
- merged_bias_gradient: float32 [4096], P(('grp', 'blk', 'head')), parts along dimension 0
- feed_gain_gradient: float32 [4096], P(('grp', 'blk', 'head')), parts along dimension 0
- feed_shift_gradient: float32 [4096], P(('grp', 'blk', 'head')), parts along dimension 0
- up_weight_gradient: float32 [4096, 8192], P(('grp', 'blk', 'head')), parts along dimension 0
- up_bias_gradient: float32 [32768], P(('grp', 'blk', 'head')), parts along dimension 0
- down_weight_gradient: float32 [32768, 1024], P(('grp', 'blk', 'head')), parts along dimension 0
- down_bias_gradient: float32 [4096], P(('grp', 'blk', 'head')), parts along dimension 0
The draws below stay inside these ranges and needn't reach their ends.
There are 4 independent parts, one for each index of `grp`. The reference program is written for one: setup_inputs(seed, part) draws one part's arguments, and reference() takes and returns one part's arrays. A program takes and returns all parts, laid end to end along the dimension named above; an argument that names none is the same for every part. Nothing has to cross between parts.
Inputs may be any that keep to these rules, and one draw needn't show every extreme that they name: `cont_lengths`: 2 continuation lengths that sum to 2048; neither is longer than 1536.
All inputs are finite; a program needn't handle non-finite values.
Results may differ from the reference program's by a relative error of at most 0.038.
Values may be sent and summed in bfloat16 or wider, within the bound.
No kernel may reach another device: no remote copies, remote signals or barrier semaphores. Data moves between devices by JAX's collectives and lax.ppermute only.
A program may use at most 448 MiB of HBM per device.

```python
import math
import jax
import jax.numpy as jnp
import numpy as np
from jax import lax

D = 1024
HEADS = 16
HD = 64
FF = 8192
PROMPT = 1024
CTOK = 2048
ENC = 512
NCONT = 2
CMOST = 1536


def block_levels(own_key, dims, cuts, smallest, top_value):
    def one(axis_at, shards_of):
        heights = jax.random.uniform(jax.random.fold_in(jax.random.fold_in(own_key, 6), axis_at), (shards_of,), jnp.float32, smallest / len(cuts), top_value / len(cuts))
        return jnp.repeat(jnp.exp(heights), dims[axis_at] // shards_of).reshape((-1,) + (1,) * (len(dims) - axis_at - 1))

    level = one(*cuts[0])
    for cut in cuts[1:]:
        level = level * one(*cut)
    return level


def profile(number_of, total, limit, lean):
    loads = [(1 << 20) // math.isqrt(grade ** lean) + 1 for grade in range(2, number_of + 1)]
    rest, counts = total - limit - (number_of - 1), [1] * (number_of - 1)
    while rest > 0:
        free = [i for i in range(number_of - 1) if counts[i] < limit]
        pool, remaining = sum([loads[i] for i in free]), rest
        for i in free:
            addition = min(limit - counts[i], max(1, remaining * loads[i] // pool), rest)
            counts[i] = counts[i] + addition
            rest = rest - addition
    return np.array([limit] + counts)


def uneven_parts(key, count, total, limit, skew):
    if count == 2:
        one = jax.random.randint(key, (), max(1, total - limit), min(limit, total - 1) + 1)
        return jnp.stack([one, total - one])
    lengths = jnp.asarray(profile(count, total, limit, skew), jnp.int32)
    couples = (count - 1) // 2
    giver, receiver = lengths[1:1 + 2 * couples:2], lengths[2:2 + 2 * couples:2]
    slack = jnp.minimum(giver - 1, limit - receiver)
    passed = jax.random.randint(jax.random.fold_in(key, 1), (couples,), 0, 1 << 20) % (slack + 1)
    lengths = lengths.at[1:1 + 2 * couples:2].set(giver - passed).at[2:2 + 2 * couples:2].set(receiver + passed)
    return lengths[jax.random.permutation(jax.random.fold_in(key, 2), count)]


def noise(rng, dims, deviation, reach, split=(), kind=jnp.bfloat16):
    values = jax.random.normal(rng, dims, jnp.float32) * deviation
    if len(split) > 0:
        values = block_levels(rng, dims, split, -0.22, 0.18) * values
    return jnp.clip(values, min=-reach, max=reach).astype(kind)


def setup_inputs(seed: int = 0, part: int = 0) -> dict:
    arg_keys = jax.random.split(jax.random.key(seed), 31)
    part_splits = jax.random.split(jax.random.fold_in(arg_keys[30], part), 31)
    prompt = noise(part_splits[0], (PROMPT, D), 1.0, 6.0, ((0, 8),))
    continued = noise(part_splits[1], (CTOK, D), 1.0, 6.0, ((0, 8),))
    encoded = noise(part_splits[2], (ENC, D), 1.0, 6.0, ((0, 8),))
    cont_lengths = uneven_parts(part_splits[3], NCONT, CTOK, CMOST, 1).astype(jnp.int32)
    self_gain = jnp.clip(1.0 + 0.18 * jax.random.normal(arg_keys[4], (D,), jnp.float32), 0.099609375, 1.8984375).astype(jnp.bfloat16)
    self_shift = noise(arg_keys[5], (D,), 0.3, 1.75, ((0, 8),))
    query_weight = noise(arg_keys[6], (D, D), D ** -0.5, 0.1875, ((0, 8),))
    query_bias = noise(arg_keys[7], (D,), 0.3, 1.75, ((0, 8),))
    key_weight = noise(arg_keys[8], (D, D), D ** -0.5, 0.1875, ((0, 8),))
    value_weight = noise(arg_keys[9], (D, D), D ** -0.5, 0.1875, ((0, 8),))
    value_bias = noise(arg_keys[10], (D,), 0.3, 1.75, ((0, 8),))
    output_weight = noise(arg_keys[11], (D, D), 16 ** -0.5, 1.5, ((0, 8),))
    output_bias = noise(arg_keys[12], (D,), 0.5, 3.0, ((0, 8),))
    cross_gain = jnp.clip(1.0 + 0.18 * jax.random.normal(arg_keys[13], (D,), jnp.float32), 0.099609375, 1.8984375).astype(jnp.bfloat16)
    cross_shift = noise(arg_keys[14], (D,), 0.3, 1.75, ((0, 8),))
    probe_weight = noise(arg_keys[15], (D, D), D ** -0.5, 0.1875, ((0, 8),))
    probe_bias = noise(arg_keys[16], (D,), 0.3, 1.75, ((0, 8),))
    lookup_weight = noise(arg_keys[17], (D, D), D ** -0.5, 0.1875, ((0, 8),))
    content_weight = noise(arg_keys[18], (D, D), D ** -0.5, 0.1875, ((0, 8),))
    content_bias = noise(arg_keys[19], (D,), 0.3, 1.75, ((0, 8),))
    merged_weight = noise(arg_keys[20], (D, D), 16 ** -0.5, 1.5, ((0, 8),))
    merged_bias = noise(arg_keys[21], (D,), 0.5, 3.0, ((0, 8),))
    feed_gain = jnp.clip(1.0 + 0.18 * jax.random.normal(arg_keys[22], (D,), jnp.float32), 0.099609375, 1.8984375).astype(jnp.bfloat16)
    feed_shift = noise(arg_keys[23], (D,), 0.3, 1.75, ((0, 8),))
    up_weight = noise(arg_keys[24], (D, FF), D ** -0.5, 0.1875, ((0, 8),))
    up_bias = noise(arg_keys[25], (FF,), 0.3, 1.75, ((0, 8),))
    down_weight = noise(arg_keys[26], (FF, D), FF ** -0.5, 0.0625, ((0, 8),))
    down_bias = noise(arg_keys[27], (D,), 0.5, 3.0, ((0, 8),))
    cot_prompt = noise(part_splits[28], (PROMPT, D), 1.0, 6.0, ((0, 8),))
    cot_cont = noise(part_splits[29], (CTOK, D), 1.0, 6.0, ((0, 8),))
    return dict(prompt=prompt, continued=continued, encoded=encoded, cont_lengths=cont_lengths, self_gain=self_gain, self_shift=self_shift, query_weight=query_weight, query_bias=query_bias, key_weight=key_weight, value_weight=value_weight, value_bias=value_bias, output_weight=output_weight, output_bias=output_bias, cross_gain=cross_gain, cross_shift=cross_shift, probe_weight=probe_weight, probe_bias=probe_bias, lookup_weight=lookup_weight, content_weight=content_weight, content_bias=content_bias, merged_weight=merged_weight, merged_bias=merged_bias, feed_gain=feed_gain, feed_shift=feed_shift, up_weight=up_weight, up_bias=up_bias, down_weight=down_weight, down_bias=down_bias, cot_prompt=cot_prompt, cot_cont=cot_cont)


@jax.custom_vjp
def low(v):
    return lax.optimization_barrier(v.astype(jnp.bfloat16)).astype(jnp.float32)

@jax.custom_vjp
def low_back(v):
    return v

def low_keep(v):
    return (low(v), None)

def low_pass(kept, grad):
    return (grad,)

def back_keep(v):
    return (v, None)

def back_low(kept, grad):
    return (low(grad),)
low.defvjp(low_keep, low_pass)
low_back.defvjp(back_keep, back_low)
highest = lax.Precision.HIGHEST
floor_value = -1e+30
PARAM_NAMES = ('self_gain', 'self_shift', 'query_weight', 'query_bias', 'key_weight', 'value_weight', 'value_bias', 'output_weight', 'output_bias', 'cross_gain', 'cross_shift', 'probe_weight', 'probe_bias', 'lookup_weight', 'content_weight', 'content_bias', 'merged_weight', 'merged_bias', 'feed_gain', 'feed_shift', 'up_weight', 'up_bias', 'down_weight', 'down_bias')

def product(left, right):
    return jnp.dot(left, right, precision=highest)

def layer_norm(rows, gain, shift):
    center = lax.optimization_barrier(jnp.mean(rows, axis=-1, keepdims=True))
    centred = rows - center
    spread = lax.optimization_barrier(jnp.mean(centred * centred, axis=-1, keepdims=True))
    return centred * lax.rsqrt(spread + 1e-05) * gain + shift

def segments(cont_lengths):
    bounds = jnp.cumsum(cont_lengths).astype(jnp.int32)
    cont_index = jnp.arange(CTOK, dtype=jnp.int32)
    later = lax.optimization_barrier(jnp.sum((cont_index[:, None] >= bounds[None, :]).astype(jnp.int32), axis=1))
    segment = jnp.concatenate([jnp.zeros((PROMPT,), jnp.int32), (1 + later).astype(jnp.int32)])
    places = jnp.concatenate([jnp.arange(PROMPT, dtype=jnp.int32), cont_index])
    return (segment, places)

def self_attention(queries, keys, values, segment, places):
    total_rows = queries.shape[0]
    block = math.gcd(total_rows, 256)
    key_heads = keys.reshape(total_rows, HEADS, HD)
    value_heads = values.reshape(total_rows, HEADS, HD)

    def one_block(args):
        query_block, seg_block, place_block = args
        query_heads = query_block.reshape(block, HEADS, HD)
        scores = jnp.einsum('qhd,khd->hqk', query_heads, key_heads, precision=highest) * HD ** (-0.5)
        scores = low_back(scores)
        from_prompt = (segment[None, :] == 0) & (seg_block[:, None] > 0)
        causal = (segment[None, :] == seg_block[:, None]) & (places[None, :] <= place_block[:, None])
        allowed = from_prompt | causal
        scores = jnp.where(allowed[None], scores, floor_value)
        top = lax.optimization_barrier(jnp.max(scores, axis=-1, keepdims=True))
        weights = jnp.exp(scores - top)
        probs = low(weights / lax.optimization_barrier(jnp.sum(weights, axis=-1, keepdims=True)))
        return jnp.einsum('hqk,khd->qhd', probs, value_heads, precision=highest).reshape(block, HEADS * HD)
    blocks = lax.map(jax.checkpoint(one_block), (queries.reshape(-1, block, HEADS * HD), segment.reshape(-1, block), places.reshape(-1, block)))
    return blocks.reshape(total_rows, HEADS * HD)

def cross_attention(probes, lookups, contents):
    total_rows = probes.shape[0]
    memory_rows = lookups.shape[0]
    block = math.gcd(total_rows, 256)
    key_heads = lookups.reshape(memory_rows, HEADS, HD)
    value_heads = contents.reshape(memory_rows, HEADS, HD)

    def one_block(probe_block):
        probe_heads = probe_block.reshape(block, HEADS, HD)
        scores = jnp.einsum('qhd,khd->hqk', probe_heads, key_heads, precision=highest) * HD ** (-0.5)
        scores = low_back(scores)
        top = lax.optimization_barrier(jnp.max(scores, axis=-1, keepdims=True))
        weights = jnp.exp(scores - top)
        probs = low(weights / lax.optimization_barrier(jnp.sum(weights, axis=-1, keepdims=True)))
        return jnp.einsum('hqk,khd->qhd', probs, value_heads, precision=highest).reshape(block, HEADS * HD)
    blocks = lax.map(jax.checkpoint(one_block), probes.reshape(-1, block, HEADS * HD))
    return blocks.reshape(total_rows, HEADS * HD)

def reference(prompt, continued, encoded, cont_lengths, self_gain, self_shift, query_weight, query_bias, key_weight, value_weight, value_bias, output_weight, output_bias, cross_gain, cross_shift, probe_weight, probe_bias, lookup_weight, content_weight, content_bias, merged_weight, merged_bias, feed_gain, feed_shift, up_weight, up_bias, down_weight, down_bias, cot_prompt, cot_cont):
    params = tuple((value.astype(jnp.float32) for value in (self_gain, self_shift, query_weight, query_bias, key_weight, value_weight, value_bias, output_weight, output_bias, cross_gain, cross_shift, probe_weight, probe_bias, lookup_weight, content_weight, content_bias, merged_weight, merged_bias, feed_gain, feed_shift, up_weight, up_bias, down_weight, down_bias)))
    segment, places = segments(cont_lengths)
    rows = jnp.concatenate([prompt, continued], axis=0).astype(jnp.float32)
    memory = encoded.astype(jnp.float32)

    def forward(rows, memory, params):
        full = dict(zip(PARAM_NAMES, params))
        normed = low(layer_norm(rows, full['self_gain'], full['self_shift']))
        queries = low(low_back(product(normed, full['query_weight']) + full['query_bias']))
        keys = low(low_back(product(normed, full['key_weight'])))
        values = low(low_back(product(normed, full['value_weight']) + full['value_bias']))
        mixed = low(low_back(self_attention(queries, keys, values, segment, places)))
        first = rows + low_back(product(mixed, full['output_weight']) + full['output_bias'])
        normed_cross = low(layer_norm(first, full['cross_gain'], full['cross_shift']))
        probes = low(low_back(product(normed_cross, full['probe_weight']) + full['probe_bias']))
        lookups = low(low_back(product(memory, full['lookup_weight'])))
        contents = low(low_back(product(memory, full['content_weight']) + full['content_bias']))
        recalled = low(low_back(cross_attention(probes, lookups, contents)))
        second = first + low_back(product(recalled, full['merged_weight']) + full['merged_bias'])
        normed_feed = low(layer_norm(second, full['feed_gain'], full['feed_shift']))
        hidden = low_back(product(normed_feed, full['up_weight']) + full['up_bias'])
        active = low(jax.nn.gelu(hidden, approximate=False))
        return second + low_back(product(active, full['down_weight']) + full['down_bias'])
    output, pull = jax.vjp(forward, rows, memory, params)
    upstream = jnp.concatenate([cot_prompt, cot_cont], axis=0).astype(jnp.float32)
    row_grads, memory_grads, param_grads = pull(upstream)
    output_low = output.astype(jnp.bfloat16)
    return (output_low[:PROMPT], output_low[PROMPT:], row_grads[:PROMPT], row_grads[PROMPT:], memory_grads, param_grads[0], param_grads[1], param_grads[2], param_grads[3], param_grads[4], param_grads[5], param_grads[6], param_grads[7], param_grads[8], param_grads[9], param_grads[10], param_grads[11], param_grads[12], param_grads[13], param_grads[14], param_grads[15], param_grads[16], param_grads[17], param_grads[18], param_grads[19], param_grads[20], param_grads[21], param_grads[22], param_grads[23])
```

```python
import functools
import math
import types

import jax
import jax.numpy as jnp
from jax import lax
from jax.experimental import pallas as pl
from jax.experimental.pallas import tpu as pltpu
from jax.sharding import PartitionSpec as P

HEADS = 16
HD = 64


floor_value = -1e30
BLK = "blk"
HEAD = "head"
GRP = "grp"
ROW_AXES = (BLK, HEAD)
ROLE_AXES = (GRP, HEAD)
ALL_AXES = (GRP, BLK, HEAD)
PARAM_NAMES = (
    "self_gain",
    "self_shift",
    "query_weight",
    "query_bias",
    "key_weight",
    "value_weight",
    "value_bias",
    "output_weight",
    "output_bias",
    "cross_gain",
    "cross_shift",
    "probe_weight",
    "probe_bias",
    "lookup_weight",
    "content_weight",
    "content_bias",
    "merged_weight",
    "merged_bias",
    "feed_gain",
    "feed_shift",
    "up_weight",
    "up_bias",
    "down_weight",
    "down_bias",
)


def layer_norm(rows, gain, shift):
    center = jnp.mean(rows, axis=-1, keepdims=True)
    centred = rows - center
    spread = jnp.mean(centred * centred, axis=-1, keepdims=True)
    return centred * lax.rsqrt(spread + 1e-05) * gain + shift


def matmul(left, right):
    return jnp.dot(left, right, preferred_element_type=jnp.float32)


def left_product(left, right):
    return jnp.einsum("rd,re->de", left, right, preferred_element_type=jnp.float32)


def right_product(left, right):
    return jnp.einsum("re,de->rd", left, right, preferred_element_type=jnp.float32)


def column_sum(values):
    return jnp.sum(values.astype(jnp.float32), axis=0)


def exact_gelu(values):
    return jax.nn.gelu(values, approximate=False)


def row_meta(global_rows, bounds, prompt_rows, cont_rows, heads_here):
    local_rows = prompt_rows + cont_rows
    span = heads_here * local_rows
    owner = global_rows // span
    inner = global_rows % span
    device = owner * heads_here + inner // local_rows
    offset = inner % local_rows
    in_prompt = offset < prompt_rows
    places = jnp.where(
        in_prompt, device * prompt_rows + offset, device * cont_rows + offset - prompt_rows
    )
    later = jnp.sum((places[:, None] >= bounds[None, :]).astype(jnp.int32), axis=1)
    segment = jnp.where(in_prompt, 0, 1 + later)
    return (segment, places)


def allowed_pairs(query_seg, query_place, key_seg, key_place):
    from_prompt = (key_seg[None, :] == 0) & (query_seg[:, None] > 0)
    causal = (key_seg[None, :] == query_seg[:, None]) & (key_place[None, :] <= query_place[:, None])
    return from_prompt | causal


def token_body(
    prompt,
    continued,
    encoded,
    cont_lengths,
    self_gain,
    self_shift,
    query_weight,
    query_bias,
    key_weight,
    value_weight,
    value_bias,
    output_weight,
    output_bias,
    cross_gain,
    cross_shift,
    probe_weight,
    probe_bias,
    lookup_weight,
    content_weight,
    content_bias,
    merged_weight,
    merged_bias,
    feed_gain,
    feed_shift,
    up_weight,
    up_bias,
    down_weight,
    down_bias,
    cot_prompt,
    cot_cont,
):
    gathered = (
        lax.all_gather(self_gain, ROW_AXES, axis=0, tiled=True),
        lax.all_gather(self_shift, ROW_AXES, axis=0, tiled=True),
        lax.all_gather(query_weight, ROW_AXES, axis=0, tiled=True),
        lax.all_gather(query_bias, ROW_AXES, axis=0, tiled=True),
        lax.all_gather(key_weight, ROW_AXES, axis=0, tiled=True),
        lax.all_gather(value_weight, ROW_AXES, axis=0, tiled=True),
        lax.all_gather(value_bias, ROW_AXES, axis=0, tiled=True),
        lax.all_gather(output_weight, ROW_AXES, axis=0, tiled=True),
        lax.all_gather(output_bias, ROW_AXES, axis=0, tiled=True),
        lax.all_gather(cross_gain, ROW_AXES, axis=0, tiled=True),
        lax.all_gather(cross_shift, ROW_AXES, axis=0, tiled=True),
        lax.all_gather(probe_weight, ROW_AXES, axis=0, tiled=True),
        lax.all_gather(probe_bias, ROW_AXES, axis=0, tiled=True),
        lax.all_gather(lookup_weight, ROW_AXES, axis=0, tiled=True),
        lax.all_gather(content_weight, ROW_AXES, axis=0, tiled=True),
        lax.all_gather(content_bias, ROW_AXES, axis=0, tiled=True),
        lax.all_gather(merged_weight, ROW_AXES, axis=0, tiled=True),
        lax.all_gather(merged_bias, ROW_AXES, axis=0, tiled=True),
        lax.all_gather(feed_gain, ROW_AXES, axis=0, tiled=True),
        lax.all_gather(feed_shift, ROW_AXES, axis=0, tiled=True),
        lax.all_gather(up_weight, ROW_AXES, axis=0, tiled=True),
        lax.all_gather(up_bias, ROW_AXES, axis=0, tiled=True),
        lax.all_gather(down_weight, ROW_AXES, axis=0, tiled=True),
        lax.all_gather(down_bias, ROW_AXES, axis=0, tiled=True),
    )
    full = types.SimpleNamespace(**dict(zip(PARAM_NAMES, gathered)))
    heads_here = lax.axis_size(HEAD)
    prompt_rows = prompt.shape[0]
    cont_rows = continued.shape[0]
    local_rows = prompt_rows + cont_rows
    span = heads_here * local_rows
    width = prompt.shape[1]
    local_heads = HEADS // heads_here
    half = local_heads * HD
    scale = HD ** (-0.5)
    bounds = jnp.cumsum(cont_lengths)
    rows = jnp.concatenate([prompt, continued], axis=0).astype(jnp.float32)
    self_gain_full = full.self_gain.astype(jnp.float32)
    self_shift_full = full.self_shift.astype(jnp.float32)
    cross_gain_full = full.cross_gain.astype(jnp.float32)
    cross_shift_full = full.cross_shift.astype(jnp.float32)
    feed_gain_full = full.feed_gain.astype(jnp.float32)
    feed_shift_full = full.feed_shift.astype(jnp.float32)
    normed = layer_norm(rows, self_gain_full, self_shift_full).astype(jnp.bfloat16)
    queries = (matmul(normed, full.query_weight) + full.query_bias).astype(jnp.bfloat16)
    keys_rows = matmul(normed, full.key_weight).astype(jnp.bfloat16)
    values_rows = (matmul(normed, full.value_weight) + full.value_bias).astype(jnp.bfloat16)
    head_queries, head_keys, head_values = (
        lax.all_to_all(queries, HEAD, split_axis=1, concat_axis=0, tiled=True),
        lax.all_to_all(keys_rows, HEAD, split_axis=1, concat_axis=0, tiled=True),
        lax.all_to_all(values_rows, HEAD, split_axis=1, concat_axis=0, tiled=True),
    )
    query_block = math.gcd(span, 512)
    query_count = span // query_block
    own_rows = lax.axis_index(BLK) * span + jnp.arange(span, dtype=jnp.int32)
    own_seg, own_place = row_meta(own_rows, bounds, prompt_rows, cont_rows, heads_here)
    query_tiles = head_queries.reshape(query_count, query_block, local_heads, HD)
    seg_tiles = own_seg.reshape(query_count, query_block)
    place_tiles = own_place.reshape(query_count, query_block)

    def key_tiles(piece_keys, piece_values):
        count = piece_keys.shape[0]
        key_block = math.gcd(count, span)
        key_count = count // key_block
        key_rows = jnp.arange(count, dtype=jnp.int32)
        key_seg, key_place = row_meta(key_rows, bounds, prompt_rows, cont_rows, heads_here)
        return (
            piece_keys.reshape(key_count, key_block, local_heads, HD),
            piece_values.reshape(key_count, key_block, local_heads, HD),
            key_seg.reshape(key_count, key_block),
            key_place.reshape(key_count, key_block),
        )

    def scores_of(query_tile, query_seg, query_place, key_tile, key_seg, key_place):
        raw = (
            jnp.einsum("qhd,khd->qhk", query_tile, key_tile, preferred_element_type=jnp.float32)
            * scale
        )
        allowed = allowed_pairs(query_seg, query_place, key_seg, key_place)[:, None, :]
        return (jnp.where(allowed, raw, floor_value), allowed)

    start_top = jnp.full((query_count, query_block, local_heads), floor_value, jnp.float32)
    start_total = jnp.zeros((query_count, query_block, local_heads), jnp.float32)
    start_sum = jnp.zeros((query_count, query_block, local_heads, HD), jnp.float32)
    piece = (
        lax.all_gather(head_keys, BLK, axis=0, tiled=True),
        lax.all_gather(head_values, BLK, axis=0, tiled=True),
    )
    tiles = key_tiles(piece[0], piece[1])

    def fold_per_query(args):
        query_tile, query_seg, query_place, running_top, running_total, running_sum = args

        def fold_per_key(state, key_args):
            key_tile, value_tile, key_seg, key_place = key_args
            top_old, total_old, sum_old = state
            scores, allowed = scores_of(
                query_tile, query_seg, query_place, key_tile, key_seg, key_place
            )
            top_new = jnp.maximum(top_old, jnp.max(scores, axis=-1))
            weights = jnp.where(allowed, jnp.exp(scores - top_new[..., None]), 0.0)
            fade = jnp.exp(top_old - top_new)
            total_new = total_old * fade + jnp.sum(weights, axis=-1)
            sum_new = sum_old * fade[..., None] + jnp.einsum(
                "qhk,khd->qhd",
                weights.astype(jnp.bfloat16),
                value_tile,
                preferred_element_type=jnp.float32,
            )
            return ((top_new, total_new, sum_new), None)

        state, unused = lax.scan(fold_per_key, (running_top, running_total, running_sum), tiles)
        return state

    top, total, summed = lax.map(
        fold_per_query, (query_tiles, seg_tiles, place_tiles, start_top, start_total, start_sum)
    )
    attended = summed / total[..., None]
    logsum = top + jnp.log(total)
    attended_low = attended.reshape(span, half).astype(jnp.bfloat16)
    mixed = lax.all_to_all(attended_low, HEAD, split_axis=0, concat_axis=1, tiled=True)
    first = rows + matmul(mixed, full.output_weight) + full.output_bias
    normed_cross = layer_norm(first, cross_gain_full, cross_shift_full).astype(jnp.bfloat16)
    probes = (matmul(normed_cross, full.probe_weight) + full.probe_bias).astype(jnp.bfloat16)
    lookups_own = matmul(encoded, full.lookup_weight).astype(jnp.bfloat16)
    contents_own = (matmul(encoded, full.content_weight) + full.content_bias).astype(
        jnp.bfloat16
    )
    lookups, contents = (
        lax.all_gather(lookups_own, ROW_AXES, axis=0, tiled=True),
        lax.all_gather(contents_own, ROW_AXES, axis=0, tiled=True),
    )
    memory_rows = lookups.shape[0]
    memory_keys = lookups.reshape(memory_rows, HEADS, HD)
    memory_values = contents.reshape(memory_rows, HEADS, HD)
    cross_block = math.gcd(local_rows, 256)
    cross_count = local_rows // cross_block
    probe_tiles = probes.reshape(cross_count, cross_block, HEADS, HD)

    def cross_scores(probe_tile):
        return (
            jnp.einsum("qhd,khd->qhk", probe_tile, memory_keys, preferred_element_type=jnp.float32)
            * scale
        )

    def cross_forward(probe_tile):
        scores = cross_scores(probe_tile)
        peak = jnp.max(scores, axis=-1, keepdims=True)
        weights = jnp.exp(scores - peak)
        weight_sum = jnp.sum(weights, axis=-1, keepdims=True)
        probs = (weights / weight_sum).astype(jnp.bfloat16)
        recalled_tile = jnp.einsum(
            "qhk,khd->qhd", probs, memory_values, preferred_element_type=jnp.float32
        )
        return (recalled_tile, (peak + jnp.log(weight_sum))[..., 0])

    recalled, cross_logsum = lax.map(cross_forward, probe_tiles)
    recalled_low = recalled.reshape(local_rows, width).astype(jnp.bfloat16)
    second = first + matmul(recalled_low, full.merged_weight) + full.merged_bias
    normed_feed = layer_norm(second, feed_gain_full, feed_shift_full).astype(jnp.bfloat16)
    hidden = matmul(normed_feed, full.up_weight) + full.up_bias
    active = exact_gelu(hidden).astype(jnp.bfloat16)
    output = second + matmul(active, full.down_weight) + full.down_bias
    output_low = output.astype(jnp.bfloat16)
    grads = types.SimpleNamespace()
    upstream = jnp.concatenate([cot_prompt, cot_cont], axis=0)
    grads.down_weight = left_product(active, upstream)
    grads.down_bias = column_sum(upstream)
    dactive = right_product(upstream, full.down_weight)
    unused, gelu_pull = jax.vjp(exact_gelu, hidden)
    dhidden = gelu_pull(dactive)[0].astype(jnp.bfloat16)
    grads.up_weight = left_product(normed_feed, dhidden)
    grads.up_bias = column_sum(dhidden)
    dnormed_feed = right_product(dhidden, full.up_weight)
    unused, feed_pull = jax.vjp(layer_norm, second, feed_gain_full, feed_shift_full)
    dsecond_part, grads.feed_gain, grads.feed_shift = feed_pull(dnormed_feed)
    dsecond = upstream.astype(jnp.float32) + dsecond_part
    dsecond_low = dsecond.astype(jnp.bfloat16)
    grads.merged_weight = left_product(recalled_low, dsecond_low)
    grads.merged_bias = column_sum(dsecond_low)
    drecalled = right_product(dsecond_low, full.merged_weight).astype(jnp.bfloat16)
    drecalled_tiles = drecalled.reshape(cross_count, cross_block, HEADS, HD)
    cross_delta = jnp.sum(drecalled_tiles.astype(jnp.float32) * recalled, axis=-1)

    def cross_backward(state, args):
        probe_tile, drecalled_tile, logsum_tile, delta_tile = args
        dlookups_acc, dcontents_acc = state
        scores = cross_scores(probe_tile)
        probs = jnp.exp(scores - logsum_tile[..., None])
        dprobs = jnp.einsum(
            "qhd,khd->qhk", drecalled_tile, memory_values, preferred_element_type=jnp.float32
        )
        dscores = (probs * (dprobs - delta_tile[..., None])).astype(jnp.bfloat16)
        dprobe_tile = (
            jnp.einsum("qhk,khd->qhd", dscores, memory_keys, preferred_element_type=jnp.float32)
            * scale
        )
        dlookups_acc = (
            dlookups_acc
            + jnp.einsum("qhk,qhd->khd", dscores, probe_tile, preferred_element_type=jnp.float32)
            * scale
        )
        dcontents_acc = dcontents_acc + jnp.einsum(
            "qhk,qhd->khd",
            probs.astype(jnp.bfloat16),
            drecalled_tile,
            preferred_element_type=jnp.float32,
        )
        return ((dlookups_acc, dcontents_acc), dprobe_tile)

    zero_memory = jnp.zeros((memory_rows, HEADS, HD), jnp.float32)
    (dlookups, dcontents), dprobes = lax.scan(
        cross_backward,
        (zero_memory, zero_memory),
        (probe_tiles, drecalled_tiles, cross_logsum, cross_delta),
    )
    mine_lookups, mine_contents = (
        lax.psum_scatter(
            dlookups.reshape(memory_rows, width).astype(jnp.bfloat16),
            ROW_AXES,
            scatter_dimension=0,
            tiled=True,
        ).astype(jnp.float32),
        lax.psum_scatter(
            dcontents.reshape(memory_rows, width).astype(jnp.bfloat16),
            ROW_AXES,
            scatter_dimension=0,
            tiled=True,
        ).astype(jnp.float32),
    )
    mine_lookups = mine_lookups.astype(jnp.bfloat16)
    mine_contents = mine_contents.astype(jnp.bfloat16)
    grads.lookup_weight = left_product(encoded, mine_lookups)
    grads.content_weight = left_product(encoded, mine_contents)
    grads.content_bias = column_sum(mine_contents)
    encoded_gradient = right_product(mine_lookups, full.lookup_weight) + right_product(
        mine_contents, full.content_weight
    )
    dprobes_low = dprobes.reshape(local_rows, width).astype(jnp.bfloat16)
    grads.probe_weight = left_product(normed_cross, dprobes_low)
    grads.probe_bias = column_sum(dprobes_low)
    dnormed_cross = right_product(dprobes_low, full.probe_weight)
    unused, cross_pull = jax.vjp(layer_norm, first, cross_gain_full, cross_shift_full)
    dfirst_part, grads.cross_gain, grads.cross_shift = cross_pull(dnormed_cross)
    dfirst = dsecond + dfirst_part
    dfirst_low = dfirst.astype(jnp.bfloat16)
    grads.output_weight = left_product(mixed, dfirst_low)
    grads.output_bias = column_sum(dfirst_low)
    dmixed = right_product(dfirst_low, full.output_weight).astype(jnp.bfloat16)
    head_dmixed = lax.all_to_all(dmixed, HEAD, split_axis=1, concat_axis=0, tiled=True)
    dmixed_tiles = head_dmixed.reshape(query_count, query_block, local_heads, HD)
    delta_tiles = jnp.sum(dmixed_tiles.astype(jnp.float32) * attended, axis=-1)
    start_dquery = jnp.zeros((query_count, query_block, local_heads, HD), jnp.float32)
    piece = (
        lax.all_gather(head_keys, BLK, axis=0, tiled=True),
        lax.all_gather(head_values, BLK, axis=0, tiled=True),
    )
    dquery_tiles = start_dquery
    count = piece[0].shape[0]
    block_dquery_tiles = dquery_tiles
    piece_keys = piece[0]
    block_tiles = key_tiles(piece_keys, piece[1])
    count = piece_keys.shape[0]

    def block_per_query(state, args):
        dkey_part, dvalue_part = state
        query_tile, query_seg, query_place, logsum_tile, delta_tile, dmixed_tile, dquery_tile = args

        def block_per_key(dquery_acc, key_args):
            key_tile, value_tile, key_seg, key_place = key_args
            scores, allowed = scores_of(
                query_tile, query_seg, query_place, key_tile, key_seg, key_place
            )
            probs = jnp.where(allowed, jnp.exp(scores - logsum_tile[..., None]), 0.0)
            dprobs = jnp.einsum(
                "qhd,khd->qhk", dmixed_tile, value_tile, preferred_element_type=jnp.float32
            )
            dscores = (probs * (dprobs - delta_tile[..., None])).astype(jnp.bfloat16)
            dquery_acc = (
                dquery_acc
                + jnp.einsum("qhk,khd->qhd", dscores, key_tile, preferred_element_type=jnp.float32)
                * scale
            )
            dkey_tile = (
                jnp.einsum("qhk,qhd->khd", dscores, query_tile, preferred_element_type=jnp.float32)
                * scale
            )
            dvalue_tile = jnp.einsum(
                "qhk,qhd->khd",
                probs.astype(jnp.bfloat16),
                dmixed_tile,
                preferred_element_type=jnp.float32,
            )
            return (dquery_acc, (dkey_tile, dvalue_tile))

        dquery_new, key_terms = lax.scan(block_per_key, dquery_tile, block_tiles)
        return ((dkey_part + key_terms[0], dvalue_part + key_terms[1]), dquery_new)

    zero_part = jnp.zeros(block_tiles[0].shape, jnp.float32)
    parts, block_dquery_tiles = lax.scan(
        block_per_query,
        (zero_part, zero_part),
        (
            query_tiles,
            seg_tiles,
            place_tiles,
            logsum,
            delta_tiles,
            dmixed_tiles,
            block_dquery_tiles,
        ),
    )
    dquery_tiles = block_dquery_tiles
    dkey_part = parts[0].reshape(count, half)
    dvalue_part = parts[1].reshape(count, half)
    dkey_rows = dkey_part
    dvalue_rows = dvalue_part
    dquery_tiles, dkey_rows, dvalue_rows = (dquery_tiles, dkey_rows, dvalue_rows)
    own_dkeys, own_dvalues = (
        lax.psum_scatter(
            dkey_rows.astype(jnp.bfloat16), BLK, scatter_dimension=0, tiled=True
        ).astype(jnp.float32),
        lax.psum_scatter(
            dvalue_rows.astype(jnp.bfloat16), BLK, scatter_dimension=0, tiled=True
        ).astype(jnp.float32),
    )
    row_dqueries, row_dkeys, row_dvalues = (
        lax.all_to_all(
            dquery_tiles.reshape(span, half).astype(jnp.bfloat16),
            HEAD,
            split_axis=0,
            concat_axis=1,
            tiled=True,
        ),
        lax.all_to_all(
            own_dkeys.astype(jnp.bfloat16), HEAD, split_axis=0, concat_axis=1, tiled=True
        ),
        lax.all_to_all(
            own_dvalues.astype(jnp.bfloat16), HEAD, split_axis=0, concat_axis=1, tiled=True
        ),
    )
    grads.query_weight = left_product(normed, row_dqueries)
    grads.query_bias = column_sum(row_dqueries)
    grads.key_weight = left_product(normed, row_dkeys)
    grads.value_weight = left_product(normed, row_dvalues)
    grads.value_bias = column_sum(row_dvalues)
    dnormed = (
        right_product(row_dqueries, full.query_weight)
        + right_product(row_dkeys, full.key_weight)
        + right_product(row_dvalues, full.value_weight)
    )
    unused, self_pull = jax.vjp(layer_norm, rows, self_gain_full, self_shift_full)
    drows_part, grads.self_gain, grads.self_shift = self_pull(dnormed)
    row_gradient = dfirst + drows_part
    shards = tuple(
        (
            lax.psum_scatter(
                grads.self_gain.astype(jnp.bfloat16),
                ROW_AXES,
                scatter_dimension=0,
                tiled=True,
            ).astype(jnp.float32),
            lax.psum_scatter(
                grads.self_shift.astype(jnp.bfloat16),
                ROW_AXES,
                scatter_dimension=0,
                tiled=True,
            ).astype(jnp.float32),
            lax.psum_scatter(
                grads.query_weight.astype(jnp.bfloat16),
                ROW_AXES,
                scatter_dimension=0,
                tiled=True,
            ).astype(jnp.float32),
            lax.psum_scatter(
                grads.query_bias.astype(jnp.bfloat16),
                ROW_AXES,
                scatter_dimension=0,
                tiled=True,
            ).astype(jnp.float32),
            lax.psum_scatter(
                grads.key_weight.astype(jnp.bfloat16),
                ROW_AXES,
                scatter_dimension=0,
                tiled=True,
            ).astype(jnp.float32),
            lax.psum_scatter(
                grads.value_weight.astype(jnp.bfloat16),
                ROW_AXES,
                scatter_dimension=0,
                tiled=True,
            ).astype(jnp.float32),
            lax.psum_scatter(
                grads.value_bias.astype(jnp.bfloat16),
                ROW_AXES,
                scatter_dimension=0,
                tiled=True,
            ).astype(jnp.float32),
            lax.psum_scatter(
                grads.output_weight.astype(jnp.bfloat16),
                ROW_AXES,
                scatter_dimension=0,
                tiled=True,
            ).astype(jnp.float32),
            lax.psum_scatter(
                grads.output_bias.astype(jnp.bfloat16),
                ROW_AXES,
                scatter_dimension=0,
                tiled=True,
            ).astype(jnp.float32),
            lax.psum_scatter(
                grads.cross_gain.astype(jnp.bfloat16),
                ROW_AXES,
                scatter_dimension=0,
                tiled=True,
            ).astype(jnp.float32),
            lax.psum_scatter(
                grads.cross_shift.astype(jnp.bfloat16),
                ROW_AXES,
                scatter_dimension=0,
                tiled=True,
            ).astype(jnp.float32),
            lax.psum_scatter(
                grads.probe_weight.astype(jnp.bfloat16),
                ROW_AXES,
                scatter_dimension=0,
                tiled=True,
            ).astype(jnp.float32),
            lax.psum_scatter(
                grads.probe_bias.astype(jnp.bfloat16),
                ROW_AXES,
                scatter_dimension=0,
                tiled=True,
            ).astype(jnp.float32),
            lax.psum_scatter(
                grads.lookup_weight.astype(jnp.bfloat16),
                ROW_AXES,
                scatter_dimension=0,
                tiled=True,
            ).astype(jnp.float32),
            lax.psum_scatter(
                grads.content_weight.astype(jnp.bfloat16),
                ROW_AXES,
                scatter_dimension=0,
                tiled=True,
            ).astype(jnp.float32),
            lax.psum_scatter(
                grads.content_bias.astype(jnp.bfloat16),
                ROW_AXES,
                scatter_dimension=0,
                tiled=True,
            ).astype(jnp.float32),
            lax.psum_scatter(
                grads.merged_weight.astype(jnp.bfloat16),
                ROW_AXES,
                scatter_dimension=0,
                tiled=True,
            ).astype(jnp.float32),
            lax.psum_scatter(
                grads.merged_bias.astype(jnp.bfloat16),
                ROW_AXES,
                scatter_dimension=0,
                tiled=True,
            ).astype(jnp.float32),
            lax.psum_scatter(
                grads.feed_gain.astype(jnp.bfloat16),
                ROW_AXES,
                scatter_dimension=0,
                tiled=True,
            ).astype(jnp.float32),
            lax.psum_scatter(
                grads.feed_shift.astype(jnp.bfloat16),
                ROW_AXES,
                scatter_dimension=0,
                tiled=True,
            ).astype(jnp.float32),
            lax.psum_scatter(
                grads.up_weight.astype(jnp.bfloat16),
                ROW_AXES,
                scatter_dimension=0,
                tiled=True,
            ).astype(jnp.float32),
            lax.psum_scatter(
                grads.up_bias.astype(jnp.bfloat16),
                ROW_AXES,
                scatter_dimension=0,
                tiled=True,
            ).astype(jnp.float32),
            lax.psum_scatter(
                grads.down_weight.astype(jnp.bfloat16),
                ROW_AXES,
                scatter_dimension=0,
                tiled=True,
            ).astype(jnp.float32),
            lax.psum_scatter(
                grads.down_bias.astype(jnp.bfloat16),
                ROW_AXES,
                scatter_dimension=0,
                tiled=True,
            ).astype(jnp.float32),
        )
    )
    return (
        output_low[:prompt_rows],
        output_low[prompt_rows:],
        row_gradient[:prompt_rows],
        row_gradient[prompt_rows:],
        encoded_gradient,
    ) + shards


NT = (((1,), (1,)), ((), ()))
TN = (((0,), (0,)), ((), ()))
PAIR = 2 * HD
TILE = 256
VMEM_BYTES = 56 * 1024 * 1024


def dot(left, right, dims=(((1,), (0,)), ((), ()))):
    return lax.dot_general(left, right, dims, preferred_element_type=jnp.float32)


def first_lanes(shape):
    return lax.broadcasted_iota(jnp.int32, shape, len(shape) - 1) < HD


def split_heads(values, fill=0.0):
    mine = first_lanes(values.shape)
    other = jnp.full(values.shape, fill, values.dtype)
    return jnp.where(mine, values, other), jnp.where(mine, other, values)


def fold(state, query, key, value, allowed=None):
    top, acc = state
    scores = dot(query, key, NT)
    if allowed is not None:
        scores = jnp.where(allowed, scores, floor_value)
    top_new = jnp.maximum(top, jnp.max(scores, axis=1, keepdims=True))
    weights = jnp.exp(scores - top_new).astype(jnp.bfloat16)
    acc_new = acc * jnp.exp(top - top_new) + dot(weights, value)
    return top_new, acc_new


def close(state0, state1):
    top0, acc0 = state0
    top1, acc1 = state1
    mine = first_lanes(acc0.shape)
    total = jnp.where(mine, pltpu.roll(acc0, HD, 1), pltpu.roll(acc1, HD, 1))
    result = jnp.where(mine, acc0, acc1) / total
    logsum = jnp.where(mine, top0, top1) + jnp.log(total)
    turned = jnp.transpose(logsum)
    return result, turned[0:1], turned[HD : HD + 1]


def segment_start(place, bounds_ref):
    start = jnp.zeros_like(place)
    for at in range(bounds_ref.shape[0] - 1):
        start = jnp.where(place >= bounds_ref[at], bounds_ref[at], start)
    return start


SLAB_OF = (0, 2, 1, 3)
COLUMN_OF = (1, 3, 0, 2)


def shard_of(role):
    quarter, side = role >> 1, role & 1
    return (((quarter & 1) << 1) | (quarter >> 1)) * 2 + side


def natural_rows(role, total, prompt_all):
    local_rows, prompt_rows = total // 8, prompt_all // 8
    order = shard_of(role)
    pieces = []
    for low, high, base in (
        (0, prompt_rows, order * prompt_rows),
        (prompt_rows, local_rows, prompt_all + order * (local_rows - prompt_rows)),
    ):
        if not isinstance(base, int):
            base = pl.multiple_of(base, prompt_rows)
        pieces.append((low, high, pl.ds(base, high - low)))
    return pieces


def group_pieces(groups, lines_ref, total, prompt_all):
    pieces = []
    at = 0
    for group in groups:
        for place in range(group.shape[0]):
            for low, high, where in natural_rows(lines_ref[at], total, prompt_all):
                pieces.append((group, place, low, high, where))
            at += 1
    return pieces


def self_forward_kernel(
    prompt_all,
    lines_ref,
    bounds_ref,
    near_ref,
    next_ref,
    far_ref,
    att_ref,
    low_ref,
    lse_ref,
    qn,
    kn,
    v0n,
    v1n,
):
    groups = (near_ref, next_ref, far_ref)
    total = qn.shape[0]
    for group, place, low, high, where in group_pieces(groups, lines_ref, total, prompt_all):
        qn[where] = group[place, low:high, 0:PAIR] * jnp.bfloat16(HD**-0.5)
        kn[where] = group[place, low:high, PAIR : 2 * PAIR]
        v0n[where], v1n[where] = split_heads(group[place, low:high, 2 * PAIR : 3 * PAIR], 1.0)

    prompt_tiles = prompt_all // TILE
    tiles = qn.shape[0] // TILE
    start = (
        jnp.full((TILE, 1), floor_value, jnp.float32),
        jnp.zeros((TILE, PAIR), jnp.float32),
    )

    def both(state, query, base, size, allowed=None):
        key = kn[pl.ds(base, size)]
        return (
            fold(state[0], query[0], key, v0n[pl.ds(base, size)], allowed),
            fold(state[1], query[1], key, v1n[pl.ds(base, size)], allowed),
        )

    def finish(tile, state):
        result, lse0, lse1 = close(*state)
        att_ref[pl.ds(tile * TILE, TILE)] = result
        lse_ref[tile, 0:1, :] = lse0
        lse_ref[tile, 1:2, :] = lse1

    query_at = lax.broadcasted_iota(jnp.int32, (TILE, TILE), 0)
    key_at = lax.broadcasted_iota(jnp.int32, (TILE, TILE), 1)

    def prompt_tile(tile, carry):
        query = split_heads(qn[pl.ds(tile * TILE, TILE)])
        state = lax.fori_loop(
            0, tile, lambda at, now: both(now, query, at * TILE, TILE), (start, start)
        )
        state = both(state, query, tile * TILE, TILE, key_at <= query_at)
        finish(tile, state)
        return carry

    lax.fori_loop(0, prompt_tiles, prompt_tile, 0)

    def cont_tile(tile, carry):
        query = split_heads(qn[pl.ds(tile * TILE, TILE)])
        state = (start, start)
        for at in range(0, prompt_all, 2 * TILE):
            state = both(state, query, at, 2 * TILE)
        first_place = tile * TILE - prompt_all
        place = first_place + query_at
        begin = segment_start(place, bounds_ref)

        def cont_step(at, now):
            key_place = at * TILE - prompt_all + key_at
            return both(now, query, at * TILE, TILE, (key_place <= place) & (key_place >= begin))

        first_key = prompt_tiles + segment_start(first_place, bounds_ref) // TILE
        state = lax.fori_loop(first_key, tile + 1, cont_step, state)
        finish(tile, state)
        return carry

    lax.fori_loop(prompt_tiles, tiles, cont_tile, 0)
    for role in range(8):
        for low, high, where in natural_rows(role, total, prompt_all):
            low_ref[role, low:high] = att_ref[where].astype(jnp.bfloat16)


def unfold(query, key, value, grad, lse, delta, allowed=None):
    probs = jnp.exp(dot(key, query, NT) - lse)
    if allowed is not None:
        probs = jnp.where(allowed, probs, 0.0)
    dscores = (probs * (dot(value, grad, NT) - delta)).astype(jnp.bfloat16)
    return probs.astype(jnp.bfloat16), dscores


def head_inner(left, right):
    turned = jnp.transpose(left * right)
    return (
        jnp.sum(turned[:HD], axis=0, keepdims=True),
        jnp.sum(turned[HD:], axis=0, keepdims=True),
    )


def self_backward_kernel(
    prompt_all,
    lines_ref,
    bounds_ref,
    near_ref,
    next_ref,
    far_ref,
    grad_ref,
    att_ref,
    lse_ref,
    near_out,
    next_out,
    far_out,
    qn,
    kn,
    vn,
    gn,
    dqn,
    dkn,
    dvn,
):
    total = qn.shape[0]
    groups = (near_ref, next_ref, far_ref)
    for group, place, low, high, where in group_pieces(groups, lines_ref, total, prompt_all):
        qn[where] = group[place, low:high, 0:PAIR] * jnp.bfloat16(HD**-0.5)
        kn[where] = group[place, low:high, PAIR : 2 * PAIR]
        vn[where] = group[place, low:high, 2 * PAIR : 3 * PAIR]
    for role in range(8):
        for low, high, where in natural_rows(role, total, prompt_all):
            gn[where] = grad_ref[role, low:high]
    dkn[...] = jnp.zeros_like(dkn)
    dvn[...] = jnp.zeros_like(dvn)
    prompt_tiles = prompt_all // TILE
    tiles = qn.shape[0] // TILE
    key_at = lax.broadcasted_iota(jnp.int32, (TILE, TILE), 0)
    query_at = lax.broadcasted_iota(jnp.int32, (TILE, TILE), 1)

    def load(tile):
        query = split_heads(qn[pl.ds(tile * TILE, TILE)])
        whole = gn[pl.ds(tile * TILE, TILE)]
        grad = split_heads(whole)
        delta = head_inner(whole.astype(jnp.float32), att_ref[pl.ds(tile * TILE, TILE)])
        lse = (lse_ref[tile, 0:1, :], lse_ref[tile, 1:2, :])
        return query, grad, lse, delta

    def step(acc, query, grad, lse, delta, base, allowed=None):
        where = pl.ds(base, TILE)
        key, value = kn[where], vn[where]
        keys = split_heads(key)
        dkey, dvalue = dkn[where], dvn[where]
        for side in range(2):
            probs, dscores = unfold(
                query[side], key, value, grad[side], lse[side], delta[side], allowed
            )
            dvalue = dvalue + dot(probs, grad[side])
            dkey = dkey + dot(dscores, query[side])
            acc = acc + dot(dscores, keys[side], TN)
        dkn[where] = dkey
        dvn[where] = dvalue
        return acc

    def finish(tile, acc):
        dqn[pl.ds(tile * TILE, TILE)] = (acc * HD**-0.5).astype(jnp.bfloat16)

    start = jnp.zeros((TILE, PAIR), jnp.float32)

    def prompt_tile(tile, carry):
        given = load(tile)
        acc = lax.fori_loop(0, tile, lambda at, now: step(now, *given, at * TILE), start)
        acc = step(acc, *given, tile * TILE, key_at <= query_at)
        finish(tile, acc)
        return carry

    lax.fori_loop(0, prompt_tiles, prompt_tile, 0)

    def cont_tile(tile, carry):
        given = load(tile)
        acc = lax.fori_loop(0, prompt_tiles, lambda at, now: step(now, *given, at * TILE), start)
        first_place = tile * TILE - prompt_all
        place = first_place + query_at
        begin = segment_start(place, bounds_ref)

        def cont_step(at, now):
            key_place = at * TILE - prompt_all + key_at
            return step(now, *given, at * TILE, (key_place <= place) & (key_place >= begin))

        first_key = prompt_tiles + segment_start(first_place, bounds_ref) // TILE
        acc = lax.fori_loop(first_key, tile + 1, cont_step, acc)
        finish(tile, acc)
        return carry

    lax.fori_loop(prompt_tiles, tiles, cont_tile, 0)
    outs = (near_out, next_out, far_out)
    for group, place, low, high, where in group_pieces(outs, lines_ref, total, prompt_all):
        group[place, low:high, 0:PAIR] = dqn[where]
        group[place, low:high, PAIR : 2 * PAIR] = dkn[where].astype(jnp.bfloat16)
        group[place, low:high, 2 * PAIR : 3 * PAIR] = dvn[where].astype(jnp.bfloat16)


def cost(micros):
    return pl.CostEstimate(
        flops=int(micros * 9e8), bytes_accessed=int(micros * 2e6), transcendentals=0
    )


def in_vmem(count):
    return [pl.BlockSpec(memory_space=pltpu.VMEM)] * count


def in_smem(count):
    return [pl.BlockSpec(memory_space=pltpu.SMEM)] * count


def self_forward(lines, bounds, groups, prompt_all):
    local_rows = groups[0].shape[1]
    total = 8 * local_rows
    natural = pltpu.VMEM((total, PAIR), jnp.bfloat16)
    return pl.pallas_call(
        functools.partial(self_forward_kernel, prompt_all),
        out_shape=(
            jax.ShapeDtypeStruct((total, PAIR), jnp.float32),
            jax.ShapeDtypeStruct((8, local_rows, PAIR), jnp.bfloat16),
            jax.ShapeDtypeStruct((total // TILE, 2, TILE), jnp.float32),
        ),
        in_specs=in_smem(2) + in_vmem(3),
        out_specs=tuple(in_vmem(3)),
        scratch_shapes=[natural] * 4,
        compiler_params=pltpu.CompilerParams(vmem_limit_bytes=VMEM_BYTES),
        cost_estimate=cost(44),
        name="self_forward",
    )(lines, bounds, *groups)


def self_backward(lines, bounds, groups, grad, att, lse, prompt_all):
    total = 8 * groups[0].shape[1]
    natural = pltpu.VMEM((total, PAIR), jnp.bfloat16)
    wide = pltpu.VMEM((total, PAIR), jnp.float32)
    return pl.pallas_call(
        functools.partial(self_backward_kernel, prompt_all),
        out_shape=tuple(jax.ShapeDtypeStruct(group.shape, jnp.bfloat16) for group in groups),
        in_specs=in_smem(2) + in_vmem(6),
        out_specs=tuple(in_vmem(3)),
        scratch_shapes=[natural] * 5 + [wide] * 2,
        compiler_params=pltpu.CompilerParams(vmem_limit_bytes=VMEM_BYTES),
        cost_estimate=cost(60),
        name="self_backward",
    )(lines, bounds, *groups, grad, att, lse)


def pick(refs, target):
    at = pl.program_id(0)
    for place, ref in enumerate(refs):

        @pl.when(at == place)
        def unused(ref=ref):
            target[...] = ref[0 : target.shape[0]]


def project_kernel(count, *refs):
    gain_ref, shift_ref, weight_ref, bias_ref = refs[count : count + 4]
    normed_ref, rows_ref, chunk = refs[count + 4 :]
    pick(refs[:count], chunk)
    unit, unused = norm_parts(chunk[...].astype(jnp.float32))
    normed = (unit * gain_ref[...] + shift_ref[...]).astype(jnp.bfloat16)
    normed_ref[0] = normed
    rows_ref[0] = (dot(normed, weight_ref[...]) + bias_ref[...]).astype(jnp.bfloat16)


def fixed(shape):
    return pl.BlockSpec(shape, lambda at, *unused: (0,) * len(shape), pipeline_mode=pl.Buffered(1))


def stepped(shape):
    return pl.BlockSpec((1,) + shape, lambda at, *unused: (at,) + (0,) * len(shape))


def project(chunks, rows, gain, shift, weight, bias):
    count = len(chunks)
    width, columns = weight.shape
    return pl.pallas_call(
        functools.partial(project_kernel, count),
        grid=(count,),
        out_shape=(
            jax.ShapeDtypeStruct((count, rows, width), jnp.bfloat16),
            jax.ShapeDtypeStruct((count, rows, columns), jnp.bfloat16),
        ),
        in_specs=[fixed(chunk.shape) for chunk in chunks]
        + [fixed((1, width)), fixed((1, width)), fixed(weight.shape), fixed((1, columns))],
        out_specs=(stepped((rows, width)), stepped((rows, columns))),
        scratch_shapes=[pltpu.VMEM((rows, width), jnp.bfloat16)],
        compiler_params=pltpu.CompilerParams(vmem_limit_bytes=VMEM_BYTES),
        cost_estimate=cost(2.3 * count),
        name="project",
    )(*chunks, gain[None], shift[None], weight, bias[None])


def feed_kernel(count, first, last, info_ref, *refs):
    chunks, refs = refs[:count], refs[count:]
    upstreams, refs = refs[:count], refs[count:]
    weights_ref, bias_ref = refs[:2]
    refs = refs[2:]
    if not first:
        up_before, down_before, sum_before = refs[:3]
        refs = refs[3:]
    out_ref, dnormed_ref, up_after, down_after, sum_after = refs[:5]
    chunk, upstream_chunk, up_sum, down_sum, bias_sum, sems = refs[5:]
    at = pl.program_id(0)

    def carried():
        return (
            pltpu.make_async_copy(up_before, up_sum, sems.at[0]),
            pltpu.make_async_copy(down_before, down_sum, sems.at[1]),
        )

    @pl.when(at == 0)
    def begin():
        if first:
            up_sum[...] = jnp.zeros_like(up_sum)
            down_sum[...] = jnp.zeros_like(down_sum)
            bias_sum[...] = jnp.zeros_like(bias_sum)
        else:
            for copy in carried():
                copy.start()
            bias_sum[...] = sum_before[...]

    pick(chunks, chunk)
    pick(upstreams, upstream_chunk)
    feed = chunk[...]
    upstream = upstream_chunk[...]
    blocks, both, width = weights_ref.shape
    step = both // 2
    out = None
    for low in range(0, blocks * step, step):
        where = slice(low, low + step)
        up = weights_ref[:, :step, where].reshape(blocks * step, step)
        down = weights_ref[low // step, step:]
        hidden = dot(feed, up) + bias_ref[:, where]
        tail = 0.5 + 0.5 * lax.erf(hidden * math.sqrt(0.5))
        active = (hidden * tail).astype(jnp.bfloat16)
        slope = tail + hidden * jnp.exp(-0.5 * hidden * hidden) * (1.0 / math.sqrt(2.0 * math.pi))
        dhidden = (dot(upstream, down, NT) * slope).astype(jnp.bfloat16)
        if low == 0 and not first:

            @pl.when(at == 0)
            def arrive():
                for copy in carried():
                    copy.wait()

        bias_sum[0:1, where] += jnp.sum(dhidden.astype(jnp.float32), axis=0, keepdims=True)
        up_sum[:, where] += dot(feed, dhidden, TN)
        down_sum[where] += dot(active, upstream, TN)
        term, dterm = dot(active, down), dot(dhidden, up, NT)
        out, dnormed = (term, dterm) if out is None else (out + term, dnormed + dterm)
    out_ref[0] = out.astype(jnp.bfloat16)
    dnormed_ref[0] = dnormed.astype(jnp.bfloat16)

    @pl.when(at == count - 1)
    def end():
        sum_after[...] = bias_sum[...]
        if last:
            rows = up_sum.shape[0] // 8
            for role in range(8):
                line = 2 * COLUMN_OF[role // 2] + role % 2
                where = slice(line * rows, (line + 1) * rows)
                up_after[role] = up_sum[where].astype(jnp.bfloat16)
            quarter = info_ref[0]
            for block in range(4):
                where = slice(block * step, (block + 1) * step)
                slot = block ^ quarter
                down_after[slot, :step] = down_sum[where].astype(jnp.bfloat16)
                down_after[slot, step:, :step] = jnp.broadcast_to(
                    bias_sum[0:1, where], (16, step)
                ).astype(jnp.bfloat16)
        else:
            pltpu.sync_copy(up_sum, up_after)
            pltpu.sync_copy(down_sum, down_after)


def feed(chunks, upstreams, info, weights, bias, before, last):
    count = len(chunks)
    rows, width = chunks[0].shape
    columns = bias.shape[0]
    first = before is None
    anywhere = pl.BlockSpec(memory_space=pl.ANY)

    sums = jax.ShapeDtypeStruct((8, columns), jnp.float32)
    out_shape = [
        jax.ShapeDtypeStruct((count, rows, width), jnp.bfloat16),
        jax.ShapeDtypeStruct((count, rows, width), jnp.bfloat16),
    ]
    if last:
        shapes = ((8, width // 8, columns), (4, columns // 4 + 16, width))
        out_shape += [jax.ShapeDtypeStruct(shape, jnp.bfloat16) for shape in shapes]
        sum_specs = [fixed(shape) for shape in shapes]
    else:
        shapes = ((width, columns), (columns, width))
        out_shape += [jax.ShapeDtypeStruct(shape, jnp.float32) for shape in shapes]
        sum_specs = [anywhere, anywhere]
    extra = [] if first else [anywhere, anywhere, fixed((8, columns))]
    carried = () if first else before
    return pl.pallas_call(
        functools.partial(feed_kernel, count, first, last),
        grid_spec=pltpu.PrefetchScalarGridSpec(
            num_scalar_prefetch=1,
            grid=(count,),
            in_specs=[fixed((rows, width))] * (2 * count)
            + [fixed(weights.shape), fixed((1, columns))]
            + extra,
            out_specs=[stepped((rows, width)), stepped((rows, width))] + sum_specs + [fixed((8, columns))],
            scratch_shapes=[
                pltpu.VMEM((rows, width), jnp.bfloat16),
                pltpu.VMEM((rows, width), jnp.bfloat16),
                pltpu.VMEM((width, columns), jnp.float32),
                pltpu.VMEM((columns, width), jnp.float32),
                pltpu.VMEM((8, columns), jnp.float32),
                pltpu.SemaphoreType.DMA((2,)),
            ],
        ),
        out_shape=out_shape + [sums],
        compiler_params=pltpu.CompilerParams(vmem_limit_bytes=VMEM_BYTES),
        cost_estimate=cost(10.5 * count),
        name="feed",
    )(info, *chunks, *upstreams, weights, bias[None], *carried)


def cross_forward_kernel(probe_ref, lookup_ref, content_ref, out_ref, lse_ref):
    query = split_heads(probe_ref[...] * jnp.bfloat16(HD**-0.5))
    key = lookup_ref[...]
    values = split_heads(content_ref[...], 1.0)
    rows = query[0].shape[0]
    start = (jnp.full((rows, 1), floor_value, jnp.float32), jnp.zeros((rows, PAIR), jnp.float32))
    states = [fold(start, query[side], key, values[side]) for side in range(2)]
    result, lse0, lse1 = close(*states)
    out_ref[...] = result
    lse_ref[0, 0:1, :] = lse0
    lse_ref[0, 1:2, :] = lse1


def cross_backward_kernel(
    probe_ref,
    lookup_ref,
    content_ref,
    grad_ref,
    out_ref,
    lse_ref,
    lookup_weight_ref,
    content_weight_ref,
    dprobe_ref,
    dmemory_ref,
    dencoded_ref,
    dencoded,
):
    query = split_heads(probe_ref[...] * jnp.bfloat16(HD**-0.5))
    key = lookup_ref[...]
    keys = split_heads(key)
    value = content_ref[...]
    whole = grad_ref[...]
    grad = split_heads(whole)
    delta = head_inner(whole.astype(jnp.float32), out_ref[...])
    terms = []
    for side in range(2):
        probs, dscores = unfold(
            query[side], key, value, grad[side], lse_ref[0, side : side + 1, :], delta[side]
        )
        terms.append(
            (
                dot(dscores, keys[side], TN),
                dot(dscores, query[side]),
                dot(probs, grad[side]),
            )
        )
    dprobe_ref[...] = ((terms[0][0] + terms[1][0]) * HD**-0.5).astype(jnp.bfloat16)
    dlookup = (terms[0][1] + terms[1][1]).astype(jnp.bfloat16)
    dcontent = (terms[0][2] + terms[1][2]).astype(jnp.bfloat16)
    rows = dmemory_ref.shape[1] // 2
    for block in range(8):
        columns = slice(block * PAIR, (block + 1) * PAIR)
        dmemory_ref[0, :rows, columns] = dlookup[block * rows : (block + 1) * rows]
        dmemory_ref[0, rows:, columns] = dcontent[block * rows : (block + 1) * rows]
    term = dot(dlookup, lookup_weight_ref[...], NT) + dot(dcontent, content_weight_ref[...], NT)

    @pl.when(pl.program_id(0) == 0)
    def begin():
        dencoded[...] = term

    @pl.when(pl.program_id(0) > 0)
    def more():
        dencoded[...] += term

    @pl.when(pl.program_id(0) == 7)
    def end():
        dencoded_ref[...] = dencoded[...].astype(jnp.bfloat16)


def pair_block(rows):
    return pl.BlockSpec((rows, PAIR), lambda at: (0, at))


def cross_forward(probes, lookups, contents):
    rows, width = probes.shape
    memory = lookups.shape[0]
    pairs = width // PAIR
    return pl.pallas_call(
        cross_forward_kernel,
        grid=(pairs,),
        out_shape=(
            jax.ShapeDtypeStruct((rows, width), jnp.float32),
            jax.ShapeDtypeStruct((pairs, 2, rows), jnp.float32),
        ),
        in_specs=[pair_block(rows), pair_block(memory), pair_block(memory)],
        out_specs=(pair_block(rows), pl.BlockSpec((1, 2, rows), lambda at: (at, 0, 0))),
        compiler_params=pltpu.CompilerParams(vmem_limit_bytes=VMEM_BYTES),
        cost_estimate=cost(10),
        name="cross_forward",
    )(probes, lookups, contents)


def cross_backward(probes, lookups, contents, grad, recalled, lse, lookup_weight, content_weight):
    rows, width = probes.shape
    memory = lookups.shape[0]
    pairs = width // PAIR
    return pl.pallas_call(
        cross_backward_kernel,
        grid=(pairs,),
        out_shape=(
            jax.ShapeDtypeStruct((rows, width), jnp.bfloat16),
            jax.ShapeDtypeStruct((pairs, 2 * memory // 8, width), jnp.bfloat16),
            jax.ShapeDtypeStruct((memory, width), jnp.bfloat16),
        ),
        in_specs=[
            pair_block(rows),
            pair_block(memory),
            pair_block(memory),
            pair_block(rows),
            pair_block(rows),
            pl.BlockSpec((1, 2, rows), lambda at: (at, 0, 0)),
            pair_block(width),
            pair_block(width),
        ],
        out_specs=(
            pair_block(rows),
            pl.BlockSpec((1, 2 * memory // 8, width), lambda at: (at, 0, 0)),
            fixed((memory, width)),
        ),
        scratch_shapes=[pltpu.VMEM((memory, width), jnp.float32)],
        compiler_params=pltpu.CompilerParams(vmem_limit_bytes=VMEM_BYTES),
        cost_estimate=cost(20),
        name="cross_backward",
    )(probes, lookups, contents, grad, recalled, lse, lookup_weight, content_weight)


def norm_parts(values):
    center = jnp.mean(values, axis=-1, keepdims=True)
    centred = values - center
    spread = jnp.mean(centred * centred, axis=-1, keepdims=True)
    rate = lax.rsqrt(spread + 1e-05)
    return centred * rate, rate


def norm_backward(grad, unit, rate, gain):
    scaled = grad * gain
    along = jnp.mean(scaled, axis=-1, keepdims=True)
    across = jnp.mean(scaled * unit, axis=-1, keepdims=True)
    return (
        rate * (scaled - along - unit * across),
        jnp.sum(grad * unit, axis=0),
        jnp.sum(grad, axis=0),
    )


def joined(group, block, side=0, sides=1):
    return (group * 4 + block) * sides + side


class Slab:
    def __init__(self):
        group, side = lax.axis_index(GRP), lax.axis_index(HEAD)
        self.group, self.side, self.block = group, side, lax.axis_index(BLK)
        column, core = group // 2, group % 2
        chips = ((0, 0), (1, 0), (1, 1), (0, 1))
        lines = [[4 * left + 2 * own + right for left, right in chips] for own in range(2)]
        self.forward = [(line[at], line[(at + 1) % 4]) for line in lines for at in range(4)]
        self.reverse = [(right, left) for left, right in self.forward]
        self.cores = [(role, role ^ 2) for role in range(8)]
        place = jnp.where(column == 0, 3 * side, 1 + side)
        owners = []
        for step, other in ((0, 0), (0, 1), (-1, 0), (1, 0), (-1, 1), (1, 1), (2, 0), (2, 1)):
            there = (place + step) % 4
            far = ((there == 1) | (there == 2)).astype(jnp.int32)
            owners.append(4 * far + 2 * ((core + other) % 2) + (there >= 2).astype(jnp.int32))
        self.lines = jnp.stack(owners).astype(jnp.int32)

    def up(self, values):
        return lax.ppermute(values, ROLE_AXES, self.forward)

    def down(self, values):
        return lax.ppermute(values, ROLE_AXES, self.reverse)

    def swap(self, values):
        return lax.ppermute(values, ROLE_AXES, self.cores)

    def gather(self, values, gates=(None, None)):
        half = values.shape[0] // 2
        left, right, other = self.up(values), self.down(values), self.swap(values)
        if gates[0] is not None:
            left, right, other = after((left, right, other), gates[0])
        pair = (self.up(left[:half]), self.down(right[half:]))
        near, far = self.swap(left), self.swap(right)
        if gates[1] is not None:
            pair, near, far = after((pair, near, far), gates[1])
        last = jnp.concatenate(pair, axis=0)
        return ((values, other), (left, right, near, far), (last, self.swap(last)))

    def scatter(self, near, after_parts, far, gates=(None, None, None)):
        low, wide = jnp.bfloat16, jnp.float32
        swaps = [self.swap(far[1]), self.swap(after_parts[2:4]), self.swap(near[1])]
        if gates[0] is not None:
            swaps = after(swaps, gates[0])
        last = far[0].astype(wide) + swaps[0]
        half = last.shape[0] // 2
        sent = (self.up(last[:half].astype(low)), self.down(last[half:].astype(low)))
        if gates[1] is not None:
            sent = after(sent, gates[1])
        left, right = sent
        pair = after_parts[0:2].astype(wide) + swaps[1]
        behind, ahead = pair[0], pair[1]
        left = jnp.concatenate([left + ahead[:half], ahead[half:]], axis=0).astype(low)
        right = jnp.concatenate([behind[:half], right + behind[half:]], axis=0).astype(low)
        sent = (self.up(left), self.down(right))
        if gates[2] is not None:
            sent = after(sent, gates[2])
        return near[0].astype(wide) + swaps[2] + sent[0] + sent[1]

    def enter(self, values):
        moves = [
            (joined(group, block), joined(SLAB_OF[block], SLAB_OF[group]))
            for group in range(4)
            for block in range(4)
        ]
        return lax.ppermute(values, (GRP, BLK), moves)

    def leave(self, values):
        moves = [
            (joined(group, block), joined(SLAB_OF[block], SLAB_OF[group]))
            for group in range(4)
            for block in range(4)
        ]
        return lax.ppermute(values, (GRP, BLK), moves)

    def leave_columns(self, values):
        moves = [
            (joined(group, block), joined(SLAB_OF[block], COLUMN_OF[group]))
            for group in range(4)
            for block in range(4)
        ]
        return lax.ppermute(values, (GRP, BLK), moves)

    def leave_quarters(self, pieces):
        result = []
        for at, piece in enumerate(pieces):
            moves = [
                (joined(group, block), joined(SLAB_OF[block], group ^ at))
                for group in range(4)
                for block in range(4)
            ]
            result.append(lax.ppermute(piece, (GRP, BLK), moves))
        return result

    def settle(self, parts, blank):
        for at, part in enumerate(parts):
            start = (self.block ^ at,) + (0,) * part.ndim
            blank = lax.dynamic_update_slice(blank, part[None].astype(blank.dtype), start)
        return blank

    def leave_own(self, values):
        moves = [
            (joined(group, block, side, 2), joined(SLAB_OF[block], group, side, 2))
            for group in range(4)
            for block in range(4)
            for side in range(2)
        ]
        return lax.ppermute(values, ALL_AXES, moves)


def by_role(values, order=SLAB_OF):
    values = values.reshape((4, 2, -1) + values.shape[1:])
    values = jnp.stack([values[at] for at in order])
    return values.reshape((8,) + values.shape[2:])


def after(values, *others):
    return lax.optimization_barrier((values,) + others)[0]


def exchange(values, axes):
    return lax.all_to_all(values, axes, split_axis=0, concat_axis=0, tiled=True)


def columns_kernel(pieces_ref, out_ref):
    part = pieces_ref.shape[2] // 4
    for role in range(8):
        for block in range(4):
            order = (block * 2 + role % 2) * 4 + role // 2
            out_ref[:, order * part : (order + 1) * part] = pieces_ref[
                role, :, block * part : (block + 1) * part
            ].astype(jnp.float32)


def settle_columns(pieces):
    roles, rows, columns = pieces.shape
    return pl.pallas_call(
        columns_kernel,
        out_shape=jax.ShapeDtypeStruct((rows, roles * columns), jnp.float32),
        in_specs=in_vmem(1),
        out_specs=pl.BlockSpec(memory_space=pltpu.VMEM),
        compiler_params=pltpu.CompilerParams(vmem_limit_bytes=VMEM_BYTES),
        cost_estimate=cost(4),
        name="settle_columns",
    )(pieces)


def heads_kernel(pieces_ref, *outs):
    for role in range(8):
        for place, out_ref in enumerate(outs):
            out_ref[:, role * PAIR : (role + 1) * PAIR] = pieces_ref[
                role, :, place * PAIR : (place + 1) * PAIR
            ].astype(jnp.float32)


def settle_heads(pieces):
    roles, rows, columns = pieces.shape
    count = columns // PAIR
    return pl.pallas_call(
        heads_kernel,
        out_shape=(jax.ShapeDtypeStruct((rows, roles * PAIR), jnp.float32),) * count,
        in_specs=in_vmem(1),
        out_specs=tuple(in_vmem(count)),
        compiler_params=pltpu.CompilerParams(vmem_limit_bytes=VMEM_BYTES),
        cost_estimate=cost(3),
        name="settle_heads",
    )(pieces)


def head_body(
    prompt,
    continued,
    encoded,
    cont_lengths,
    self_gain,
    self_shift,
    query_weight,
    query_bias,
    key_weight,
    value_weight,
    value_bias,
    output_weight,
    output_bias,
    cross_gain,
    cross_shift,
    probe_weight,
    probe_bias,
    lookup_weight,
    content_weight,
    content_bias,
    merged_weight,
    merged_bias,
    feed_gain,
    feed_shift,
    up_weight,
    up_bias,
    down_weight,
    down_bias,
    cot_prompt,
    cot_cont,
):
    slab = Slab()
    low = jnp.bfloat16
    width = prompt.shape[1]
    shard = width // 8
    piece = shard // 4
    prompt_rows = prompt.shape[0]
    local_rows = prompt_rows + continued.shape[0]
    prompt_all = 8 * prompt_rows
    memory_rows = encoded.shape[0]
    quarter, side = slab.group, slab.side
    role = 2 * quarter + side

    swapped = [
        (joined(group, block), joined(block, SLAB_OF[group]))
        for group in range(4)
        for block in range(4)
    ]
    lengths = lax.ppermute(cont_lengths, (GRP, BLK), swapped)
    bounds = jnp.cumsum(lengths).astype(jnp.int32)

    own_all = slab.enter(jnp.concatenate([prompt, continued, encoded], axis=0))

    def head_columns(weight):
        mine = lax.dynamic_slice_in_dim(weight.reshape(shard, 4, 2 * shard), quarter, 1, axis=1)
        return mine.reshape(shard, 2, shard).transpose(1, 0, 2)

    small = (
        self_gain,
        self_shift,
        output_bias,
        cross_gain,
        cross_shift,
        probe_bias,
        merged_bias,
        feed_gain,
        feed_shift,
        down_bias,
        content_bias,
        query_bias,
        value_bias,
    )
    vectors = jnp.concatenate(small + (up_bias,) + (self_gain,) * 3).reshape(1, 8, 3 * shard)
    mixed_in = jnp.concatenate(
        [
            jnp.concatenate(
                [head_columns(query_weight), head_columns(key_weight), head_columns(value_weight)],
                axis=2,
            ),
            jnp.broadcast_to(vectors, (2, 8, 3 * shard)),
        ],
        axis=1,
    )
    mixed_in = jnp.broadcast_to(mixed_in[None], (4,) + mixed_in.shape)
    mixed_in = exchange(mixed_in.reshape(8, shard + 8, 3 * shard), ROW_AXES)
    own_all, mixed_in = lax.optimization_barrier((own_all, mixed_in))
    head_weights = mixed_in[:, :shard].reshape(width, 3 * shard)
    vectors = mixed_in[:, shard:].reshape(8, 24, shard)
    packed = vectors[:, : len(small)].transpose(1, 0, 2).reshape(len(small), width)
    (
        self_gain_full,
        self_shift_full,
        output_bias_full,
        cross_gain_full,
        cross_shift_full,
        probe_bias_full,
        merged_bias_full,
        feed_gain_full,
        feed_shift_full,
        down_bias_full,
        content_bias_full,
        query_bias_full,
        value_bias_full,
    ) = [packed[at].astype(jnp.float32) for at in range(len(small))]
    ups = vectors[:, len(small) : len(small) + 8].reshape(4, 2, 4, -1)
    ups = lax.dynamic_index_in_dim(ups, side, 1, keepdims=False)
    up_bias_own = lax.dynamic_index_in_dim(ups, quarter, 1, keepdims=False).reshape(width)
    up_bias_own = up_bias_own.astype(jnp.float32)

    row_groups = slab.gather(own_all)
    up_mine = lax.dynamic_index_in_dim(
        up_weight.reshape(shard, 4, 2, 4, -1), quarter, 3, keepdims=False
    )
    up_mine = up_mine.transpose(2, 0, 1, 3).reshape(2, shard, width)
    up_mine = exchange(after(up_mine, own_all), HEAD).reshape(2 * shard, width)
    down_mine = lax.dynamic_slice_in_dim(down_weight, quarter * 2 * shard, 2 * shard, axis=0)

    squares = (output_weight, probe_weight, merged_weight, lookup_weight, content_weight)
    shared = jnp.concatenate(
        [lax.dynamic_slice_in_dim(weight, quarter * piece, piece, axis=0) for weight in squares],
        axis=0,
    )
    shared = after(shared, own_all)
    shared = lax.all_gather(shared, (BLK, HEAD, GRP), axis=0, tiled=False)
    shared = shared.reshape(32, len(squares), piece, width)
    output_full, probe_full, merged_full, lookup_full, content_full = [
        shared[:, at].reshape(width, width) for at in range(len(squares))
    ]

    rows = own_all[:local_rows].astype(jnp.float32)

    def own_columns(vector):
        return lax.dynamic_slice_in_dim(vector, role * shard, shard, axis=0)

    head_bias = jnp.concatenate(
        [
            own_columns(query_bias_full),
            jnp.zeros((shard,), jnp.float32),
            own_columns(value_bias_full),
        ]
    )
    projected = [
        project(group, local_rows, self_gain_full, self_shift_full, head_weights, head_bias)
        for group in row_groups
    ]
    upstream = slab.enter(
        after(jnp.concatenate([cot_prompt, cot_cont], axis=0), own_all)
    )
    feed_weights = jnp.concatenate([up_mine, down_mine], axis=0)
    feed_weights = lax.all_gather(feed_weights, BLK, axis=0, tiled=False)
    head_groups = [pair[1] for pair in projected]
    attended, attended_low, logsum = self_forward(slab.lines, bounds, head_groups, prompt_all)
    upstream_groups = slab.gather(
        after(upstream, row_groups[2]), (head_groups[2], attended_low)
    )
    mixed = exchange(attended_low, ROLE_AXES).transpose(1, 0, 2).reshape(local_rows, width)
    first = rows + matmul(mixed, output_full) + output_bias_full
    first_unit, first_rate = norm_parts(first)
    normed_cross = (first_unit * cross_gain_full + cross_shift_full).astype(low)
    probes = (matmul(normed_cross, probe_full) + probe_bias_full).astype(low)

    memory = jnp.zeros((8 * memory_rows, width), low)
    chunks = [chunk for group in row_groups for chunk in group]
    for at, chunk in enumerate(chunks):
        memory = lax.dynamic_update_slice_in_dim(
            memory, chunk[local_rows:], slab.lines[at] * memory_rows, axis=0
        )
    lookups = matmul(memory, lookup_full).astype(low)
    contents = (matmul(memory, content_full) + content_bias_full).astype(low)
    recalled, cross_logsum = cross_forward(probes, lookups, contents)
    recalled_low = recalled.astype(low)
    second = first + matmul(recalled_low, merged_full) + merged_bias_full
    second_unit, second_rate = norm_parts(second)
    normed_feed = (second_unit * feed_gain_full + feed_shift_full).astype(low)

    before, dnormed_parts, output_parts = None, [], []
    feed_groups = slab.gather(normed_feed)
    info = quarter[None].astype(jnp.int32)
    for group, upstream_group in zip(feed_groups, upstream_groups):
        last = group is feed_groups[-1]
        output, dnormed, *before = feed(
            group, upstream_group, info, feed_weights, up_bias_own, before, last
        )
        dnormed_parts.append(dnormed)
        output_parts.append(output)
    up_gradient, down_gradient, unused = before
    dnormed_feed = slab.scatter(*dnormed_parts)
    up_gradient, down_gradient, output_parts = after(
        (up_gradient, down_gradient, output_parts), dnormed_feed
    )
    up_gradient = exchange(up_gradient, ROLE_AXES)
    down_gradient = slab.leave_quarters([down_gradient[at] for at in range(4)])

    part, feed_gain_sum, feed_shift_sum = norm_backward(
        dnormed_feed, second_unit, second_rate, feed_gain_full
    )
    dsecond = upstream.astype(jnp.float32) + part
    dsecond_low = dsecond.astype(low)
    drecalled = right_product(dsecond_low, merged_full).astype(low)
    dprobes, dmemory, encoded_gradient = cross_backward(
        probes,
        lookups,
        contents,
        drecalled,
        recalled,
        cross_logsum,
        lookup_full,
        content_full,
    )
    dnormed_cross = right_product(dprobes, probe_full)
    part, cross_gain_sum, cross_shift_sum = norm_backward(
        dnormed_cross, first_unit, first_rate, cross_gain_full
    )
    dfirst = dsecond + part
    dfirst_low = dfirst.astype(low)
    dmixed = right_product(dfirst_low, output_full).astype(low)
    dmixed = dmixed.reshape(local_rows, 8, shard).transpose(1, 0, 2)
    output = slab.scatter(*output_parts, (drecalled, dprobes, dmixed))
    output = slab.leave((second + output + down_bias_full).astype(low))
    up_gradient, down_gradient, dmixed = lax.optimization_barrier(
        (up_gradient, down_gradient, dmixed)
    )
    dmixed = exchange(dmixed, ROLE_AXES)
    up_gradient = slab.leave_columns(up_gradient)

    sums = jnp.stack(
        (
            column_sum(dfirst_low),
            cross_gain_sum,
            cross_shift_sum,
            column_sum(dprobes),
            column_sum(dsecond_low),
            feed_gain_sum,
            feed_shift_sum,
            column_sum(upstream),
        )
    )
    sums = by_role(sums.T).transpose(0, 2, 1).reshape(8, 1, width)
    sums = jnp.broadcast_to(sums, (8, 16, width))
    scattered = jnp.concatenate(
        [
            by_role(left_product(recalled_low, dsecond_low).astype(low)),
            by_role(left_product(normed_cross, dprobes).astype(low)),
            encoded_gradient.reshape(8, memory_rows, width),
            by_role(left_product(mixed, dfirst_low).astype(low)),
            sums.astype(low),
            dmemory,
        ],
        axis=1,
    )
    scattered = lax.psum_scatter(scattered, ROLE_AXES, scatter_dimension=0, tiled=False)

    dhead_groups = self_backward(
        slab.lines, bounds, head_groups, dmixed, attended, logsum, prompt_all
    )
    done = dhead_groups[0]

    dnormed = slab.scatter(
        *[
            right_product(group.reshape(-1, 3 * shard), head_weights)
            .astype(low)
            .reshape(group.shape[0], local_rows, width)
            for group in dhead_groups
        ]
    )

    up_gradient, down_gradient, output, scattered = after(
        (up_gradient, down_gradient, output, scattered), done
    )
    up_weight_gradient = settle_columns(up_gradient)
    down_weight_gradient = slab.settle(
        [part[: 2 * shard] for part in down_gradient], jnp.zeros((4, 2 * shard, width), jnp.float32)
    ).reshape(width, width)
    up_bias_gradient = slab.settle(
        [part[2 * shard, : 2 * shard] for part in down_gradient],
        jnp.zeros((4, 2 * shard), jnp.float32),
    ).reshape(width)

    encoded_end = 2 * shard + memory_rows
    squares_end = encoded_end + shard + 16
    mine_dmemory = scattered[squares_end:].reshape(2, memory_rows, 8, shard)
    mine_dmemory = mine_dmemory.transpose(0, 2, 1, 3)
    mine_dmemory = mine_dmemory.reshape(2, 8 * memory_rows, shard)

    head_gradient = [
        sum(
            left_product(normed.reshape(-1, width), group.reshape(-1, 3 * shard))
            for (normed, unused), group in zip(projected, dhead_groups)
        ),
        left_product(memory, mine_dmemory[0]),
        left_product(memory, mine_dmemory[1]),
    ]
    head_gradient = jnp.concatenate([part.astype(low) for part in head_gradient], axis=1)
    head_gradient = exchange(by_role(head_gradient, COLUMN_OF), ROLE_AXES)
    (
        query_weight_gradient,
        key_weight_gradient,
        value_weight_gradient,
        lookup_weight_gradient,
        content_weight_gradient,
    ) = settle_heads(slab.leave_columns(head_gradient))
    head_sums = sum(column_sum(group.reshape(-1, 3 * shard)) for group in dhead_groups)
    head_sums = slab.leave_own(
        jnp.stack([head_sums[:shard], head_sums[2 * shard :], column_sum(mine_dmemory[1])])
    )
    unit, rate = norm_parts(rows)
    part, self_gain_sum, self_shift_sum = norm_backward(dnormed, unit, rate, self_gain_full)
    row_gradient = jnp.concatenate([(dfirst + part).astype(low), scattered[:squares_end]], axis=0)
    row_gradient = slab.leave(row_gradient).astype(jnp.float32)
    square_gradient = row_gradient[local_rows:]
    merged_weight_gradient = square_gradient[:shard]
    probe_weight_gradient = square_gradient[shard : 2 * shard]
    encoded_gradient = square_gradient[2 * shard : encoded_end]
    output_weight_gradient = square_gradient[encoded_end : encoded_end + shard]
    small_sums = square_gradient[encoded_end + shard].reshape(8, shard)
    (
        output_bias_gradient,
        cross_gain_gradient,
        cross_shift_gradient,
        probe_bias_gradient,
        merged_bias_gradient,
        feed_gain_gradient,
        feed_shift_gradient,
        down_bias_gradient,
    ) = [small_sums[at] for at in range(8)]

    sums = by_role(jnp.stack((self_gain_sum, self_shift_sum), axis=1))
    sums = jnp.sum(exchange(sums.transpose(0, 2, 1), ROLE_AXES), axis=0)
    sums = slab.leave(sums)
    up_bias_gradient = up_bias_gradient.reshape(-1)
    query_bias_gradient, value_bias_gradient, content_bias_gradient = [
        head_sums[at] for at in range(3)
    ]
    self_gain_gradient, self_shift_gradient = sums[0], sums[1]

    return (
        (
            output[:prompt_rows],
            output[prompt_rows:],
            row_gradient[:prompt_rows],
            row_gradient[prompt_rows:local_rows],
            encoded_gradient,
            self_gain_gradient,
            self_shift_gradient,
            query_weight_gradient,
            query_bias_gradient,
            key_weight_gradient,
            value_weight_gradient,
            value_bias_gradient,
            output_weight_gradient,
            output_bias_gradient,
            cross_gain_gradient,
            cross_shift_gradient,
            probe_weight_gradient,
            probe_bias_gradient,
            lookup_weight_gradient,
            content_weight_gradient,
            content_bias_gradient,
            merged_weight_gradient,
            merged_bias_gradient,
            feed_gain_gradient,
            feed_shift_gradient,
            up_weight_gradient,
            up_bias_gradient,
            down_weight_gradient,
            down_bias_gradient,
        )
    )


def solution(mesh):
    rows, group = P(ALL_AXES, None), P(ALL_AXES)
    weight, vector = P(ROW_AXES, None), P(ROW_AXES)
    ranks = [2 if "weight" in name else 1 for name in PARAM_NAMES]
    sizes = tuple(mesh.shape[axis] for axis in ALL_AXES)
    return jax.shard_map(
        head_body if sizes == (4, 4, 2) and HEADS * HD == 8 * PAIR else token_body,
        mesh=mesh,
        in_specs=(rows, rows, rows, P(GRP))
        + tuple(weight if rank == 2 else vector for rank in ranks)
        + (rows, rows),
        out_specs=(rows,) * 5 + tuple(rows if rank == 2 else group for rank in ranks),
        check_vma=False,
    )
```

```python
import functools
import math
import types

import jax
import jax.numpy as jnp
from jax import lax
from jax.experimental import pallas as pl
from jax.experimental.pallas import tpu as pltpu
from jax.sharding import PartitionSpec as P

HEADS = 16
HD = 64


floor_value = -1e30
BLK = "blk"
HEAD = "head"
GRP = "grp"
ROW_AXES = (BLK, HEAD)
ROLE_AXES = (GRP, HEAD)
ALL_AXES = (GRP, BLK, HEAD)
PARAM_NAMES = (
    "self_gain",
    "self_shift",
    "query_weight",
    "query_bias",
    "key_weight",
    "value_weight",
    "value_bias",
    "output_weight",
    "output_bias",
    "cross_gain",
    "cross_shift",
    "probe_weight",
    "probe_bias",
    "lookup_weight",
    "content_weight",
    "content_bias",
    "merged_weight",
    "merged_bias",
    "feed_gain",
    "feed_shift",
    "up_weight",
    "up_bias",
    "down_weight",
    "down_bias",
)


def layer_norm(rows, gain, shift):
    center = jnp.mean(rows, axis=-1, keepdims=True)
    centred = rows - center
    spread = jnp.mean(centred * centred, axis=-1, keepdims=True)
    return centred * lax.rsqrt(spread + 1e-05) * gain + shift


def matmul(left, right):
    return jnp.dot(left, right, preferred_element_type=jnp.float32)


def left_product(left, right):
    return jnp.einsum("rd,re->de", left, right, preferred_element_type=jnp.float32)


def right_product(left, right):
    return jnp.einsum("re,de->rd", left, right, preferred_element_type=jnp.float32)


def column_sum(values):
    return jnp.sum(values.astype(jnp.float32), axis=0)


def exact_gelu(values):
    return jax.nn.gelu(values, approximate=False)


def row_meta(global_rows, bounds, prompt_rows, cont_rows, heads_here):
    local_rows = prompt_rows + cont_rows
    span = heads_here * local_rows
    owner = global_rows // span
    inner = global_rows % span
    device = owner * heads_here + inner // local_rows
    offset = inner % local_rows
    in_prompt = offset < prompt_rows
    places = jnp.where(
        in_prompt, device * prompt_rows + offset, device * cont_rows + offset - prompt_rows
    )
    later = jnp.sum((places[:, None] >= bounds[None, :]).astype(jnp.int32), axis=1)
    segment = jnp.where(in_prompt, 0, 1 + later)
    return (segment, places)


def allowed_pairs(query_seg, query_place, key_seg, key_place):
    from_prompt = (key_seg[None, :] == 0) & (query_seg[:, None] > 0)
    causal = (key_seg[None, :] == query_seg[:, None]) & (key_place[None, :] <= query_place[:, None])
    return from_prompt | causal


def token_body(
    prompt,
    continued,
    encoded,
    cont_lengths,
    self_gain,
    self_shift,
    query_weight,
    query_bias,
    key_weight,
    value_weight,
    value_bias,
    output_weight,
    output_bias,
    cross_gain,
    cross_shift,
    probe_weight,
    probe_bias,
    lookup_weight,
    content_weight,
    content_bias,
    merged_weight,
    merged_bias,
    feed_gain,
    feed_shift,
    up_weight,
    up_bias,
    down_weight,
    down_bias,
    cot_prompt,
    cot_cont,
):
    gathered = (
        lax.all_gather(self_gain, ROW_AXES, axis=0, tiled=True),
        lax.all_gather(self_shift, ROW_AXES, axis=0, tiled=True),
        lax.all_gather(query_weight, ROW_AXES, axis=0, tiled=True),
        lax.all_gather(query_bias, ROW_AXES, axis=0, tiled=True),
        lax.all_gather(key_weight, ROW_AXES, axis=0, tiled=True),
        lax.all_gather(value_weight, ROW_AXES, axis=0, tiled=True),
        lax.all_gather(value_bias, ROW_AXES, axis=0, tiled=True),
        lax.all_gather(output_weight, ROW_AXES, axis=0, tiled=True),
        lax.all_gather(output_bias, ROW_AXES, axis=0, tiled=True),
        lax.all_gather(cross_gain, ROW_AXES, axis=0, tiled=True),
        lax.all_gather(cross_shift, ROW_AXES, axis=0, tiled=True),
        lax.all_gather(probe_weight, ROW_AXES, axis=0, tiled=True),
        lax.all_gather(probe_bias, ROW_AXES, axis=0, tiled=True),
        lax.all_gather(lookup_weight, ROW_AXES, axis=0, tiled=True),
        lax.all_gather(content_weight, ROW_AXES, axis=0, tiled=True),
        lax.all_gather(content_bias, ROW_AXES, axis=0, tiled=True),
        lax.all_gather(merged_weight, ROW_AXES, axis=0, tiled=True),
        lax.all_gather(merged_bias, ROW_AXES, axis=0, tiled=True),
        lax.all_gather(feed_gain, ROW_AXES, axis=0, tiled=True),
        lax.all_gather(feed_shift, ROW_AXES, axis=0, tiled=True),
        lax.all_gather(up_weight, ROW_AXES, axis=0, tiled=True),
        lax.all_gather(up_bias, ROW_AXES, axis=0, tiled=True),
        lax.all_gather(down_weight, ROW_AXES, axis=0, tiled=True),
        lax.all_gather(down_bias, ROW_AXES, axis=0, tiled=True),
    )
    full = types.SimpleNamespace(**dict(zip(PARAM_NAMES, gathered)))
    heads_here = lax.axis_size(HEAD)
    prompt_rows = prompt.shape[0]
    cont_rows = continued.shape[0]
    local_rows = prompt_rows + cont_rows
    span = heads_here * local_rows
    width = prompt.shape[1]
    local_heads = HEADS // heads_here
    half = local_heads * HD
    scale = HD ** (-0.5)
    bounds = jnp.cumsum(cont_lengths)
    rows = jnp.concatenate([prompt, continued], axis=0).astype(jnp.float32)
    self_gain_full = full.self_gain.astype(jnp.float32)
    self_shift_full = full.self_shift.astype(jnp.float32)
    cross_gain_full = full.cross_gain.astype(jnp.float32)
    cross_shift_full = full.cross_shift.astype(jnp.float32)
    feed_gain_full = full.feed_gain.astype(jnp.float32)
    feed_shift_full = full.feed_shift.astype(jnp.float32)
    normed = layer_norm(rows, self_gain_full, self_shift_full).astype(jnp.bfloat16)
    queries = (matmul(normed, full.query_weight) + full.query_bias).astype(jnp.bfloat16)
    keys_rows = matmul(normed, full.key_weight).astype(jnp.bfloat16)
    values_rows = (matmul(normed, full.value_weight) + full.value_bias).astype(jnp.bfloat16)
    head_queries, head_keys, head_values = (
        lax.all_to_all(queries, HEAD, split_axis=1, concat_axis=0, tiled=True),
        lax.all_to_all(keys_rows, HEAD, split_axis=1, concat_axis=0, tiled=True),
        lax.all_to_all(values_rows, HEAD, split_axis=1, concat_axis=0, tiled=True),
    )
    query_block = math.gcd(span, 512)
    query_count = span // query_block
    own_rows = lax.axis_index(BLK) * span + jnp.arange(span, dtype=jnp.int32)
    own_seg, own_place = row_meta(own_rows, bounds, prompt_rows, cont_rows, heads_here)
    query_tiles = head_queries.reshape(query_count, query_block, local_heads, HD)
    seg_tiles = own_seg.reshape(query_count, query_block)
    place_tiles = own_place.reshape(query_count, query_block)

    def key_tiles(piece_keys, piece_values):
        count = piece_keys.shape[0]
        key_block = math.gcd(count, span)
        key_count = count // key_block
        key_rows = jnp.arange(count, dtype=jnp.int32)
        key_seg, key_place = row_meta(key_rows, bounds, prompt_rows, cont_rows, heads_here)
        return (
            piece_keys.reshape(key_count, key_block, local_heads, HD),
            piece_values.reshape(key_count, key_block, local_heads, HD),
            key_seg.reshape(key_count, key_block),
            key_place.reshape(key_count, key_block),
        )

    def scores_of(query_tile, query_seg, query_place, key_tile, key_seg, key_place):
        raw = (
            jnp.einsum("qhd,khd->qhk", query_tile, key_tile, preferred_element_type=jnp.float32)
            * scale
        )
        allowed = allowed_pairs(query_seg, query_place, key_seg, key_place)[:, None, :]
        return (jnp.where(allowed, raw, floor_value), allowed)

    start_top = jnp.full((query_count, query_block, local_heads), floor_value, jnp.float32)
    start_total = jnp.zeros((query_count, query_block, local_heads), jnp.float32)
    start_sum = jnp.zeros((query_count, query_block, local_heads, HD), jnp.float32)
    piece = (
        lax.all_gather(head_keys, BLK, axis=0, tiled=True),
        lax.all_gather(head_values, BLK, axis=0, tiled=True),
    )
    tiles = key_tiles(piece[0], piece[1])

    def fold_per_query(args):
        query_tile, query_seg, query_place, running_top, running_total, running_sum = args

        def fold_per_key(state, key_args):
            key_tile, value_tile, key_seg, key_place = key_args
            top_old, total_old, sum_old = state
            scores, allowed = scores_of(
                query_tile, query_seg, query_place, key_tile, key_seg, key_place
            )
            top_new = jnp.maximum(top_old, jnp.max(scores, axis=-1))
            weights = jnp.where(allowed, jnp.exp(scores - top_new[..., None]), 0.0)
            fade = jnp.exp(top_old - top_new)
            total_new = total_old * fade + jnp.sum(weights, axis=-1)
            sum_new = sum_old * fade[..., None] + jnp.einsum(
                "qhk,khd->qhd",
                weights.astype(jnp.bfloat16),
                value_tile,
                preferred_element_type=jnp.float32,
            )
            return ((top_new, total_new, sum_new), None)

        state, unused = lax.scan(fold_per_key, (running_top, running_total, running_sum), tiles)
        return state

    top, total, summed = lax.map(
        fold_per_query, (query_tiles, seg_tiles, place_tiles, start_top, start_total, start_sum)
    )
    attended = summed / total[..., None]
    logsum = top + jnp.log(total)
    attended_low = attended.reshape(span, half).astype(jnp.bfloat16)
    mixed = lax.all_to_all(attended_low, HEAD, split_axis=0, concat_axis=1, tiled=True)
    first = rows + matmul(mixed, full.output_weight) + full.output_bias
    normed_cross = layer_norm(first, cross_gain_full, cross_shift_full).astype(jnp.bfloat16)
    probes = (matmul(normed_cross, full.probe_weight) + full.probe_bias).astype(jnp.bfloat16)
    lookups_own = matmul(encoded, full.lookup_weight).astype(jnp.bfloat16)
    contents_own = (matmul(encoded, full.content_weight) + full.content_bias).astype(
        jnp.bfloat16
    )
    lookups, contents = (
        lax.all_gather(lookups_own, ROW_AXES, axis=0, tiled=True),
        lax.all_gather(contents_own, ROW_AXES, axis=0, tiled=True),
    )
    memory_rows = lookups.shape[0]
    memory_keys = lookups.reshape(memory_rows, HEADS, HD)
    memory_values = contents.reshape(memory_rows, HEADS, HD)
    cross_block = math.gcd(local_rows, 256)
    cross_count = local_rows // cross_block
    probe_tiles = probes.reshape(cross_count, cross_block, HEADS, HD)

    def cross_scores(probe_tile):
        return (
            jnp.einsum("qhd,khd->qhk", probe_tile, memory_keys, preferred_element_type=jnp.float32)
            * scale
        )

    def cross_forward(probe_tile):
        scores = cross_scores(probe_tile)
        peak = jnp.max(scores, axis=-1, keepdims=True)
        weights = jnp.exp(scores - peak)
        weight_sum = jnp.sum(weights, axis=-1, keepdims=True)
        probs = (weights / weight_sum).astype(jnp.bfloat16)
        recalled_tile = jnp.einsum(
            "qhk,khd->qhd", probs, memory_values, preferred_element_type=jnp.float32
        )
        return (recalled_tile, (peak + jnp.log(weight_sum))[..., 0])

    recalled, cross_logsum = lax.map(cross_forward, probe_tiles)
    recalled_low = recalled.reshape(local_rows, width).astype(jnp.bfloat16)
    second = first + matmul(recalled_low, full.merged_weight) + full.merged_bias
    normed_feed = layer_norm(second, feed_gain_full, feed_shift_full).astype(jnp.bfloat16)
    hidden = matmul(normed_feed, full.up_weight) + full.up_bias
    active = exact_gelu(hidden).astype(jnp.bfloat16)
    output = second + matmul(active, full.down_weight) + full.down_bias
    output_low = output.astype(jnp.bfloat16)
    grads = types.SimpleNamespace()
    upstream = jnp.concatenate([cot_prompt, cot_cont], axis=0)
    grads.down_weight = left_product(active, upstream)
    grads.down_bias = column_sum(upstream)
    dactive = right_product(upstream, full.down_weight)
    unused, gelu_pull = jax.vjp(exact_gelu, hidden)
    dhidden = gelu_pull(dactive)[0].astype(jnp.bfloat16)
    grads.up_weight = left_product(normed_feed, dhidden)
    grads.up_bias = column_sum(dhidden)
    dnormed_feed = right_product(dhidden, full.up_weight)
    unused, feed_pull = jax.vjp(layer_norm, second, feed_gain_full, feed_shift_full)
    dsecond_part, grads.feed_gain, grads.feed_shift = feed_pull(dnormed_feed)
    dsecond = upstream.astype(jnp.float32) + dsecond_part
    dsecond_low = dsecond.astype(jnp.bfloat16)
    grads.merged_weight = left_product(recalled_low, dsecond_low)
    grads.merged_bias = column_sum(dsecond_low)
    drecalled = right_product(dsecond_low, full.merged_weight).astype(jnp.bfloat16)
    drecalled_tiles = drecalled.reshape(cross_count, cross_block, HEADS, HD)
    cross_delta = jnp.sum(drecalled_tiles.astype(jnp.float32) * recalled, axis=-1)

    def cross_backward(state, args):
        probe_tile, drecalled_tile, logsum_tile, delta_tile = args
        dlookups_acc, dcontents_acc = state
        scores = cross_scores(probe_tile)
        probs = jnp.exp(scores - logsum_tile[..., None])
        dprobs = jnp.einsum(
            "qhd,khd->qhk", drecalled_tile, memory_values, preferred_element_type=jnp.float32
        )
        dscores = (probs * (dprobs - delta_tile[..., None])).astype(jnp.bfloat16)
        dprobe_tile = (
            jnp.einsum("qhk,khd->qhd", dscores, memory_keys, preferred_element_type=jnp.float32)
            * scale
        )
        dlookups_acc = (
            dlookups_acc
            + jnp.einsum("qhk,qhd->khd", dscores, probe_tile, preferred_element_type=jnp.float32)
            * scale
        )
        dcontents_acc = dcontents_acc + jnp.einsum(
            "qhk,qhd->khd",
            probs.astype(jnp.bfloat16),
            drecalled_tile,
            preferred_element_type=jnp.float32,
        )
        return ((dlookups_acc, dcontents_acc), dprobe_tile)

    zero_memory = jnp.zeros((memory_rows, HEADS, HD), jnp.float32)
    (dlookups, dcontents), dprobes = lax.scan(
        cross_backward,
        (zero_memory, zero_memory),
        (probe_tiles, drecalled_tiles, cross_logsum, cross_delta),
    )
    mine_lookups, mine_contents = (
        lax.psum_scatter(
            dlookups.reshape(memory_rows, width).astype(jnp.bfloat16),
            ROW_AXES,
            scatter_dimension=0,
            tiled=True,
        ).astype(jnp.float32),
        lax.psum_scatter(
            dcontents.reshape(memory_rows, width).astype(jnp.bfloat16),
            ROW_AXES,
            scatter_dimension=0,
            tiled=True,
        ).astype(jnp.float32),
    )
    mine_lookups = mine_lookups.astype(jnp.bfloat16)
    mine_contents = mine_contents.astype(jnp.bfloat16)
    grads.lookup_weight = left_product(encoded, mine_lookups)
    grads.content_weight = left_product(encoded, mine_contents)
    grads.content_bias = column_sum(mine_contents)
    encoded_gradient = right_product(mine_lookups, full.lookup_weight) + right_product(
        mine_contents, full.content_weight
    )
    dprobes_low = dprobes.reshape(local_rows, width).astype(jnp.bfloat16)
    grads.probe_weight = left_product(normed_cross, dprobes_low)
    grads.probe_bias = column_sum(dprobes_low)
    dnormed_cross = right_product(dprobes_low, full.probe_weight)
    unused, cross_pull = jax.vjp(layer_norm, first, cross_gain_full, cross_shift_full)
    dfirst_part, grads.cross_gain, grads.cross_shift = cross_pull(dnormed_cross)
    dfirst = dsecond + dfirst_part
    dfirst_low = dfirst.astype(jnp.bfloat16)
    grads.output_weight = left_product(mixed, dfirst_low)
    grads.output_bias = column_sum(dfirst_low)
    dmixed = right_product(dfirst_low, full.output_weight).astype(jnp.bfloat16)
    head_dmixed = lax.all_to_all(dmixed, HEAD, split_axis=1, concat_axis=0, tiled=True)
    dmixed_tiles = head_dmixed.reshape(query_count, query_block, local_heads, HD)
    delta_tiles = jnp.sum(dmixed_tiles.astype(jnp.float32) * attended, axis=-1)
    start_dquery = jnp.zeros((query_count, query_block, local_heads, HD), jnp.float32)
    piece = (
        lax.all_gather(head_keys, BLK, axis=0, tiled=True),
        lax.all_gather(head_values, BLK, axis=0, tiled=True),
    )
    dquery_tiles = start_dquery
    count = piece[0].shape[0]
    block_dquery_tiles = dquery_tiles
    piece_keys = piece[0]
    block_tiles = key_tiles(piece_keys, piece[1])
    count = piece_keys.shape[0]

    def block_per_query(state, args):
        dkey_part, dvalue_part = state
        query_tile, query_seg, query_place, logsum_tile, delta_tile, dmixed_tile, dquery_tile = args

        def block_per_key(dquery_acc, key_args):
            key_tile, value_tile, key_seg, key_place = key_args
            scores, allowed = scores_of(
                query_tile, query_seg, query_place, key_tile, key_seg, key_place
            )
            probs = jnp.where(allowed, jnp.exp(scores - logsum_tile[..., None]), 0.0)
            dprobs = jnp.einsum(
                "qhd,khd->qhk", dmixed_tile, value_tile, preferred_element_type=jnp.float32
            )
            dscores = (probs * (dprobs - delta_tile[..., None])).astype(jnp.bfloat16)
            dquery_acc = (
                dquery_acc
                + jnp.einsum("qhk,khd->qhd", dscores, key_tile, preferred_element_type=jnp.float32)
                * scale
            )
            dkey_tile = (
                jnp.einsum("qhk,qhd->khd", dscores, query_tile, preferred_element_type=jnp.float32)
                * scale
            )
            dvalue_tile = jnp.einsum(
                "qhk,qhd->khd",
                probs.astype(jnp.bfloat16),
                dmixed_tile,
                preferred_element_type=jnp.float32,
            )
            return (dquery_acc, (dkey_tile, dvalue_tile))

        dquery_new, key_terms = lax.scan(block_per_key, dquery_tile, block_tiles)
        return ((dkey_part + key_terms[0], dvalue_part + key_terms[1]), dquery_new)

    zero_part = jnp.zeros(block_tiles[0].shape, jnp.float32)
    parts, block_dquery_tiles = lax.scan(
        block_per_query,
        (zero_part, zero_part),
        (
            query_tiles,
            seg_tiles,
            place_tiles,
            logsum,
            delta_tiles,
            dmixed_tiles,
            block_dquery_tiles,
        ),
    )
    dquery_tiles = block_dquery_tiles
    dkey_part = parts[0].reshape(count, half)
    dvalue_part = parts[1].reshape(count, half)
    dkey_rows = dkey_part
    dvalue_rows = dvalue_part
    dquery_tiles, dkey_rows, dvalue_rows = (dquery_tiles, dkey_rows, dvalue_rows)
    own_dkeys, own_dvalues = (
        lax.psum_scatter(
            dkey_rows.astype(jnp.bfloat16), BLK, scatter_dimension=0, tiled=True
        ).astype(jnp.float32),
        lax.psum_scatter(
            dvalue_rows.astype(jnp.bfloat16), BLK, scatter_dimension=0, tiled=True
        ).astype(jnp.float32),
    )
    row_dqueries, row_dkeys, row_dvalues = (
        lax.all_to_all(
            dquery_tiles.reshape(span, half).astype(jnp.bfloat16),
            HEAD,
            split_axis=0,
            concat_axis=1,
            tiled=True,
        ),
        lax.all_to_all(
            own_dkeys.astype(jnp.bfloat16), HEAD, split_axis=0, concat_axis=1, tiled=True
        ),
        lax.all_to_all(
            own_dvalues.astype(jnp.bfloat16), HEAD, split_axis=0, concat_axis=1, tiled=True
        ),
    )
    grads.query_weight = left_product(normed, row_dqueries)
    grads.query_bias = column_sum(row_dqueries)
    grads.key_weight = left_product(normed, row_dkeys)
    grads.value_weight = left_product(normed, row_dvalues)
    grads.value_bias = column_sum(row_dvalues)
    dnormed = (
        right_product(row_dqueries, full.query_weight)
        + right_product(row_dkeys, full.key_weight)
        + right_product(row_dvalues, full.value_weight)
    )
    unused, self_pull = jax.vjp(layer_norm, rows, self_gain_full, self_shift_full)
    drows_part, grads.self_gain, grads.self_shift = self_pull(dnormed)
    row_gradient = dfirst + drows_part
    shards = tuple(
        (
            lax.psum_scatter(
                grads.self_gain.astype(jnp.bfloat16),
                ROW_AXES,
                scatter_dimension=0,
                tiled=True,
            ).astype(jnp.float32),
            lax.psum_scatter(
                grads.self_shift.astype(jnp.bfloat16),
                ROW_AXES,
                scatter_dimension=0,
                tiled=True,
            ).astype(jnp.float32),
            lax.psum_scatter(
                grads.query_weight.astype(jnp.bfloat16),
                ROW_AXES,
                scatter_dimension=0,
                tiled=True,
            ).astype(jnp.float32),
            lax.psum_scatter(
                grads.query_bias.astype(jnp.bfloat16),
                ROW_AXES,
                scatter_dimension=0,
                tiled=True,
            ).astype(jnp.float32),
            lax.psum_scatter(
                grads.key_weight.astype(jnp.bfloat16),
                ROW_AXES,
                scatter_dimension=0,
                tiled=True,
            ).astype(jnp.float32),
            lax.psum_scatter(
                grads.value_weight.astype(jnp.bfloat16),
                ROW_AXES,
                scatter_dimension=0,
                tiled=True,
            ).astype(jnp.float32),
            lax.psum_scatter(
                grads.value_bias.astype(jnp.bfloat16),
                ROW_AXES,
                scatter_dimension=0,
                tiled=True,
            ).astype(jnp.float32),
            lax.psum_scatter(
                grads.output_weight.astype(jnp.bfloat16),
                ROW_AXES,
                scatter_dimension=0,
                tiled=True,
            ).astype(jnp.float32),
            lax.psum_scatter(
                grads.output_bias.astype(jnp.bfloat16),
                ROW_AXES,
                scatter_dimension=0,
                tiled=True,
            ).astype(jnp.float32),
            lax.psum_scatter(
                grads.cross_gain.astype(jnp.bfloat16),
                ROW_AXES,
                scatter_dimension=0,
                tiled=True,
            ).astype(jnp.float32),
            lax.psum_scatter(
                grads.cross_shift.astype(jnp.bfloat16),
                ROW_AXES,
                scatter_dimension=0,
                tiled=True,
            ).astype(jnp.float32),
            lax.psum_scatter(
                grads.probe_weight.astype(jnp.bfloat16),
                ROW_AXES,
                scatter_dimension=0,
                tiled=True,
            ).astype(jnp.float32),
            lax.psum_scatter(
                grads.probe_bias.astype(jnp.bfloat16),
                ROW_AXES,
                scatter_dimension=0,
                tiled=True,
            ).astype(jnp.float32),
            lax.psum_scatter(
                grads.lookup_weight.astype(jnp.bfloat16),
                ROW_AXES,
                scatter_dimension=0,
                tiled=True,
            ).astype(jnp.float32),
            lax.psum_scatter(
                grads.content_weight.astype(jnp.bfloat16),
                ROW_AXES,
                scatter_dimension=0,
                tiled=True,
            ).astype(jnp.float32),
            lax.psum_scatter(
                grads.content_bias.astype(jnp.bfloat16),
                ROW_AXES,
                scatter_dimension=0,
                tiled=True,
            ).astype(jnp.float32),
            lax.psum_scatter(
                grads.merged_weight.astype(jnp.bfloat16),
                ROW_AXES,
                scatter_dimension=0,
                tiled=True,
            ).astype(jnp.float32),
            lax.psum_scatter(
                grads.merged_bias.astype(jnp.bfloat16),
                ROW_AXES,
                scatter_dimension=0,
                tiled=True,
            ).astype(jnp.float32),
            lax.psum_scatter(
                grads.feed_gain.astype(jnp.bfloat16),
                ROW_AXES,
                scatter_dimension=0,
                tiled=True,
            ).astype(jnp.float32),
            lax.psum_scatter(
                grads.feed_shift.astype(jnp.bfloat16),
                ROW_AXES,
                scatter_dimension=0,
                tiled=True,
            ).astype(jnp.float32),
            lax.psum_scatter(
                grads.up_weight.astype(jnp.bfloat16),
                ROW_AXES,
                scatter_dimension=0,
                tiled=True,
            ).astype(jnp.float32),
            lax.psum_scatter(
                grads.up_bias.astype(jnp.bfloat16),
                ROW_AXES,
                scatter_dimension=0,
                tiled=True,
            ).astype(jnp.float32),
            lax.psum_scatter(
                grads.down_weight.astype(jnp.bfloat16),
                ROW_AXES,
                scatter_dimension=0,
                tiled=True,
            ).astype(jnp.float32),
            lax.psum_scatter(
                grads.down_bias.astype(jnp.bfloat16),
                ROW_AXES,
                scatter_dimension=0,
                tiled=True,
            ).astype(jnp.float32),
        )
    )
    return (
        output_low[:prompt_rows],
        output_low[prompt_rows:],
        row_gradient[:prompt_rows],
        row_gradient[prompt_rows:],
        encoded_gradient,
    ) + shards


NT = (((1,), (1,)), ((), ()))
TN = (((0,), (0,)), ((), ()))
PAIR = 2 * HD
TILE = 256
VMEM_BYTES = 56 * 1024 * 1024


def dot(left, right, dims=(((1,), (0,)), ((), ()))):
    return lax.dot_general(left, right, dims, preferred_element_type=jnp.float32)


def first_lanes(shape):
    return lax.broadcasted_iota(jnp.int32, shape, len(shape) - 1) < HD


def split_heads(values, fill=0.0):
    mine = first_lanes(values.shape)
    other = jnp.full(values.shape, fill, values.dtype)
    return jnp.where(mine, values, other), jnp.where(mine, other, values)


def fold(state, query, key, value, allowed=None):
    top, acc = state
    scores = dot(query, key, NT)
    if allowed is not None:
        scores = jnp.where(allowed, scores, floor_value)
    top_new = jnp.maximum(top, jnp.max(scores, axis=1, keepdims=True))
    weights = jnp.exp(scores - top_new).astype(jnp.bfloat16)
    acc_new = acc * jnp.exp(top - top_new) + dot(weights, value)
    return top_new, acc_new


def close(state0, state1):
    top0, acc0 = state0
    top1, acc1 = state1
    mine = first_lanes(acc0.shape)
    total = jnp.where(mine, pltpu.roll(acc0, HD, 1), pltpu.roll(acc1, HD, 1))
    result = jnp.where(mine, acc0, acc1) / total
    logsum = jnp.where(mine, top0, top1) + jnp.log(total)
    turned = jnp.transpose(logsum)
    return result, turned[0:1], turned[HD : HD + 1]


def segment_start(place, bounds_ref):
    start = jnp.zeros_like(place)
    for at in range(bounds_ref.shape[0] - 1):
        start = jnp.where(place >= bounds_ref[at], bounds_ref[at], start)
    return start


SLAB_OF = (0, 2, 1, 3)
COLUMN_OF = (1, 3, 0, 2)


def shard_of(role):
    quarter, side = role >> 1, role & 1
    return (((quarter & 1) << 1) | (quarter >> 1)) * 2 + side


def natural_rows(role, total, prompt_all):
    local_rows, prompt_rows = total // 8, prompt_all // 8
    order = shard_of(role)
    pieces = []
    for low, high, base in (
        (0, prompt_rows, order * prompt_rows),
        (prompt_rows, local_rows, prompt_all + order * (local_rows - prompt_rows)),
    ):
        if not isinstance(base, int):
            base = pl.multiple_of(base, prompt_rows)
        pieces.append((low, high, pl.ds(base, high - low)))
    return pieces


def group_pieces(groups, lines_ref, total, prompt_all):
    pieces = []
    at = 0
    for group in groups:
        for place in range(group.shape[0]):
            for low, high, where in natural_rows(lines_ref[at], total, prompt_all):
                pieces.append((group, place, low, high, where))
            at += 1
    return pieces


def self_forward_kernel(
    prompt_all,
    lines_ref,
    bounds_ref,
    near_ref,
    next_ref,
    far_ref,
    att_ref,
    low_ref,
    lse_ref,
    qn,
    kn,
    v0n,
    v1n,
):
    groups = (near_ref, next_ref, far_ref)
    total = qn.shape[0]
    for group, place, low, high, where in group_pieces(groups, lines_ref, total, prompt_all):
        qn[where] = group[place, low:high, 0:PAIR] * jnp.bfloat16(HD**-0.5)
        kn[where] = group[place, low:high, PAIR : 2 * PAIR]
        v0n[where], v1n[where] = split_heads(group[place, low:high, 2 * PAIR : 3 * PAIR], 1.0)

    prompt_tiles = prompt_all // TILE
    tiles = qn.shape[0] // TILE
    start = (
        jnp.full((TILE, 1), floor_value, jnp.float32),
        jnp.zeros((TILE, PAIR), jnp.float32),
    )

    def both(state, query, base, size, allowed=None):
        key = kn[pl.ds(base, size)]
        return (
            fold(state[0], query[0], key, v0n[pl.ds(base, size)], allowed),
            fold(state[1], query[1], key, v1n[pl.ds(base, size)], allowed),
        )

    def finish(tile, state):
        result, lse0, lse1 = close(*state)
        att_ref[pl.ds(tile * TILE, TILE)] = result
        lse_ref[tile, 0:1, :] = lse0
        lse_ref[tile, 1:2, :] = lse1

    query_at = lax.broadcasted_iota(jnp.int32, (TILE, TILE), 0)
    key_at = lax.broadcasted_iota(jnp.int32, (TILE, TILE), 1)

    def prompt_tile(tile, carry):
        query = split_heads(qn[pl.ds(tile * TILE, TILE)])
        state = lax.fori_loop(
            0, tile, lambda at, now: both(now, query, at * TILE, TILE), (start, start)
        )
        state = both(state, query, tile * TILE, TILE, key_at <= query_at)
        finish(tile, state)
        return carry

    lax.fori_loop(0, prompt_tiles, prompt_tile, 0)

    def cont_tile(tile, carry):
        query = split_heads(qn[pl.ds(tile * TILE, TILE)])
        state = (start, start)
        for at in range(0, prompt_all, 2 * TILE):
            state = both(state, query, at, 2 * TILE)
        first_place = tile * TILE - prompt_all
        place = first_place + query_at
        begin = segment_start(place, bounds_ref)

        def cont_step(at, now):
            key_place = at * TILE - prompt_all + key_at
            return both(now, query, at * TILE, TILE, (key_place <= place) & (key_place >= begin))

        first_key = prompt_tiles + segment_start(first_place, bounds_ref) // TILE
        state = lax.fori_loop(first_key, tile + 1, cont_step, state)
        finish(tile, state)
        return carry

    lax.fori_loop(prompt_tiles, tiles, cont_tile, 0)
    for role in range(8):
        for low, high, where in natural_rows(role, total, prompt_all):
            low_ref[role, low:high] = att_ref[where].astype(jnp.bfloat16)


def unfold(query, key, value, grad, lse, delta, allowed=None):
    probs = jnp.exp(dot(key, query, NT) - lse)
    if allowed is not None:
        probs = jnp.where(allowed, probs, 0.0)
    dscores = (probs * (dot(value, grad, NT) - delta)).astype(jnp.bfloat16)
    return probs.astype(jnp.bfloat16), dscores


def head_inner(left, right):
    turned = jnp.transpose(left * right)
    return (
        jnp.sum(turned[:HD], axis=0, keepdims=True),
        jnp.sum(turned[HD:], axis=0, keepdims=True),
    )


def self_backward_kernel(
    prompt_all,
    lines_ref,
    bounds_ref,
    near_ref,
    next_ref,
    far_ref,
    grad_ref,
    att_ref,
    lse_ref,
    near_out,
    next_out,
    far_out,
    qn,
    kn,
    vn,
    gn,
    dqn,
    dkn,
    dvn,
):
    total = qn.shape[0]
    groups = (near_ref, next_ref, far_ref)
    for group, place, low, high, where in group_pieces(groups, lines_ref, total, prompt_all):
        qn[where] = group[place, low:high, 0:PAIR] * jnp.bfloat16(HD**-0.5)
        kn[where] = group[place, low:high, PAIR : 2 * PAIR]
        vn[where] = group[place, low:high, 2 * PAIR : 3 * PAIR]
    for role in range(8):
        for low, high, where in natural_rows(role, total, prompt_all):
            gn[where] = grad_ref[role, low:high]
    dkn[...] = jnp.zeros_like(dkn)
    dvn[...] = jnp.zeros_like(dvn)
    prompt_tiles = prompt_all // TILE
    tiles = qn.shape[0] // TILE
    key_at = lax.broadcasted_iota(jnp.int32, (TILE, TILE), 0)
    query_at = lax.broadcasted_iota(jnp.int32, (TILE, TILE), 1)

    def load(tile):
        query = split_heads(qn[pl.ds(tile * TILE, TILE)])
        whole = gn[pl.ds(tile * TILE, TILE)]
        grad = split_heads(whole)
        delta = head_inner(whole.astype(jnp.float32), att_ref[pl.ds(tile * TILE, TILE)])
        lse = (lse_ref[tile, 0:1, :], lse_ref[tile, 1:2, :])
        return query, grad, lse, delta

    def step(acc, query, grad, lse, delta, base, allowed=None):
        where = pl.ds(base, TILE)
        key, value = kn[where], vn[where]
        keys = split_heads(key)
        dkey, dvalue = dkn[where], dvn[where]
        for side in range(2):
            probs, dscores = unfold(
                query[side], key, value, grad[side], lse[side], delta[side], allowed
            )
            dvalue = dvalue + dot(probs, grad[side])
            dkey = dkey + dot(dscores, query[side])
            acc = acc + dot(dscores, keys[side], TN)
        dkn[where] = dkey
        dvn[where] = dvalue
        return acc

    def finish(tile, acc):
        dqn[pl.ds(tile * TILE, TILE)] = (acc * HD**-0.5).astype(jnp.bfloat16)

    start = jnp.zeros((TILE, PAIR), jnp.float32)

    def prompt_tile(tile, carry):
        given = load(tile)
        acc = lax.fori_loop(0, tile, lambda at, now: step(now, *given, at * TILE), start)
        acc = step(acc, *given, tile * TILE, key_at <= query_at)
        finish(tile, acc)
        return carry

    lax.fori_loop(0, prompt_tiles, prompt_tile, 0)

    def cont_tile(tile, carry):
        given = load(tile)
        acc = lax.fori_loop(0, prompt_tiles, lambda at, now: step(now, *given, at * TILE), start)
        first_place = tile * TILE - prompt_all
        place = first_place + query_at
        begin = segment_start(place, bounds_ref)

        def cont_step(at, now):
            key_place = at * TILE - prompt_all + key_at
            return step(now, *given, at * TILE, (key_place <= place) & (key_place >= begin))

        first_key = prompt_tiles + segment_start(first_place, bounds_ref) // TILE
        acc = lax.fori_loop(first_key, tile + 1, cont_step, acc)
        finish(tile, acc)
        return carry

    lax.fori_loop(prompt_tiles, tiles, cont_tile, 0)
    outs = (near_out, next_out, far_out)
    for group, place, low, high, where in group_pieces(outs, lines_ref, total, prompt_all):
        group[place, low:high, 0:PAIR] = dqn[where]
        group[place, low:high, PAIR : 2 * PAIR] = dkn[where].astype(jnp.bfloat16)
        group[place, low:high, 2 * PAIR : 3 * PAIR] = dvn[where].astype(jnp.bfloat16)


def cost(micros):
    return pl.CostEstimate(
        flops=int(micros * 9e8), bytes_accessed=int(micros * 2e6), transcendentals=0
    )


def in_vmem(count):
    return [pl.BlockSpec(memory_space=pltpu.VMEM)] * count


def in_smem(count):
    return [pl.BlockSpec(memory_space=pltpu.SMEM)] * count


def self_forward(lines, bounds, groups, prompt_all):
    local_rows = groups[0].shape[1]
    total = 8 * local_rows
    natural = pltpu.VMEM((total, PAIR), jnp.bfloat16)
    return pl.pallas_call(
        functools.partial(self_forward_kernel, prompt_all),
        out_shape=(
            jax.ShapeDtypeStruct((total, PAIR), jnp.float32),
            jax.ShapeDtypeStruct((8, local_rows, PAIR), jnp.bfloat16),
            jax.ShapeDtypeStruct((total // TILE, 2, TILE), jnp.float32),
        ),
        in_specs=in_smem(2) + in_vmem(3),
        out_specs=tuple(in_vmem(3)),
        scratch_shapes=[natural] * 4,
        compiler_params=pltpu.CompilerParams(vmem_limit_bytes=VMEM_BYTES),
        cost_estimate=cost(44),
        name="self_forward",
    )(lines, bounds, *groups)


def self_backward(lines, bounds, groups, grad, att, lse, prompt_all):
    total = 8 * groups[0].shape[1]
    natural = pltpu.VMEM((total, PAIR), jnp.bfloat16)
    wide = pltpu.VMEM((total, PAIR), jnp.float32)
    return pl.pallas_call(
        functools.partial(self_backward_kernel, prompt_all),
        out_shape=tuple(jax.ShapeDtypeStruct(group.shape, jnp.bfloat16) for group in groups),
        in_specs=in_smem(2) + in_vmem(6),
        out_specs=tuple(in_vmem(3)),
        scratch_shapes=[natural] * 5 + [wide] * 2,
        compiler_params=pltpu.CompilerParams(vmem_limit_bytes=VMEM_BYTES),
        cost_estimate=cost(60),
        name="self_backward",
    )(lines, bounds, *groups, grad, att, lse)


def pick(refs, target):
    at = pl.program_id(0)
    for place, ref in enumerate(refs):

        @pl.when(at == place)
        def unused(ref=ref):
            target[...] = ref[0 : target.shape[0]]


def project_kernel(count, *refs):
    gain_ref, shift_ref, weight_ref, bias_ref = refs[count : count + 4]
    normed_ref, rows_ref, chunk = refs[count + 4 :]
    pick(refs[:count], chunk)
    unit, unused = norm_parts(chunk[...].astype(jnp.float32))
    normed = (unit * gain_ref[...] + shift_ref[...]).astype(jnp.bfloat16)
    normed_ref[0] = normed
    rows_ref[0] = (dot(normed, weight_ref[...]) + bias_ref[...]).astype(jnp.bfloat16)


def fixed(shape):
    return pl.BlockSpec(shape, lambda at, *unused: (0,) * len(shape), pipeline_mode=pl.Buffered(1))


def stepped(shape):
    return pl.BlockSpec((1,) + shape, lambda at, *unused: (at,) + (0,) * len(shape))


def project(chunks, rows, gain, shift, weight, bias):
    count = len(chunks)
    width, columns = weight.shape
    return pl.pallas_call(
        functools.partial(project_kernel, count),
        grid=(count,),
        out_shape=(
            jax.ShapeDtypeStruct((count, rows, width), jnp.bfloat16),
            jax.ShapeDtypeStruct((count, rows, columns), jnp.bfloat16),
        ),
        in_specs=[fixed(chunk.shape) for chunk in chunks]
        + [fixed((1, width)), fixed((1, width)), fixed(weight.shape), fixed((1, columns))],
        out_specs=(stepped((rows, width)), stepped((rows, columns))),
        scratch_shapes=[pltpu.VMEM((rows, width), jnp.bfloat16)],
        compiler_params=pltpu.CompilerParams(vmem_limit_bytes=VMEM_BYTES),
        cost_estimate=cost(2.3 * count),
        name="project",
    )(*chunks, gain[None], shift[None], weight, bias[None])


def feed_kernel(count, *refs):
    chunks, upstreams = refs[:count], refs[count : 2 * count]
    weights_ref, bias_ref = refs[2 * count : 2 * count + 2]
    sums_ref, feed_ref, upstream_ref, active_ref, dhidden_ref = refs[2 * count + 2 :]
    pick(chunks, feed_ref.at[0])
    pick(upstreams, upstream_ref.at[0])
    feed = feed_ref[0]
    upstream = upstream_ref[0]
    blocks, both, width = weights_ref.shape
    step = both // 2
    out = None
    for low in range(0, blocks * step, step):
        where = slice(low, low + step)
        up = weights_ref[:, :step, where].reshape(blocks * step, step)
        down = weights_ref[low // step, step:]
        hidden = dot(feed, up) + bias_ref[:, where]
        tail = 0.5 + 0.5 * lax.erf(hidden * math.sqrt(0.5))
        active = (hidden * tail).astype(jnp.bfloat16)
        slope = tail + hidden * jnp.exp(-0.5 * hidden * hidden) * (1.0 / math.sqrt(2.0 * math.pi))
        dhidden = (dot(upstream, down, NT) * slope).astype(jnp.bfloat16)
        active_ref[0, :, where] = active
        dhidden_ref[0, :, where] = dhidden
        term, dterm = dot(active, down), dot(dhidden, up, NT)
        out, dnormed = (term, dterm) if out is None else (out + term, dnormed + dterm)
    rows = feed.shape[0]
    sums_ref[0, :rows] = dnormed.astype(jnp.bfloat16)
    sums_ref[0, rows:] = out.astype(jnp.bfloat16)


def feed(chunks, upstreams, weights, bias):
    count = len(chunks)
    rows, width = chunks[0].shape
    columns = bias.shape[0]
    return pl.pallas_call(
        functools.partial(feed_kernel, count),
        grid=(count,),
        in_specs=[fixed((rows, width))] * (2 * count)
        + [fixed(weights.shape), fixed((1, columns))],
        out_specs=[stepped((2 * rows, width))]
        + [stepped((rows, width))] * 2
        + [stepped((rows, columns))] * 2,
        out_shape=[jax.ShapeDtypeStruct((count, 2 * rows, width), jnp.bfloat16)]
        + [jax.ShapeDtypeStruct((count, rows, width), jnp.bfloat16)] * 2
        + [jax.ShapeDtypeStruct((count, rows, columns), jnp.bfloat16)] * 2,
        compiler_params=pltpu.CompilerParams(vmem_limit_bytes=VMEM_BYTES),
        cost_estimate=cost(6.5 * count),
        name="feed",
    )(*chunks, *upstreams, weights, bias[None])


def cross_forward_kernel(probe_ref, lookup_ref, content_ref, out_ref, lse_ref):
    query = split_heads(probe_ref[...] * jnp.bfloat16(HD**-0.5))
    key = lookup_ref[...]
    values = split_heads(content_ref[...], 1.0)
    rows = query[0].shape[0]
    start = (jnp.full((rows, 1), floor_value, jnp.float32), jnp.zeros((rows, PAIR), jnp.float32))
    states = [fold(start, query[side], key, values[side]) for side in range(2)]
    result, lse0, lse1 = close(*states)
    out_ref[...] = result
    lse_ref[0, 0:1, :] = lse0
    lse_ref[0, 1:2, :] = lse1


def cross_backward_kernel(
    probe_ref,
    lookup_ref,
    content_ref,
    grad_ref,
    out_ref,
    lse_ref,
    lookup_weight_ref,
    content_weight_ref,
    dprobe_ref,
    dmemory_ref,
    dencoded_ref,
    dencoded,
):
    query = split_heads(probe_ref[...] * jnp.bfloat16(HD**-0.5))
    key = lookup_ref[...]
    keys = split_heads(key)
    value = content_ref[...]
    whole = grad_ref[...]
    grad = split_heads(whole)
    delta = head_inner(whole.astype(jnp.float32), out_ref[...])
    terms = []
    for side in range(2):
        probs, dscores = unfold(
            query[side], key, value, grad[side], lse_ref[0, side : side + 1, :], delta[side]
        )
        terms.append(
            (
                dot(dscores, keys[side], TN),
                dot(dscores, query[side]),
                dot(probs, grad[side]),
            )
        )
    dprobe_ref[...] = ((terms[0][0] + terms[1][0]) * HD**-0.5).astype(jnp.bfloat16)
    dlookup = (terms[0][1] + terms[1][1]).astype(jnp.bfloat16)
    dcontent = (terms[0][2] + terms[1][2]).astype(jnp.bfloat16)
    rows = dmemory_ref.shape[1] // 2
    for block in range(8):
        columns = slice(block * PAIR, (block + 1) * PAIR)
        dmemory_ref[0, :rows, columns] = dlookup[block * rows : (block + 1) * rows]
        dmemory_ref[0, rows:, columns] = dcontent[block * rows : (block + 1) * rows]
    term = dot(dlookup, lookup_weight_ref[...], NT) + dot(dcontent, content_weight_ref[...], NT)

    @pl.when(pl.program_id(0) == 0)
    def begin():
        dencoded[...] = term

    @pl.when(pl.program_id(0) > 0)
    def more():
        dencoded[...] += term

    @pl.when(pl.program_id(0) == 7)
    def end():
        dencoded_ref[...] = dencoded[...].astype(jnp.bfloat16)


def pair_block(rows):
    return pl.BlockSpec((rows, PAIR), lambda at: (0, at))


def cross_forward(probes, lookups, contents):
    rows, width = probes.shape
    memory = lookups.shape[0]
    pairs = width // PAIR
    return pl.pallas_call(
        cross_forward_kernel,
        grid=(pairs,),
        out_shape=(
            jax.ShapeDtypeStruct((rows, width), jnp.float32),
            jax.ShapeDtypeStruct((pairs, 2, rows), jnp.float32),
        ),
        in_specs=[pair_block(rows), pair_block(memory), pair_block(memory)],
        out_specs=(pair_block(rows), pl.BlockSpec((1, 2, rows), lambda at: (at, 0, 0))),
        compiler_params=pltpu.CompilerParams(vmem_limit_bytes=VMEM_BYTES),
        cost_estimate=cost(10),
        name="cross_forward",
    )(probes, lookups, contents)


def cross_backward(probes, lookups, contents, grad, recalled, lse, lookup_weight, content_weight):
    rows, width = probes.shape
    memory = lookups.shape[0]
    pairs = width // PAIR
    return pl.pallas_call(
        cross_backward_kernel,
        grid=(pairs,),
        out_shape=(
            jax.ShapeDtypeStruct((rows, width), jnp.bfloat16),
            jax.ShapeDtypeStruct((pairs, 2 * memory // 8, width), jnp.bfloat16),
            jax.ShapeDtypeStruct((memory, width), jnp.bfloat16),
        ),
        in_specs=[
            pair_block(rows),
            pair_block(memory),
            pair_block(memory),
            pair_block(rows),
            pair_block(rows),
            pl.BlockSpec((1, 2, rows), lambda at: (at, 0, 0)),
            pair_block(width),
            pair_block(width),
        ],
        out_specs=(
            pair_block(rows),
            pl.BlockSpec((1, 2 * memory // 8, width), lambda at: (at, 0, 0)),
            fixed((memory, width)),
        ),
        scratch_shapes=[pltpu.VMEM((memory, width), jnp.float32)],
        compiler_params=pltpu.CompilerParams(vmem_limit_bytes=VMEM_BYTES),
        cost_estimate=cost(20),
        name="cross_backward",
    )(probes, lookups, contents, grad, recalled, lse, lookup_weight, content_weight)


def norm_parts(values):
    center = jnp.mean(values, axis=-1, keepdims=True)
    centred = values - center
    spread = jnp.mean(centred * centred, axis=-1, keepdims=True)
    rate = lax.rsqrt(spread + 1e-05)
    return centred * rate, rate


def norm_backward(grad, unit, rate, gain):
    scaled = grad * gain
    along = jnp.mean(scaled, axis=-1, keepdims=True)
    across = jnp.mean(scaled * unit, axis=-1, keepdims=True)
    return (
        rate * (scaled - along - unit * across),
        jnp.sum(grad * unit, axis=0),
        jnp.sum(grad, axis=0),
    )


def joined(group, block, side=0, sides=1):
    return (group * 4 + block) * sides + side


class Slab:
    def __init__(self):
        group, side = lax.axis_index(GRP), lax.axis_index(HEAD)
        self.group, self.side, self.block = group, side, lax.axis_index(BLK)
        column, core = group // 2, group % 2
        chips = ((0, 0), (1, 0), (1, 1), (0, 1))
        lines = [[4 * left + 2 * own + right for left, right in chips] for own in range(2)]
        self.forward = [(line[at], line[(at + 1) % 4]) for line in lines for at in range(4)]
        self.reverse = [(right, left) for left, right in self.forward]
        self.cores = [(role, role ^ 2) for role in range(8)]
        place = jnp.where(column == 0, 3 * side, 1 + side)
        owners = []
        for step, other in ((0, 0), (0, 1), (-1, 0), (1, 0), (-1, 1), (1, 1), (2, 0), (2, 1)):
            there = (place + step) % 4
            far = ((there == 1) | (there == 2)).astype(jnp.int32)
            owners.append(4 * far + 2 * ((core + other) % 2) + (there >= 2).astype(jnp.int32))
        self.lines = jnp.stack(owners).astype(jnp.int32)

    def up(self, values):
        return lax.ppermute(values, ROLE_AXES, self.forward)

    def down(self, values):
        return lax.ppermute(values, ROLE_AXES, self.reverse)

    def swap(self, values):
        return lax.ppermute(values, ROLE_AXES, self.cores)

    def gather(self, values, gates=(None, None)):
        half = values.shape[0] // 2
        left, right, other = self.up(values), self.down(values), self.swap(values)
        if gates[0] is not None:
            left, right, other = after((left, right, other), gates[0])
        pair = (self.up(left[:half]), self.down(right[half:]))
        near, far = self.swap(left), self.swap(right)
        if gates[1] is not None:
            pair, near, far = after((pair, near, far), gates[1])
        last = jnp.concatenate(pair, axis=0)
        return ((values, other), (left, right, near, far), (last, self.swap(last)))

    def scatter(self, near, after_parts, far, gates=(None, None, None)):
        low, wide = jnp.bfloat16, jnp.float32
        swaps = [self.swap(far[1]), self.swap(after_parts[2:4]), self.swap(near[1])]
        if gates[0] is not None:
            swaps = after(swaps, gates[0])
        last = far[0].astype(wide) + swaps[0]
        half = last.shape[0] // 2
        sent = (self.up(last[:half].astype(low)), self.down(last[half:].astype(low)))
        if gates[1] is not None:
            sent = after(sent, gates[1])
        self.mark = left, right = sent
        pair = after_parts[0:2].astype(wide) + swaps[1]
        behind, ahead = pair[0], pair[1]
        left = jnp.concatenate([left + ahead[:half], ahead[half:]], axis=0).astype(low)
        right = jnp.concatenate([behind[:half], right + behind[half:]], axis=0).astype(low)
        sent = (self.up(left), self.down(right))
        if gates[2] is not None:
            sent = after(sent, gates[2])
        return near[0].astype(wide) + swaps[2] + sent[0] + sent[1]

    def enter(self, values):
        moves = [
            (joined(group, block), joined(SLAB_OF[block], SLAB_OF[group]))
            for group in range(4)
            for block in range(4)
        ]
        return lax.ppermute(values, (GRP, BLK), moves)

    def leave(self, values):
        moves = [
            (joined(group, block), joined(SLAB_OF[block], SLAB_OF[group]))
            for group in range(4)
            for block in range(4)
        ]
        return lax.ppermute(values, (GRP, BLK), moves)

    def leave_columns(self, values):
        moves = [
            (joined(group, block), joined(SLAB_OF[block], COLUMN_OF[group]))
            for group in range(4)
            for block in range(4)
        ]
        return lax.ppermute(values, (GRP, BLK), moves)

    def leave_quarters(self, pieces):
        result = []
        for at, piece in enumerate(pieces):
            moves = [
                (joined(group, block), joined(SLAB_OF[block], group ^ at))
                for group in range(4)
                for block in range(4)
            ]
            result.append(lax.ppermute(piece, (GRP, BLK), moves))
        return result

    def settle(self, parts, blank):
        for at, part in enumerate(parts):
            start = (self.block ^ at,) + (0,) * part.ndim
            blank = lax.dynamic_update_slice(blank, part[None].astype(blank.dtype), start)
        return blank

    def leave_own(self, values):
        moves = [
            (joined(group, block, side, 2), joined(SLAB_OF[block], group, side, 2))
            for group in range(4)
            for block in range(4)
            for side in range(2)
        ]
        return lax.ppermute(values, ALL_AXES, moves)


def by_role(values, order=SLAB_OF):
    values = values.reshape((4, 2, -1) + values.shape[1:])
    values = jnp.stack([values[at] for at in order])
    return values.reshape((8,) + values.shape[2:])


def after(values, *others):
    return lax.optimization_barrier((values,) + others)[0]


def exchange(values, axes):
    return lax.all_to_all(values, axes, split_axis=0, concat_axis=0, tiled=True)


def columns_kernel(pieces_ref, out_ref):
    part = pieces_ref.shape[2] // 4
    for role in range(8):
        for block in range(4):
            order = (block * 2 + role % 2) * 4 + role // 2
            out_ref[:, order * part : (order + 1) * part] = pieces_ref[
                role, :, block * part : (block + 1) * part
            ].astype(jnp.float32)


def settle_columns(pieces):
    roles, rows, columns = pieces.shape
    return pl.pallas_call(
        columns_kernel,
        out_shape=jax.ShapeDtypeStruct((rows, roles * columns), jnp.float32),
        in_specs=in_vmem(1),
        out_specs=pl.BlockSpec(memory_space=pltpu.VMEM),
        compiler_params=pltpu.CompilerParams(vmem_limit_bytes=VMEM_BYTES),
        cost_estimate=cost(4),
        name="settle_columns",
    )(pieces)


def heads_kernel(pieces_ref, *outs):
    for role in range(8):
        for place, out_ref in enumerate(outs):
            out_ref[:, role * PAIR : (role + 1) * PAIR] = pieces_ref[
                role, :, place * PAIR : (place + 1) * PAIR
            ].astype(jnp.float32)


def settle_heads(pieces):
    roles, rows, columns = pieces.shape
    count = columns // PAIR
    return pl.pallas_call(
        heads_kernel,
        out_shape=(jax.ShapeDtypeStruct((rows, roles * PAIR), jnp.float32),) * count,
        in_specs=in_vmem(1),
        out_specs=tuple(in_vmem(count)),
        compiler_params=pltpu.CompilerParams(vmem_limit_bytes=VMEM_BYTES),
        cost_estimate=cost(3),
        name="settle_heads",
    )(pieces)


def head_body(
    prompt,
    continued,
    encoded,
    cont_lengths,
    self_gain,
    self_shift,
    query_weight,
    query_bias,
    key_weight,
    value_weight,
    value_bias,
    output_weight,
    output_bias,
    cross_gain,
    cross_shift,
    probe_weight,
    probe_bias,
    lookup_weight,
    content_weight,
    content_bias,
    merged_weight,
    merged_bias,
    feed_gain,
    feed_shift,
    up_weight,
    up_bias,
    down_weight,
    down_bias,
    cot_prompt,
    cot_cont,
):
    slab = Slab()
    low = jnp.bfloat16
    width = prompt.shape[1]
    shard = width // 8
    piece = shard // 4
    prompt_rows = prompt.shape[0]
    local_rows = prompt_rows + continued.shape[0]
    prompt_all = 8 * prompt_rows
    memory_rows = encoded.shape[0]
    quarter, side = slab.group, slab.side
    role = 2 * quarter + side

    swapped = [
        (joined(group, block), joined(block, SLAB_OF[group]))
        for group in range(4)
        for block in range(4)
    ]
    lengths = lax.ppermute(cont_lengths, (GRP, BLK), swapped)
    bounds = jnp.cumsum(lengths).astype(jnp.int32)

    own_all = slab.enter(jnp.concatenate([prompt, continued, encoded], axis=0))

    def head_columns(weight):
        mine = lax.dynamic_slice_in_dim(weight.reshape(shard, 4, 2 * shard), quarter, 1, axis=1)
        return mine.reshape(shard, 2, shard).transpose(1, 0, 2)

    small = (
        self_gain,
        self_shift,
        output_bias,
        cross_gain,
        cross_shift,
        probe_bias,
        merged_bias,
        feed_gain,
        feed_shift,
        down_bias,
        content_bias,
        query_bias,
        value_bias,
    )
    vectors = jnp.concatenate(small + (up_bias,) + (self_gain,) * 3).reshape(1, 8, 3 * shard)
    mixed_in = jnp.concatenate(
        [
            jnp.concatenate(
                [head_columns(query_weight), head_columns(key_weight), head_columns(value_weight)],
                axis=2,
            ),
            jnp.broadcast_to(vectors, (2, 8, 3 * shard)),
        ],
        axis=1,
    )
    mixed_in = jnp.broadcast_to(mixed_in[None], (4,) + mixed_in.shape)
    mixed_in = exchange(mixed_in.reshape(8, shard + 8, 3 * shard), ROW_AXES)
    own_all, mixed_in = lax.optimization_barrier((own_all, mixed_in))
    head_weights = mixed_in[:, :shard].reshape(width, 3 * shard)
    vectors = mixed_in[:, shard:].reshape(8, 24, shard)
    packed = vectors[:, : len(small)].transpose(1, 0, 2).reshape(len(small), width)
    (
        self_gain_full,
        self_shift_full,
        output_bias_full,
        cross_gain_full,
        cross_shift_full,
        probe_bias_full,
        merged_bias_full,
        feed_gain_full,
        feed_shift_full,
        down_bias_full,
        content_bias_full,
        query_bias_full,
        value_bias_full,
    ) = [packed[at].astype(jnp.float32) for at in range(len(small))]
    ups = vectors[:, len(small) : len(small) + 8].reshape(4, 2, 4, -1)
    ups = lax.dynamic_index_in_dim(ups, side, 1, keepdims=False)
    up_bias_own = lax.dynamic_index_in_dim(ups, quarter, 1, keepdims=False).reshape(width)
    up_bias_own = up_bias_own.astype(jnp.float32)

    row_groups = slab.gather(own_all)
    up_mine = lax.dynamic_index_in_dim(
        up_weight.reshape(shard, 4, 2, 4, -1), quarter, 3, keepdims=False
    )
    up_mine = up_mine.transpose(2, 0, 1, 3).reshape(2, shard, width)
    up_mine = exchange(after(up_mine, own_all), HEAD).reshape(2 * shard, width)
    down_mine = lax.dynamic_slice_in_dim(down_weight, quarter * 2 * shard, 2 * shard, axis=0)

    squares = (output_weight, probe_weight, merged_weight, lookup_weight, content_weight)
    shared = jnp.concatenate(
        [lax.dynamic_slice_in_dim(weight, quarter * piece, piece, axis=0) for weight in squares],
        axis=0,
    )
    shared = after(shared, own_all)
    shared = lax.all_gather(shared, (BLK, HEAD, GRP), axis=0, tiled=False)
    shared = shared.reshape(32, len(squares), piece, width)
    output_full, probe_full, merged_full, lookup_full, content_full = [
        shared[:, at].reshape(width, width) for at in range(len(squares))
    ]

    rows = own_all[:local_rows].astype(jnp.float32)

    def own_columns(vector):
        return lax.dynamic_slice_in_dim(vector, role * shard, shard, axis=0)

    head_bias = jnp.concatenate(
        [
            own_columns(query_bias_full),
            jnp.zeros((shard,), jnp.float32),
            own_columns(value_bias_full),
        ]
    )
    projected = [
        project(group, local_rows, self_gain_full, self_shift_full, head_weights, head_bias)
        for group in row_groups
    ]
    upstream = slab.enter(
        after(jnp.concatenate([cot_prompt, cot_cont], axis=0), own_all)
    )
    feed_weights = jnp.concatenate([up_mine, down_mine], axis=0)
    feed_weights = lax.all_gather(feed_weights, BLK, axis=0, tiled=False)
    head_groups = [pair[1] for pair in projected]
    attended, attended_low, logsum = self_forward(slab.lines, bounds, head_groups, prompt_all)
    upstream_groups = slab.gather(
        after(upstream, row_groups[2]), (head_groups[2], attended_low)
    )
    mixed = exchange(attended_low, ROLE_AXES).transpose(1, 0, 2).reshape(local_rows, width)
    first = rows + matmul(mixed, output_full) + output_bias_full
    first_unit, first_rate = norm_parts(first)
    normed_cross = (first_unit * cross_gain_full + cross_shift_full).astype(low)
    probes = (matmul(normed_cross, probe_full) + probe_bias_full).astype(low)

    memory = jnp.zeros((8 * memory_rows, width), low)
    chunks = [chunk for group in row_groups for chunk in group]
    for at, chunk in enumerate(chunks):
        memory = lax.dynamic_update_slice_in_dim(
            memory, chunk[local_rows:], slab.lines[at] * memory_rows, axis=0
        )
    lookups = matmul(memory, lookup_full).astype(low)
    contents = (matmul(memory, content_full) + content_bias_full).astype(low)
    recalled, cross_logsum = cross_forward(probes, lookups, contents)
    recalled_low = recalled.astype(low)
    second = first + matmul(recalled_low, merged_full) + merged_bias_full
    second_unit, second_rate = norm_parts(second)
    normed_feed = (second_unit * feed_gain_full + feed_shift_full).astype(low)

    fed = [
        feed(group, upstream_group, feed_weights, up_bias_own)
        for group, upstream_group in zip(slab.gather(normed_feed), upstream_groups)
    ]
    dnormed_feed = slab.scatter(*[parts[0] for parts in fed])
    output = second + dnormed_feed[local_rows:] + down_bias_full
    dnormed_feed = dnormed_feed[:local_rows]

    kept = after([parts[1:] for parts in fed], slab.mark)

    def summed(left, right):
        return sum(
            left_product(parts[left].reshape(-1, width), parts[right].reshape(-1, width))
            for parts in kept
        ).astype(low)

    down_gradient = summed(2, 1).reshape(4, 2 * shard, width)
    up_sum = sum(column_sum(parts[3].reshape(-1, width)) for parts in kept).astype(low)
    up_sum = jnp.broadcast_to(
        jnp.pad(up_sum.reshape(4, 1, 2 * shard), ((0, 0), (0, 0), (0, width - 2 * shard))),
        (4, 16, width),
    )
    down_gradient = jnp.concatenate([down_gradient, up_sum], axis=1)
    down_gradient = after(down_gradient, dnormed_feed)
    down_gradient = slab.leave_quarters(
        [
            lax.dynamic_index_in_dim(down_gradient, quarter ^ at, 0, keepdims=False)
            for at in range(4)
        ]
    )
    up_gradient = after(by_role(summed(0, 3), COLUMN_OF), dnormed_feed)
    up_gradient = exchange(up_gradient, ROLE_AXES)

    part, feed_gain_sum, feed_shift_sum = norm_backward(
        dnormed_feed, second_unit, second_rate, feed_gain_full
    )
    dsecond = upstream.astype(jnp.float32) + part
    dsecond_low = dsecond.astype(low)
    drecalled = right_product(dsecond_low, merged_full).astype(low)
    dprobes, dmemory, encoded_gradient = cross_backward(
        probes,
        lookups,
        contents,
        drecalled,
        recalled,
        cross_logsum,
        lookup_full,
        content_full,
    )
    dnormed_cross = right_product(after(dprobes, (up_gradient, down_gradient)), probe_full)
    part, cross_gain_sum, cross_shift_sum = norm_backward(
        dnormed_cross, first_unit, first_rate, cross_gain_full
    )
    dfirst = dsecond + part
    dfirst_low = dfirst.astype(low)
    dmixed = right_product(dfirst_low, output_full).astype(low)
    dmixed = dmixed.reshape(local_rows, 8, shard).transpose(1, 0, 2)
    dmixed = exchange(dmixed, ROLE_AXES)
    up_gradient = slab.leave_columns(after(up_gradient, dmixed))

    sums = jnp.stack(
        (
            column_sum(dfirst_low),
            cross_gain_sum,
            cross_shift_sum,
            column_sum(dprobes),
            column_sum(dsecond_low),
            feed_gain_sum,
            feed_shift_sum,
            column_sum(upstream),
        )
    )
    sums = by_role(sums.T).transpose(0, 2, 1).reshape(8, 1, width)
    sums = jnp.broadcast_to(sums, (8, 16, width))
    scattered = jnp.concatenate(
        [
            by_role(left_product(recalled_low, dsecond_low).astype(low)),
            by_role(left_product(normed_cross, dprobes).astype(low)),
            encoded_gradient.reshape(8, memory_rows, width),
            by_role(left_product(mixed, dfirst_low).astype(low)),
            sums.astype(low),
            dmemory,
        ],
        axis=1,
    )
    scattered = lax.psum_scatter(scattered, ROLE_AXES, scatter_dimension=0, tiled=False)

    dhead_groups = self_backward(
        slab.lines, bounds, head_groups, dmixed, attended, logsum, prompt_all
    )
    done = dhead_groups[0]
    output = slab.leave(after(output.astype(low), done))

    dnormed = slab.scatter(
        *[
            right_product(group.reshape(-1, 3 * shard), head_weights)
            .astype(low)
            .reshape(group.shape[0], local_rows, width)
            for group in dhead_groups
        ]
    )

    up_gradient, down_gradient, scattered = after(
        (up_gradient, down_gradient, scattered), done
    )
    up_weight_gradient = settle_columns(up_gradient)
    down_weight_gradient = slab.settle(
        [part[: 2 * shard] for part in down_gradient], jnp.zeros((4, 2 * shard, width), jnp.float32)
    ).reshape(width, width)
    up_bias_gradient = slab.settle(
        [part[2 * shard, : 2 * shard] for part in down_gradient],
        jnp.zeros((4, 2 * shard), jnp.float32),
    ).reshape(width)

    encoded_end = 2 * shard + memory_rows
    squares_end = encoded_end + shard + 16
    mine_dmemory = scattered[squares_end:].reshape(2, memory_rows, 8, shard)
    mine_dmemory = mine_dmemory.transpose(0, 2, 1, 3)
    mine_dmemory = mine_dmemory.reshape(2, 8 * memory_rows, shard)

    head_gradient = [
        sum(
            left_product(normed.reshape(-1, width), group.reshape(-1, 3 * shard))
            for (normed, unused), group in zip(projected, dhead_groups)
        ),
        left_product(memory, mine_dmemory[0]),
        left_product(memory, mine_dmemory[1]),
    ]
    head_gradient = jnp.concatenate([part.astype(low) for part in head_gradient], axis=1)
    head_gradient = exchange(by_role(head_gradient, COLUMN_OF), ROLE_AXES)
    (
        query_weight_gradient,
        key_weight_gradient,
        value_weight_gradient,
        lookup_weight_gradient,
        content_weight_gradient,
    ) = settle_heads(slab.leave_columns(head_gradient))
    head_sums = sum(column_sum(group.reshape(-1, 3 * shard)) for group in dhead_groups)
    head_sums = slab.leave_own(
        jnp.stack([head_sums[:shard], head_sums[2 * shard :], column_sum(mine_dmemory[1])])
    )
    unit, rate = norm_parts(rows)
    part, self_gain_sum, self_shift_sum = norm_backward(dnormed, unit, rate, self_gain_full)
    row_gradient = jnp.concatenate([(dfirst + part).astype(low), scattered[:squares_end]], axis=0)
    row_gradient = slab.leave(row_gradient).astype(jnp.float32)
    square_gradient = row_gradient[local_rows:]
    merged_weight_gradient = square_gradient[:shard]
    probe_weight_gradient = square_gradient[shard : 2 * shard]
    encoded_gradient = square_gradient[2 * shard : encoded_end]
    output_weight_gradient = square_gradient[encoded_end : encoded_end + shard]
    small_sums = square_gradient[encoded_end + shard].reshape(8, shard)
    (
        output_bias_gradient,
        cross_gain_gradient,
        cross_shift_gradient,
        probe_bias_gradient,
        merged_bias_gradient,
        feed_gain_gradient,
        feed_shift_gradient,
        down_bias_gradient,
    ) = [small_sums[at] for at in range(8)]

    sums = after(jnp.stack((self_gain_sum, self_shift_sum), axis=1), head_gradient)
    sums = by_role(sums)
    sums = jnp.sum(exchange(sums.transpose(0, 2, 1), ROLE_AXES), axis=0)
    sums = slab.leave(sums)
    up_bias_gradient = up_bias_gradient.reshape(-1)
    query_bias_gradient, value_bias_gradient, content_bias_gradient = [
        head_sums[at] for at in range(3)
    ]
    self_gain_gradient, self_shift_gradient = sums[0], sums[1]

    return (
        (
            output[:prompt_rows],
            output[prompt_rows:],
            row_gradient[:prompt_rows],
            row_gradient[prompt_rows:local_rows],
            encoded_gradient,
            self_gain_gradient,
            self_shift_gradient,
            query_weight_gradient,
            query_bias_gradient,
            key_weight_gradient,
            value_weight_gradient,
            value_bias_gradient,
            output_weight_gradient,
            output_bias_gradient,
            cross_gain_gradient,
            cross_shift_gradient,
            probe_weight_gradient,
            probe_bias_gradient,
            lookup_weight_gradient,
            content_weight_gradient,
            content_bias_gradient,
            merged_weight_gradient,
            merged_bias_gradient,
            feed_gain_gradient,
            feed_shift_gradient,
            up_weight_gradient,
            up_bias_gradient,
            down_weight_gradient,
            down_bias_gradient,
        )
    )


def solution(mesh):
    rows, group = P(ALL_AXES, None), P(ALL_AXES)
    weight, vector = P(ROW_AXES, None), P(ROW_AXES)
    ranks = [2 if "weight" in name else 1 for name in PARAM_NAMES]
    sizes = tuple(mesh.shape[axis] for axis in ALL_AXES)
    return jax.shard_map(
        head_body if sizes == (4, 4, 2) and HEADS * HD == 8 * PAIR else token_body,
        mesh=mesh,
        in_specs=(rows, rows, rows, P(GRP))
        + tuple(weight if rank == 2 else vector for rank in ranks)
        + (rows, rows),
        out_specs=(rows,) * 5 + tuple(rows if rank == 2 else group for rank in ranks),
        check_vma=False,
    )
```

```python
import functools
import math
import types

import jax
import jax.numpy as jnp
from jax import lax
from jax.experimental import pallas as pl
from jax.experimental.pallas import tpu as pltpu
from jax.sharding import PartitionSpec as P

HEADS = 16
HD = 64


floor_value = -1e30
BLK = "blk"
HEAD = "head"
GRP = "grp"
ROW_AXES = (BLK, HEAD)
ROLE_AXES = (GRP, HEAD)
ALL_AXES = (GRP, BLK, HEAD)
PARAM_NAMES = (
    "self_gain",
    "self_shift",
    "query_weight",
    "query_bias",
    "key_weight",
    "value_weight",
    "value_bias",
    "output_weight",
    "output_bias",
    "cross_gain",
    "cross_shift",
    "probe_weight",
    "probe_bias",
    "lookup_weight",
    "content_weight",
    "content_bias",
    "merged_weight",
    "merged_bias",
    "feed_gain",
    "feed_shift",
    "up_weight",
    "up_bias",
    "down_weight",
    "down_bias",
)


def layer_norm(rows, gain, shift):
    center = jnp.mean(rows, axis=-1, keepdims=True)
    centred = rows - center
    spread = jnp.mean(centred * centred, axis=-1, keepdims=True)
    return centred * lax.rsqrt(spread + 1e-05) * gain + shift


def matmul(left, right):
    return jnp.dot(left, right, preferred_element_type=jnp.float32)


def left_product(left, right):
    return jnp.einsum("rd,re->de", left, right, preferred_element_type=jnp.float32)


def right_product(left, right):
    return jnp.einsum("re,de->rd", left, right, preferred_element_type=jnp.float32)


def column_sum(values):
    return jnp.sum(values.astype(jnp.float32), axis=0)


def exact_gelu(values):
    return jax.nn.gelu(values, approximate=False)


def row_meta(global_rows, bounds, prompt_rows, cont_rows, heads_here):
    local_rows = prompt_rows + cont_rows
    span = heads_here * local_rows
    owner = global_rows // span
    inner = global_rows % span
    device = owner * heads_here + inner // local_rows
    offset = inner % local_rows
    in_prompt = offset < prompt_rows
    places = jnp.where(
        in_prompt, device * prompt_rows + offset, device * cont_rows + offset - prompt_rows
    )
    later = jnp.sum((places[:, None] >= bounds[None, :]).astype(jnp.int32), axis=1)
    segment = jnp.where(in_prompt, 0, 1 + later)
    return (segment, places)


def allowed_pairs(query_seg, query_place, key_seg, key_place):
    from_prompt = (key_seg[None, :] == 0) & (query_seg[:, None] > 0)
    causal = (key_seg[None, :] == query_seg[:, None]) & (key_place[None, :] <= query_place[:, None])
    return from_prompt | causal


def token_body(
    prompt,
    continued,
    encoded,
    cont_lengths,
    self_gain,
    self_shift,
    query_weight,
    query_bias,
    key_weight,
    value_weight,
    value_bias,
    output_weight,
    output_bias,
    cross_gain,
    cross_shift,
    probe_weight,
    probe_bias,
    lookup_weight,
    content_weight,
    content_bias,
    merged_weight,
    merged_bias,
    feed_gain,
    feed_shift,
    up_weight,
    up_bias,
    down_weight,
    down_bias,
    cot_prompt,
    cot_cont,
):
    gathered = (
        lax.all_gather(self_gain, ROW_AXES, axis=0, tiled=True),
        lax.all_gather(self_shift, ROW_AXES, axis=0, tiled=True),
        lax.all_gather(query_weight, ROW_AXES, axis=0, tiled=True),
        lax.all_gather(query_bias, ROW_AXES, axis=0, tiled=True),
        lax.all_gather(key_weight, ROW_AXES, axis=0, tiled=True),
        lax.all_gather(value_weight, ROW_AXES, axis=0, tiled=True),
        lax.all_gather(value_bias, ROW_AXES, axis=0, tiled=True),
        lax.all_gather(output_weight, ROW_AXES, axis=0, tiled=True),
        lax.all_gather(output_bias, ROW_AXES, axis=0, tiled=True),
        lax.all_gather(cross_gain, ROW_AXES, axis=0, tiled=True),
        lax.all_gather(cross_shift, ROW_AXES, axis=0, tiled=True),
        lax.all_gather(probe_weight, ROW_AXES, axis=0, tiled=True),
        lax.all_gather(probe_bias, ROW_AXES, axis=0, tiled=True),
        lax.all_gather(lookup_weight, ROW_AXES, axis=0, tiled=True),
        lax.all_gather(content_weight, ROW_AXES, axis=0, tiled=True),
        lax.all_gather(content_bias, ROW_AXES, axis=0, tiled=True),
        lax.all_gather(merged_weight, ROW_AXES, axis=0, tiled=True),
        lax.all_gather(merged_bias, ROW_AXES, axis=0, tiled=True),
        lax.all_gather(feed_gain, ROW_AXES, axis=0, tiled=True),
        lax.all_gather(feed_shift, ROW_AXES, axis=0, tiled=True),
        lax.all_gather(up_weight, ROW_AXES, axis=0, tiled=True),
        lax.all_gather(up_bias, ROW_AXES, axis=0, tiled=True),
        lax.all_gather(down_weight, ROW_AXES, axis=0, tiled=True),
        lax.all_gather(down_bias, ROW_AXES, axis=0, tiled=True),
    )
    full = types.SimpleNamespace(**dict(zip(PARAM_NAMES, gathered)))
    heads_here = lax.axis_size(HEAD)
    prompt_rows = prompt.shape[0]
    cont_rows = continued.shape[0]
    local_rows = prompt_rows + cont_rows
    span = heads_here * local_rows
    width = prompt.shape[1]
    local_heads = HEADS // heads_here
    half = local_heads * HD
    scale = HD ** (-0.5)
    bounds = jnp.cumsum(cont_lengths)
    rows = jnp.concatenate([prompt, continued], axis=0).astype(jnp.float32)
    self_gain_full = full.self_gain.astype(jnp.float32)
    self_shift_full = full.self_shift.astype(jnp.float32)
    cross_gain_full = full.cross_gain.astype(jnp.float32)
    cross_shift_full = full.cross_shift.astype(jnp.float32)
    feed_gain_full = full.feed_gain.astype(jnp.float32)
    feed_shift_full = full.feed_shift.astype(jnp.float32)
    normed = layer_norm(rows, self_gain_full, self_shift_full).astype(jnp.bfloat16)
    queries = (matmul(normed, full.query_weight) + full.query_bias).astype(jnp.bfloat16)
    keys_rows = matmul(normed, full.key_weight).astype(jnp.bfloat16)
    values_rows = (matmul(normed, full.value_weight) + full.value_bias).astype(jnp.bfloat16)
    head_queries, head_keys, head_values = (
        lax.all_to_all(queries, HEAD, split_axis=1, concat_axis=0, tiled=True),
        lax.all_to_all(keys_rows, HEAD, split_axis=1, concat_axis=0, tiled=True),
        lax.all_to_all(values_rows, HEAD, split_axis=1, concat_axis=0, tiled=True),
    )
    query_block = math.gcd(span, 512)
    query_count = span // query_block
    own_rows = lax.axis_index(BLK) * span + jnp.arange(span, dtype=jnp.int32)
    own_seg, own_place = row_meta(own_rows, bounds, prompt_rows, cont_rows, heads_here)
    query_tiles = head_queries.reshape(query_count, query_block, local_heads, HD)
    seg_tiles = own_seg.reshape(query_count, query_block)
    place_tiles = own_place.reshape(query_count, query_block)

    def key_tiles(piece_keys, piece_values):
        count = piece_keys.shape[0]
        key_block = math.gcd(count, span)
        key_count = count // key_block
        key_rows = jnp.arange(count, dtype=jnp.int32)
        key_seg, key_place = row_meta(key_rows, bounds, prompt_rows, cont_rows, heads_here)
        return (
            piece_keys.reshape(key_count, key_block, local_heads, HD),
            piece_values.reshape(key_count, key_block, local_heads, HD),
            key_seg.reshape(key_count, key_block),
            key_place.reshape(key_count, key_block),
        )

    def scores_of(query_tile, query_seg, query_place, key_tile, key_seg, key_place):
        raw = (
            jnp.einsum("qhd,khd->qhk", query_tile, key_tile, preferred_element_type=jnp.float32)
            * scale
        )
        allowed = allowed_pairs(query_seg, query_place, key_seg, key_place)[:, None, :]
        return (jnp.where(allowed, raw, floor_value), allowed)

    start_top = jnp.full((query_count, query_block, local_heads), floor_value, jnp.float32)
    start_total = jnp.zeros((query_count, query_block, local_heads), jnp.float32)
    start_sum = jnp.zeros((query_count, query_block, local_heads, HD), jnp.float32)
    piece = (
        lax.all_gather(head_keys, BLK, axis=0, tiled=True),
        lax.all_gather(head_values, BLK, axis=0, tiled=True),
    )
    tiles = key_tiles(piece[0], piece[1])

    def fold_per_query(args):
        query_tile, query_seg, query_place, running_top, running_total, running_sum = args

        def fold_per_key(state, key_args):
            key_tile, value_tile, key_seg, key_place = key_args
            top_old, total_old, sum_old = state
            scores, allowed = scores_of(
                query_tile, query_seg, query_place, key_tile, key_seg, key_place
            )
            top_new = jnp.maximum(top_old, jnp.max(scores, axis=-1))
            weights = jnp.where(allowed, jnp.exp(scores - top_new[..., None]), 0.0)
            fade = jnp.exp(top_old - top_new)
            total_new = total_old * fade + jnp.sum(weights, axis=-1)
            sum_new = sum_old * fade[..., None] + jnp.einsum(
                "qhk,khd->qhd",
                weights.astype(jnp.bfloat16),
                value_tile,
                preferred_element_type=jnp.float32,
            )
            return ((top_new, total_new, sum_new), None)

        state, unused = lax.scan(fold_per_key, (running_top, running_total, running_sum), tiles)
        return state

    top, total, summed = lax.map(
        fold_per_query, (query_tiles, seg_tiles, place_tiles, start_top, start_total, start_sum)
    )
    attended = summed / total[..., None]
    logsum = top + jnp.log(total)
    attended_low = attended.reshape(span, half).astype(jnp.bfloat16)
    mixed = lax.all_to_all(attended_low, HEAD, split_axis=0, concat_axis=1, tiled=True)
    first = rows + matmul(mixed, full.output_weight) + full.output_bias
    normed_cross = layer_norm(first, cross_gain_full, cross_shift_full).astype(jnp.bfloat16)
    probes = (matmul(normed_cross, full.probe_weight) + full.probe_bias).astype(jnp.bfloat16)
    lookups_own = matmul(encoded, full.lookup_weight).astype(jnp.bfloat16)
    contents_own = (matmul(encoded, full.content_weight) + full.content_bias).astype(
        jnp.bfloat16
    )
    lookups, contents = (
        lax.all_gather(lookups_own, ROW_AXES, axis=0, tiled=True),
        lax.all_gather(contents_own, ROW_AXES, axis=0, tiled=True),
    )
    memory_rows = lookups.shape[0]
    memory_keys = lookups.reshape(memory_rows, HEADS, HD)
    memory_values = contents.reshape(memory_rows, HEADS, HD)
    cross_block = math.gcd(local_rows, 256)
    cross_count = local_rows // cross_block
    probe_tiles = probes.reshape(cross_count, cross_block, HEADS, HD)

    def cross_scores(probe_tile):
        return (
            jnp.einsum("qhd,khd->qhk", probe_tile, memory_keys, preferred_element_type=jnp.float32)
            * scale
        )

    def cross_forward(probe_tile):
        scores = cross_scores(probe_tile)
        peak = jnp.max(scores, axis=-1, keepdims=True)
        weights = jnp.exp(scores - peak)
        weight_sum = jnp.sum(weights, axis=-1, keepdims=True)
        probs = (weights / weight_sum).astype(jnp.bfloat16)
        recalled_tile = jnp.einsum(
            "qhk,khd->qhd", probs, memory_values, preferred_element_type=jnp.float32
        )
        return (recalled_tile, (peak + jnp.log(weight_sum))[..., 0])

    recalled, cross_logsum = lax.map(cross_forward, probe_tiles)
    recalled_low = recalled.reshape(local_rows, width).astype(jnp.bfloat16)
    second = first + matmul(recalled_low, full.merged_weight) + full.merged_bias
    normed_feed = layer_norm(second, feed_gain_full, feed_shift_full).astype(jnp.bfloat16)
    hidden = matmul(normed_feed, full.up_weight) + full.up_bias
    active = exact_gelu(hidden).astype(jnp.bfloat16)
    output = second + matmul(active, full.down_weight) + full.down_bias
    output_low = output.astype(jnp.bfloat16)
    grads = types.SimpleNamespace()
    upstream = jnp.concatenate([cot_prompt, cot_cont], axis=0)
    grads.down_weight = left_product(active, upstream)
    grads.down_bias = column_sum(upstream)
    dactive = right_product(upstream, full.down_weight)
    unused, gelu_pull = jax.vjp(exact_gelu, hidden)
    dhidden = gelu_pull(dactive)[0].astype(jnp.bfloat16)
    grads.up_weight = left_product(normed_feed, dhidden)
    grads.up_bias = column_sum(dhidden)
    dnormed_feed = right_product(dhidden, full.up_weight)
    unused, feed_pull = jax.vjp(layer_norm, second, feed_gain_full, feed_shift_full)
    dsecond_part, grads.feed_gain, grads.feed_shift = feed_pull(dnormed_feed)
    dsecond = upstream.astype(jnp.float32) + dsecond_part
    dsecond_low = dsecond.astype(jnp.bfloat16)
    grads.merged_weight = left_product(recalled_low, dsecond_low)
    grads.merged_bias = column_sum(dsecond_low)
    drecalled = right_product(dsecond_low, full.merged_weight).astype(jnp.bfloat16)
    drecalled_tiles = drecalled.reshape(cross_count, cross_block, HEADS, HD)
    cross_delta = jnp.sum(drecalled_tiles.astype(jnp.float32) * recalled, axis=-1)

    def cross_backward(state, args):
        probe_tile, drecalled_tile, logsum_tile, delta_tile = args
        dlookups_acc, dcontents_acc = state
        scores = cross_scores(probe_tile)
        probs = jnp.exp(scores - logsum_tile[..., None])
        dprobs = jnp.einsum(
            "qhd,khd->qhk", drecalled_tile, memory_values, preferred_element_type=jnp.float32
        )
        dscores = (probs * (dprobs - delta_tile[..., None])).astype(jnp.bfloat16)
        dprobe_tile = (
            jnp.einsum("qhk,khd->qhd", dscores, memory_keys, preferred_element_type=jnp.float32)
            * scale
        )
        dlookups_acc = (
            dlookups_acc
            + jnp.einsum("qhk,qhd->khd", dscores, probe_tile, preferred_element_type=jnp.float32)
            * scale
        )
        dcontents_acc = dcontents_acc + jnp.einsum(
            "qhk,qhd->khd",
            probs.astype(jnp.bfloat16),
            drecalled_tile,
            preferred_element_type=jnp.float32,
        )
        return ((dlookups_acc, dcontents_acc), dprobe_tile)

    zero_memory = jnp.zeros((memory_rows, HEADS, HD), jnp.float32)
    (dlookups, dcontents), dprobes = lax.scan(
        cross_backward,
        (zero_memory, zero_memory),
        (probe_tiles, drecalled_tiles, cross_logsum, cross_delta),
    )
    mine_lookups, mine_contents = (
        lax.psum_scatter(
            dlookups.reshape(memory_rows, width).astype(jnp.bfloat16),
            ROW_AXES,
            scatter_dimension=0,
            tiled=True,
        ).astype(jnp.float32),
        lax.psum_scatter(
            dcontents.reshape(memory_rows, width).astype(jnp.bfloat16),
            ROW_AXES,
            scatter_dimension=0,
            tiled=True,
        ).astype(jnp.float32),
    )
    mine_lookups = mine_lookups.astype(jnp.bfloat16)
    mine_contents = mine_contents.astype(jnp.bfloat16)
    grads.lookup_weight = left_product(encoded, mine_lookups)
    grads.content_weight = left_product(encoded, mine_contents)
    grads.content_bias = column_sum(mine_contents)
    encoded_gradient = right_product(mine_lookups, full.lookup_weight) + right_product(
        mine_contents, full.content_weight
    )
    dprobes_low = dprobes.reshape(local_rows, width).astype(jnp.bfloat16)
    grads.probe_weight = left_product(normed_cross, dprobes_low)
    grads.probe_bias = column_sum(dprobes_low)
    dnormed_cross = right_product(dprobes_low, full.probe_weight)
    unused, cross_pull = jax.vjp(layer_norm, first, cross_gain_full, cross_shift_full)
    dfirst_part, grads.cross_gain, grads.cross_shift = cross_pull(dnormed_cross)
    dfirst = dsecond + dfirst_part
    dfirst_low = dfirst.astype(jnp.bfloat16)
    grads.output_weight = left_product(mixed, dfirst_low)
    grads.output_bias = column_sum(dfirst_low)
    dmixed = right_product(dfirst_low, full.output_weight).astype(jnp.bfloat16)
    head_dmixed = lax.all_to_all(dmixed, HEAD, split_axis=1, concat_axis=0, tiled=True)
    dmixed_tiles = head_dmixed.reshape(query_count, query_block, local_heads, HD)
    delta_tiles = jnp.sum(dmixed_tiles.astype(jnp.float32) * attended, axis=-1)
    start_dquery = jnp.zeros((query_count, query_block, local_heads, HD), jnp.float32)
    piece = (
        lax.all_gather(head_keys, BLK, axis=0, tiled=True),
        lax.all_gather(head_values, BLK, axis=0, tiled=True),
    )
    dquery_tiles = start_dquery
    count = piece[0].shape[0]
    block_dquery_tiles = dquery_tiles
    piece_keys = piece[0]
    block_tiles = key_tiles(piece_keys, piece[1])
    count = piece_keys.shape[0]

    def block_per_query(state, args):
        dkey_part, dvalue_part = state
        query_tile, query_seg, query_place, logsum_tile, delta_tile, dmixed_tile, dquery_tile = args

        def block_per_key(dquery_acc, key_args):
            key_tile, value_tile, key_seg, key_place = key_args
            scores, allowed = scores_of(
                query_tile, query_seg, query_place, key_tile, key_seg, key_place
            )
            probs = jnp.where(allowed, jnp.exp(scores - logsum_tile[..., None]), 0.0)
            dprobs = jnp.einsum(
                "qhd,khd->qhk", dmixed_tile, value_tile, preferred_element_type=jnp.float32
            )
            dscores = (probs * (dprobs - delta_tile[..., None])).astype(jnp.bfloat16)
            dquery_acc = (
                dquery_acc
                + jnp.einsum("qhk,khd->qhd", dscores, key_tile, preferred_element_type=jnp.float32)
                * scale
            )
            dkey_tile = (
                jnp.einsum("qhk,qhd->khd", dscores, query_tile, preferred_element_type=jnp.float32)
                * scale
            )
            dvalue_tile = jnp.einsum(
                "qhk,qhd->khd",
                probs.astype(jnp.bfloat16),
                dmixed_tile,
                preferred_element_type=jnp.float32,
            )
            return (dquery_acc, (dkey_tile, dvalue_tile))

        dquery_new, key_terms = lax.scan(block_per_key, dquery_tile, block_tiles)
        return ((dkey_part + key_terms[0], dvalue_part + key_terms[1]), dquery_new)

    zero_part = jnp.zeros(block_tiles[0].shape, jnp.float32)
    parts, block_dquery_tiles = lax.scan(
        block_per_query,
        (zero_part, zero_part),
        (
            query_tiles,
            seg_tiles,
            place_tiles,
            logsum,
            delta_tiles,
            dmixed_tiles,
            block_dquery_tiles,
        ),
    )
    dquery_tiles = block_dquery_tiles
    dkey_part = parts[0].reshape(count, half)
    dvalue_part = parts[1].reshape(count, half)
    dkey_rows = dkey_part
    dvalue_rows = dvalue_part
    dquery_tiles, dkey_rows, dvalue_rows = (dquery_tiles, dkey_rows, dvalue_rows)
    own_dkeys, own_dvalues = (
        lax.psum_scatter(
            dkey_rows.astype(jnp.bfloat16), BLK, scatter_dimension=0, tiled=True
        ).astype(jnp.float32),
        lax.psum_scatter(
            dvalue_rows.astype(jnp.bfloat16), BLK, scatter_dimension=0, tiled=True
        ).astype(jnp.float32),
    )
    row_dqueries, row_dkeys, row_dvalues = (
        lax.all_to_all(
            dquery_tiles.reshape(span, half).astype(jnp.bfloat16),
            HEAD,
            split_axis=0,
            concat_axis=1,
            tiled=True,
        ),
        lax.all_to_all(
            own_dkeys.astype(jnp.bfloat16), HEAD, split_axis=0, concat_axis=1, tiled=True
        ),
        lax.all_to_all(
            own_dvalues.astype(jnp.bfloat16), HEAD, split_axis=0, concat_axis=1, tiled=True
        ),
    )
    grads.query_weight = left_product(normed, row_dqueries)
    grads.query_bias = column_sum(row_dqueries)
    grads.key_weight = left_product(normed, row_dkeys)
    grads.value_weight = left_product(normed, row_dvalues)
    grads.value_bias = column_sum(row_dvalues)
    dnormed = (
        right_product(row_dqueries, full.query_weight)
        + right_product(row_dkeys, full.key_weight)
        + right_product(row_dvalues, full.value_weight)
    )
    unused, self_pull = jax.vjp(layer_norm, rows, self_gain_full, self_shift_full)
    drows_part, grads.self_gain, grads.self_shift = self_pull(dnormed)
    row_gradient = dfirst + drows_part
    shards = tuple(
        (
            lax.psum_scatter(
                grads.self_gain.astype(jnp.bfloat16),
                ROW_AXES,
                scatter_dimension=0,
                tiled=True,
            ).astype(jnp.float32),
            lax.psum_scatter(
                grads.self_shift.astype(jnp.bfloat16),
                ROW_AXES,
                scatter_dimension=0,
                tiled=True,
            ).astype(jnp.float32),
            lax.psum_scatter(
                grads.query_weight.astype(jnp.bfloat16),
                ROW_AXES,
                scatter_dimension=0,
                tiled=True,
            ).astype(jnp.float32),
            lax.psum_scatter(
                grads.query_bias.astype(jnp.bfloat16),
                ROW_AXES,
                scatter_dimension=0,
                tiled=True,
            ).astype(jnp.float32),
            lax.psum_scatter(
                grads.key_weight.astype(jnp.bfloat16),
                ROW_AXES,
                scatter_dimension=0,
                tiled=True,
            ).astype(jnp.float32),
            lax.psum_scatter(
                grads.value_weight.astype(jnp.bfloat16),
                ROW_AXES,
                scatter_dimension=0,
                tiled=True,
            ).astype(jnp.float32),
            lax.psum_scatter(
                grads.value_bias.astype(jnp.bfloat16),
                ROW_AXES,
                scatter_dimension=0,
                tiled=True,
            ).astype(jnp.float32),
            lax.psum_scatter(
                grads.output_weight.astype(jnp.bfloat16),
                ROW_AXES,
                scatter_dimension=0,
                tiled=True,
            ).astype(jnp.float32),
            lax.psum_scatter(
                grads.output_bias.astype(jnp.bfloat16),
                ROW_AXES,
                scatter_dimension=0,
                tiled=True,
            ).astype(jnp.float32),
            lax.psum_scatter(
                grads.cross_gain.astype(jnp.bfloat16),
                ROW_AXES,
                scatter_dimension=0,
                tiled=True,
            ).astype(jnp.float32),
            lax.psum_scatter(
                grads.cross_shift.astype(jnp.bfloat16),
                ROW_AXES,
                scatter_dimension=0,
                tiled=True,
            ).astype(jnp.float32),
            lax.psum_scatter(
                grads.probe_weight.astype(jnp.bfloat16),
                ROW_AXES,
                scatter_dimension=0,
                tiled=True,
            ).astype(jnp.float32),
            lax.psum_scatter(
                grads.probe_bias.astype(jnp.bfloat16),
                ROW_AXES,
                scatter_dimension=0,
                tiled=True,
            ).astype(jnp.float32),
            lax.psum_scatter(
                grads.lookup_weight.astype(jnp.bfloat16),
                ROW_AXES,
                scatter_dimension=0,
                tiled=True,
            ).astype(jnp.float32),
            lax.psum_scatter(
                grads.content_weight.astype(jnp.bfloat16),
                ROW_AXES,
                scatter_dimension=0,
                tiled=True,
            ).astype(jnp.float32),
            lax.psum_scatter(
                grads.content_bias.astype(jnp.bfloat16),
                ROW_AXES,
                scatter_dimension=0,
                tiled=True,
            ).astype(jnp.float32),
            lax.psum_scatter(
                grads.merged_weight.astype(jnp.bfloat16),
                ROW_AXES,
                scatter_dimension=0,
                tiled=True,
            ).astype(jnp.float32),
            lax.psum_scatter(
                grads.merged_bias.astype(jnp.bfloat16),
                ROW_AXES,
                scatter_dimension=0,
                tiled=True,
            ).astype(jnp.float32),
            lax.psum_scatter(
                grads.feed_gain.astype(jnp.bfloat16),
                ROW_AXES,
                scatter_dimension=0,
                tiled=True,
            ).astype(jnp.float32),
            lax.psum_scatter(
                grads.feed_shift.astype(jnp.bfloat16),
                ROW_AXES,
                scatter_dimension=0,
                tiled=True,
            ).astype(jnp.float32),
            lax.psum_scatter(
                grads.up_weight.astype(jnp.bfloat16),
                ROW_AXES,
                scatter_dimension=0,
                tiled=True,
            ).astype(jnp.float32),
            lax.psum_scatter(
                grads.up_bias.astype(jnp.bfloat16),
                ROW_AXES,
                scatter_dimension=0,
                tiled=True,
            ).astype(jnp.float32),
            lax.psum_scatter(
                grads.down_weight.astype(jnp.bfloat16),
                ROW_AXES,
                scatter_dimension=0,
                tiled=True,
            ).astype(jnp.float32),
            lax.psum_scatter(
                grads.down_bias.astype(jnp.bfloat16),
                ROW_AXES,
                scatter_dimension=0,
                tiled=True,
            ).astype(jnp.float32),
        )
    )
    return (
        output_low[:prompt_rows],
        output_low[prompt_rows:],
        row_gradient[:prompt_rows],
        row_gradient[prompt_rows:],
        encoded_gradient,
    ) + shards


NT = (((1,), (1,)), ((), ()))
TN = (((0,), (0,)), ((), ()))
PAIR = 2 * HD
TILE = 512
VMEM_BYTES = 56 * 1024 * 1024


def dot(left, right, dims=(((1,), (0,)), ((), ()))):
    return lax.dot_general(left, right, dims, preferred_element_type=jnp.float32)


def first_lanes(shape):
    return lax.broadcasted_iota(jnp.int32, shape, len(shape) - 1) < HD


def split_heads(values, fill=0.0):
    mine = first_lanes(values.shape)
    other = jnp.full(values.shape, fill, values.dtype)
    return jnp.where(mine, values, other), jnp.where(mine, other, values)


def fold(state, query, key, value, allowed=None):
    top, acc = state
    scores = dot(query, key, NT)
    if allowed is not None:
        scores = jnp.where(allowed, scores, floor_value)
    top_new = jnp.maximum(top, jnp.max(scores, axis=1, keepdims=True))
    weights = jnp.exp(scores - top_new).astype(jnp.bfloat16)
    acc_new = acc * jnp.exp(top - top_new) + dot(weights, value)
    return top_new, acc_new


def close(state0, state1):
    top0, acc0 = state0
    top1, acc1 = state1
    mine = first_lanes(acc0.shape)
    total = jnp.where(mine, pltpu.roll(acc0, HD, 1), pltpu.roll(acc1, HD, 1))
    result = jnp.where(mine, acc0, acc1) / total
    logsum = jnp.where(mine, top0, top1) + jnp.log(total)
    turned = jnp.transpose(logsum)
    return result, turned[0:1], turned[HD : HD + 1]


def segment_start(place, bounds_ref):
    start = jnp.zeros_like(place)
    for at in range(bounds_ref.shape[0] - 1):
        start = jnp.where(place >= bounds_ref[at], bounds_ref[at], start)
    return start


SLAB_OF = (0, 2, 1, 3)
COLUMN_OF = (1, 3, 0, 2)


def shard_of(role):
    quarter, side = role >> 1, role & 1
    return (((quarter & 1) << 1) | (quarter >> 1)) * 2 + side


def natural_rows(role, total, prompt_all):
    local_rows, prompt_rows = total // 8, prompt_all // 8
    order = shard_of(role)
    pieces = []
    for low, high, base in (
        (0, prompt_rows, order * prompt_rows),
        (prompt_rows, local_rows, prompt_all + order * (local_rows - prompt_rows)),
    ):
        if not isinstance(base, int):
            base = pl.multiple_of(base, prompt_rows)
        pieces.append((low, high, pl.ds(base, high - low)))
    return pieces


def group_pieces(groups, lines_ref, total, prompt_all):
    pieces = []
    at = 0
    for group in groups:
        for place in range(group.shape[0]):
            for low, high, where in natural_rows(lines_ref[at], total, prompt_all):
                pieces.append((group, place, low, high, where))
            at += 1
    return pieces


def self_forward_kernel(
    prompt_all,
    lines_ref,
    bounds_ref,
    near_ref,
    next_ref,
    far_ref,
    att_ref,
    low_ref,
    lse_ref,
    qn,
    kn,
    v0n,
    v1n,
):
    groups = (near_ref, next_ref, far_ref)
    total = qn.shape[0]
    for group, place, low, high, where in group_pieces(groups, lines_ref, total, prompt_all):
        qn[where] = group[place, low:high, 0:PAIR] * jnp.bfloat16(HD**-0.5)
        kn[where] = group[place, low:high, PAIR : 2 * PAIR]
        v0n[where], v1n[where] = split_heads(group[place, low:high, 2 * PAIR : 3 * PAIR], 1.0)

    prompt_tiles = prompt_all // TILE
    tiles = qn.shape[0] // TILE
    start = (
        jnp.full((TILE, 1), floor_value, jnp.float32),
        jnp.zeros((TILE, PAIR), jnp.float32),
    )

    def both(state, query, base, size, allowed=None):
        key = kn[pl.ds(base, size)]
        return (
            fold(state[0], query[0], key, v0n[pl.ds(base, size)], allowed),
            fold(state[1], query[1], key, v1n[pl.ds(base, size)], allowed),
        )

    def finish(tile, state):
        result, lse0, lse1 = close(*state)
        att_ref[pl.ds(tile * TILE, TILE)] = result
        lse_ref[tile, 0:1, :] = lse0
        lse_ref[tile, 1:2, :] = lse1

    query_at = lax.broadcasted_iota(jnp.int32, (TILE, TILE), 0)
    key_at = lax.broadcasted_iota(jnp.int32, (TILE, TILE), 1)

    def prompt_tile(tile, carry):
        query = split_heads(qn[pl.ds(tile * TILE, TILE)])
        state = lax.fori_loop(
            0, tile, lambda at, now: both(now, query, at * TILE, TILE), (start, start)
        )
        state = both(state, query, tile * TILE, TILE, key_at <= query_at)
        finish(tile, state)
        return carry

    lax.fori_loop(0, prompt_tiles, prompt_tile, 0)

    def cont_tile(tile, carry):
        query = split_heads(qn[pl.ds(tile * TILE, TILE)])
        state = (start, start)
        for at in range(0, prompt_all, 2 * TILE):
            state = both(state, query, at, 2 * TILE)
        first_place = tile * TILE - prompt_all
        place = first_place + query_at
        begin = segment_start(place, bounds_ref)

        def cont_step(at, now):
            key_place = at * TILE - prompt_all + key_at
            return both(now, query, at * TILE, TILE, (key_place <= place) & (key_place >= begin))

        first_key = prompt_tiles + segment_start(first_place, bounds_ref) // TILE
        state = lax.fori_loop(first_key, tile + 1, cont_step, state)
        finish(tile, state)
        return carry

    lax.fori_loop(prompt_tiles, tiles, cont_tile, 0)
    for role in range(8):
        for low, high, where in natural_rows(role, total, prompt_all):
            low_ref[role, low:high] = att_ref[where].astype(jnp.bfloat16)


def unfold(query, key, value, grad, lse, delta, allowed=None):
    probs = jnp.exp(dot(key, query, NT) - lse)
    if allowed is not None:
        probs = jnp.where(allowed, probs, 0.0)
    dscores = (probs * (dot(value, grad, NT) - delta)).astype(jnp.bfloat16)
    return probs.astype(jnp.bfloat16), dscores


def head_inner(left, right):
    turned = jnp.transpose(left * right)
    return (
        jnp.sum(turned[:HD], axis=0, keepdims=True),
        jnp.sum(turned[HD:], axis=0, keepdims=True),
    )


def self_backward_kernel(
    prompt_all,
    lines_ref,
    bounds_ref,
    near_ref,
    next_ref,
    far_ref,
    grad_ref,
    att_ref,
    lse_ref,
    near_out,
    next_out,
    far_out,
    qn,
    kn,
    vn,
    gn,
    dqn,
    dkn,
    dvn,
):
    total = qn.shape[0]
    groups = (near_ref, next_ref, far_ref)
    for group, place, low, high, where in group_pieces(groups, lines_ref, total, prompt_all):
        qn[where] = group[place, low:high, 0:PAIR] * jnp.bfloat16(HD**-0.5)
        kn[where] = group[place, low:high, PAIR : 2 * PAIR]
        vn[where] = group[place, low:high, 2 * PAIR : 3 * PAIR]
    for role in range(8):
        for low, high, where in natural_rows(role, total, prompt_all):
            gn[where] = grad_ref[role, low:high]
    dkn[...] = jnp.zeros_like(dkn)
    dvn[...] = jnp.zeros_like(dvn)
    prompt_tiles = prompt_all // TILE
    tiles = qn.shape[0] // TILE
    key_at = lax.broadcasted_iota(jnp.int32, (TILE, TILE), 0)
    query_at = lax.broadcasted_iota(jnp.int32, (TILE, TILE), 1)

    def load(tile):
        query = split_heads(qn[pl.ds(tile * TILE, TILE)])
        whole = gn[pl.ds(tile * TILE, TILE)]
        grad = split_heads(whole)
        delta = head_inner(whole.astype(jnp.float32), att_ref[pl.ds(tile * TILE, TILE)])
        lse = (lse_ref[tile, 0:1, :], lse_ref[tile, 1:2, :])
        return query, grad, lse, delta

    def step(acc, query, grad, lse, delta, base, allowed=None):
        where = pl.ds(base, TILE)
        key, value = kn[where], vn[where]
        keys = split_heads(key)
        dkey, dvalue = dkn[where], dvn[where]
        for side in range(2):
            probs, dscores = unfold(
                query[side], key, value, grad[side], lse[side], delta[side], allowed
            )
            dvalue = dvalue + dot(probs, grad[side])
            dkey = dkey + dot(dscores, query[side])
            acc = acc + dot(dscores, keys[side], TN)
        dkn[where] = dkey
        dvn[where] = dvalue
        return acc

    def finish(tile, acc):
        dqn[pl.ds(tile * TILE, TILE)] = (acc * HD**-0.5).astype(jnp.bfloat16)

    start = jnp.zeros((TILE, PAIR), jnp.float32)

    def prompt_tile(tile, carry):
        given = load(tile)
        acc = lax.fori_loop(0, tile, lambda at, now: step(now, *given, at * TILE), start)
        acc = step(acc, *given, tile * TILE, key_at <= query_at)
        finish(tile, acc)
        return carry

    lax.fori_loop(0, prompt_tiles, prompt_tile, 0)

    def cont_tile(tile, carry):
        given = load(tile)
        acc = lax.fori_loop(0, prompt_tiles, lambda at, now: step(now, *given, at * TILE), start)
        first_place = tile * TILE - prompt_all
        place = first_place + query_at
        begin = segment_start(place, bounds_ref)

        def cont_step(at, now):
            key_place = at * TILE - prompt_all + key_at
            return step(now, *given, at * TILE, (key_place <= place) & (key_place >= begin))

        first_key = prompt_tiles + segment_start(first_place, bounds_ref) // TILE
        acc = lax.fori_loop(first_key, tile + 1, cont_step, acc)
        finish(tile, acc)
        return carry

    lax.fori_loop(prompt_tiles, tiles, cont_tile, 0)
    outs = (near_out, next_out, far_out)
    for group, place, low, high, where in group_pieces(outs, lines_ref, total, prompt_all):
        group[place, low:high, 0:PAIR] = dqn[where]
        group[place, low:high, PAIR : 2 * PAIR] = dkn[where].astype(jnp.bfloat16)
        group[place, low:high, 2 * PAIR : 3 * PAIR] = dvn[where].astype(jnp.bfloat16)


def cost(micros):
    return pl.CostEstimate(
        flops=int(micros * 9e8), bytes_accessed=int(micros * 2e6), transcendentals=0
    )


def in_vmem(count):
    return [pl.BlockSpec(memory_space=pltpu.VMEM)] * count


def in_smem(count):
    return [pl.BlockSpec(memory_space=pltpu.SMEM)] * count


def self_forward(lines, bounds, groups, prompt_all):
    local_rows = groups[0].shape[1]
    total = 8 * local_rows
    natural = pltpu.VMEM((total, PAIR), jnp.bfloat16)
    return pl.pallas_call(
        functools.partial(self_forward_kernel, prompt_all),
        out_shape=(
            jax.ShapeDtypeStruct((total, PAIR), jnp.float32),
            jax.ShapeDtypeStruct((8, local_rows, PAIR), jnp.bfloat16),
            jax.ShapeDtypeStruct((total // TILE, 2, TILE), jnp.float32),
        ),
        in_specs=in_smem(2) + in_vmem(3),
        out_specs=tuple(in_vmem(3)),
        scratch_shapes=[natural] * 4,
        compiler_params=pltpu.CompilerParams(vmem_limit_bytes=VMEM_BYTES),
        cost_estimate=cost(25),
        name="self_forward",
    )(lines, bounds, *groups)


def self_backward(lines, bounds, groups, grad, att, lse, prompt_all):
    total = 8 * groups[0].shape[1]
    natural = pltpu.VMEM((total, PAIR), jnp.bfloat16)
    wide = pltpu.VMEM((total, PAIR), jnp.float32)
    return pl.pallas_call(
        functools.partial(self_backward_kernel, prompt_all),
        out_shape=tuple(jax.ShapeDtypeStruct(group.shape, jnp.bfloat16) for group in groups),
        in_specs=in_smem(2) + in_vmem(6),
        out_specs=tuple(in_vmem(3)),
        scratch_shapes=[natural] * 5 + [wide] * 2,
        compiler_params=pltpu.CompilerParams(vmem_limit_bytes=VMEM_BYTES),
        cost_estimate=cost(37),
        name="self_backward",
    )(lines, bounds, *groups, grad, att, lse)


def pick(refs, target):
    at = pl.program_id(0)
    for place, ref in enumerate(refs):

        @pl.when(at == place)
        def unused(ref=ref):
            target[...] = ref[0 : target.shape[0]]


def project_kernel(count, *refs):
    gain_ref, shift_ref, weight_ref, bias_ref = refs[count : count + 4]
    normed_ref, rows_ref, chunk = refs[count + 4 :]
    pick(refs[:count], chunk)
    unit, unused = norm_parts(chunk[...].astype(jnp.float32))
    normed = (unit * gain_ref[...] + shift_ref[...]).astype(jnp.bfloat16)
    normed_ref[0] = normed
    rows_ref[0] = (dot(normed, weight_ref[...]) + bias_ref[...]).astype(jnp.bfloat16)


def fixed(shape):
    return pl.BlockSpec(shape, lambda at, *unused: (0,) * len(shape), pipeline_mode=pl.Buffered(1))


def stepped(shape):
    return pl.BlockSpec((1,) + shape, lambda at, *unused: (at,) + (0,) * len(shape))


def project(chunks, rows, gain, shift, weight, bias):
    count = len(chunks)
    width, columns = weight.shape
    return pl.pallas_call(
        functools.partial(project_kernel, count),
        grid=(count,),
        out_shape=(
            jax.ShapeDtypeStruct((count, rows, width), jnp.bfloat16),
            jax.ShapeDtypeStruct((count, rows, columns), jnp.bfloat16),
        ),
        in_specs=[fixed(chunk.shape) for chunk in chunks]
        + [fixed((1, width)), fixed((1, width)), fixed(weight.shape), fixed((1, columns))],
        out_specs=(stepped((rows, width)), stepped((rows, columns))),
        scratch_shapes=[pltpu.VMEM((rows, width), jnp.bfloat16)],
        compiler_params=pltpu.CompilerParams(vmem_limit_bytes=VMEM_BYTES),
        cost_estimate=cost(2.3 * count),
        name="project",
    )(*chunks, gain[None], shift[None], weight, bias[None])


def feed_kernel(count, *refs):
    chunks, upstreams = refs[:count], refs[count : 2 * count]
    weights_ref, bias_ref = refs[2 * count : 2 * count + 2]
    sums_ref, feed_ref, upstream_ref, active_ref, dhidden_ref = refs[2 * count + 2 :]
    pick(chunks, feed_ref.at[0])
    pick(upstreams, upstream_ref.at[0])
    feed = feed_ref[0]
    upstream = upstream_ref[0]
    blocks, both, width = weights_ref.shape
    step = both // 2
    out = None
    for low in range(0, blocks * step, step):
        where = slice(low, low + step)
        up = weights_ref[:, :step, where].reshape(blocks * step, step)
        down = weights_ref[low // step, step:]
        hidden = dot(feed, up) + bias_ref[:, where]
        tail = 0.5 + 0.5 * lax.erf(hidden * math.sqrt(0.5))
        active = (hidden * tail).astype(jnp.bfloat16)
        slope = tail + hidden * jnp.exp(-0.5 * hidden * hidden) * (1.0 / math.sqrt(2.0 * math.pi))
        dhidden = (dot(upstream, down, NT) * slope).astype(jnp.bfloat16)
        active_ref[0, :, where] = active
        dhidden_ref[0, :, where] = dhidden
        term, dterm = dot(active, down), dot(dhidden, up, NT)
        out, dnormed = (term, dterm) if out is None else (out + term, dnormed + dterm)
    rows = feed.shape[0]
    sums_ref[0, :rows] = dnormed.astype(jnp.bfloat16)
    sums_ref[0, rows:] = out.astype(jnp.bfloat16)


def feed(chunks, upstreams, weights, bias):
    count = len(chunks)
    rows, width = chunks[0].shape
    columns = bias.shape[0]
    return pl.pallas_call(
        functools.partial(feed_kernel, count),
        grid=(count,),
        in_specs=[fixed((rows, width))] * (2 * count)
        + [fixed(weights.shape), fixed((1, columns))],
        out_specs=[stepped((2 * rows, width))]
        + [stepped((rows, width))] * 2
        + [stepped((rows, columns))] * 2,
        out_shape=[jax.ShapeDtypeStruct((count, 2 * rows, width), jnp.bfloat16)]
        + [jax.ShapeDtypeStruct((count, rows, width), jnp.bfloat16)] * 2
        + [jax.ShapeDtypeStruct((count, rows, columns), jnp.bfloat16)] * 2,
        compiler_params=pltpu.CompilerParams(vmem_limit_bytes=VMEM_BYTES),
        cost_estimate=cost(6.5 * count),
        name="feed",
    )(*chunks, *upstreams, weights, bias[None])


def cross_forward_kernel(probe_ref, lookup_ref, content_ref, out_ref, lse_ref):
    query = split_heads(probe_ref[...] * jnp.bfloat16(HD**-0.5))
    key = lookup_ref[...]
    values = split_heads(content_ref[...], 1.0)
    rows = query[0].shape[0]
    start = (jnp.full((rows, 1), floor_value, jnp.float32), jnp.zeros((rows, PAIR), jnp.float32))
    states = [fold(start, query[side], key, values[side]) for side in range(2)]
    result, lse0, lse1 = close(*states)
    out_ref[...] = result
    lse_ref[0, 0:1, :] = lse0
    lse_ref[0, 1:2, :] = lse1


def cross_backward_kernel(
    probe_ref,
    lookup_ref,
    content_ref,
    grad_ref,
    out_ref,
    lse_ref,
    dprobe_ref,
    dmemory_ref,
    dlookup_ref,
    dcontent_ref,
):
    query = split_heads(probe_ref[...] * jnp.bfloat16(HD**-0.5))
    key = lookup_ref[...]
    keys = split_heads(key)
    value = content_ref[...]
    whole = grad_ref[...]
    grad = split_heads(whole)
    delta = head_inner(whole.astype(jnp.float32), out_ref[...])
    terms = []
    for side in range(2):
        probs, dscores = unfold(
            query[side], key, value, grad[side], lse_ref[0, side : side + 1, :], delta[side]
        )
        terms.append(
            (
                dot(dscores, keys[side], TN),
                dot(dscores, query[side]),
                dot(probs, grad[side]),
            )
        )
    dprobe_ref[...] = ((terms[0][0] + terms[1][0]) * HD**-0.5).astype(jnp.bfloat16)
    dlookup = (terms[0][1] + terms[1][1]).astype(jnp.bfloat16)
    dcontent = (terms[0][2] + terms[1][2]).astype(jnp.bfloat16)
    rows = dmemory_ref.shape[1] // 2
    for block in range(8):
        columns = slice(block * PAIR, (block + 1) * PAIR)
        dmemory_ref[0, :rows, columns] = dlookup[block * rows : (block + 1) * rows]
        dmemory_ref[0, rows:, columns] = dcontent[block * rows : (block + 1) * rows]
    dlookup_ref[...] = dlookup
    dcontent_ref[...] = dcontent


def pair_block(rows):
    return pl.BlockSpec((rows, PAIR), lambda at: (0, at))


def cross_forward(probes, lookups, contents):
    rows, width = probes.shape
    memory = lookups.shape[0]
    pairs = width // PAIR
    return pl.pallas_call(
        cross_forward_kernel,
        grid=(pairs,),
        out_shape=(
            jax.ShapeDtypeStruct((rows, width), jnp.float32),
            jax.ShapeDtypeStruct((pairs, 2, rows), jnp.float32),
        ),
        in_specs=[pair_block(rows), pair_block(memory), pair_block(memory)],
        out_specs=(pair_block(rows), pl.BlockSpec((1, 2, rows), lambda at: (at, 0, 0))),
        compiler_params=pltpu.CompilerParams(vmem_limit_bytes=VMEM_BYTES),
        cost_estimate=cost(10),
        name="cross_forward",
    )(probes, lookups, contents)


def cross_backward(probes, lookups, contents, grad, recalled, lse):
    rows, width = probes.shape
    memory = lookups.shape[0]
    pairs = width // PAIR
    return pl.pallas_call(
        cross_backward_kernel,
        grid=(pairs,),
        out_shape=(
            jax.ShapeDtypeStruct((rows, width), jnp.bfloat16),
            jax.ShapeDtypeStruct((pairs, 2 * memory // 8, width), jnp.bfloat16),
            jax.ShapeDtypeStruct((memory, width), jnp.bfloat16),
            jax.ShapeDtypeStruct((memory, width), jnp.bfloat16),
        ),
        in_specs=[
            pair_block(rows),
            pair_block(memory),
            pair_block(memory),
            pair_block(rows),
            pair_block(rows),
            pl.BlockSpec((1, 2, rows), lambda at: (at, 0, 0)),
        ],
        out_specs=(
            pair_block(rows),
            pl.BlockSpec((1, 2 * memory // 8, width), lambda at: (at, 0, 0)),
            pair_block(memory),
            pair_block(memory),
        ),
        compiler_params=pltpu.CompilerParams(vmem_limit_bytes=VMEM_BYTES),
        cost_estimate=cost(13),
        name="cross_backward",
    )(probes, lookups, contents, grad, recalled, lse)


def norm_parts(values):
    center = jnp.mean(values, axis=-1, keepdims=True)
    centred = values - center
    spread = jnp.mean(centred * centred, axis=-1, keepdims=True)
    rate = lax.rsqrt(spread + 1e-05)
    return centred * rate, rate


def norm_backward(grad, unit, rate, gain):
    scaled = grad * gain
    along = jnp.mean(scaled, axis=-1, keepdims=True)
    across = jnp.mean(scaled * unit, axis=-1, keepdims=True)
    return (
        rate * (scaled - along - unit * across),
        jnp.sum(grad * unit, axis=0),
        jnp.sum(grad, axis=0),
    )


def joined(group, block, side=0, sides=1):
    return (group * 4 + block) * sides + side


class Slab:
    def __init__(self):
        group, side = lax.axis_index(GRP), lax.axis_index(HEAD)
        self.group, self.side, self.block = group, side, lax.axis_index(BLK)
        column, core = group // 2, group % 2
        chips = ((0, 0), (1, 0), (1, 1), (0, 1))
        lines = [[4 * left + 2 * own + right for left, right in chips] for own in range(2)]
        self.forward = [(line[at], line[(at + 1) % 4]) for line in lines for at in range(4)]
        self.reverse = [(right, left) for left, right in self.forward]
        self.cores = [(role, role ^ 2) for role in range(8)]
        place = jnp.where(column == 0, 3 * side, 1 + side)
        owners = []
        for step, other in ((0, 0), (0, 1), (-1, 0), (1, 0), (-1, 1), (1, 1), (2, 0), (2, 1)):
            there = (place + step) % 4
            far = ((there == 1) | (there == 2)).astype(jnp.int32)
            owners.append(4 * far + 2 * ((core + other) % 2) + (there >= 2).astype(jnp.int32))
        self.lines = jnp.stack(owners).astype(jnp.int32)

    def up(self, values):
        return lax.ppermute(values, ROLE_AXES, self.forward)

    def down(self, values):
        return lax.ppermute(values, ROLE_AXES, self.reverse)

    def swap(self, values):
        return lax.ppermute(values, ROLE_AXES, self.cores)

    def gather(self, values, gates=(None, None)):
        half = values.shape[0] // 2
        left, right, other = self.up(values), self.down(values), self.swap(values)
        if gates[0] is not None:
            left, right, other = after((left, right, other), gates[0])
        pair = (self.up(left[:half]), self.down(right[half:]))
        near, far = self.swap(left), self.swap(right)
        if gates[1] is not None:
            pair, near, far = after((pair, near, far), gates[1])
        last = jnp.concatenate(pair, axis=0)
        return ((values, other), (left, right, near, far), (last, self.swap(last)))

    def scatter(self, near, after_parts, far, gates=(None, None, None)):
        low, wide = jnp.bfloat16, jnp.float32
        swaps = [self.swap(far[1]), self.swap(after_parts[2:4]), self.swap(near[1])]
        if gates[0] is not None:
            swaps = after(swaps, gates[0])
        last = far[0].astype(wide) + swaps[0]
        half = last.shape[0] // 2
        sent = (self.up(last[:half].astype(low)), self.down(last[half:].astype(low)))
        if gates[1] is not None:
            sent = after(sent, gates[1])
        self.mark = left, right = sent
        pair = after_parts[0:2].astype(wide) + swaps[1]
        behind, ahead = pair[0], pair[1]
        left = jnp.concatenate([left + ahead[:half], ahead[half:]], axis=0).astype(low)
        right = jnp.concatenate([behind[:half], right + behind[half:]], axis=0).astype(low)
        sent = (self.up(left), self.down(right))
        if gates[2] is not None:
            sent = after(sent, gates[2])
        return near[0].astype(wide) + swaps[2] + sent[0] + sent[1]

    def enter(self, values):
        moves = [
            (joined(group, block), joined(SLAB_OF[block], SLAB_OF[group]))
            for group in range(4)
            for block in range(4)
        ]
        return lax.ppermute(values, (GRP, BLK), moves)

    def leave(self, values):
        moves = [
            (joined(group, block), joined(SLAB_OF[block], SLAB_OF[group]))
            for group in range(4)
            for block in range(4)
        ]
        return lax.ppermute(values, (GRP, BLK), moves)

    def leave_columns(self, values):
        moves = [
            (joined(group, block), joined(SLAB_OF[block], COLUMN_OF[group]))
            for group in range(4)
            for block in range(4)
        ]
        return lax.ppermute(values, (GRP, BLK), moves)

    def leave_quarters(self, pieces):
        result = []
        for at, piece in enumerate(pieces):
            moves = [
                (joined(group, block), joined(SLAB_OF[block], group ^ at))
                for group in range(4)
                for block in range(4)
            ]
            result.append(lax.ppermute(piece, (GRP, BLK), moves))
        return result

    def settle(self, parts, blank):
        for at, part in enumerate(parts):
            start = (self.block ^ at,) + (0,) * part.ndim
            blank = lax.dynamic_update_slice(blank, part[None].astype(blank.dtype), start)
        return blank

    def leave_own(self, values):
        moves = [
            (joined(group, block, side, 2), joined(SLAB_OF[block], group, side, 2))
            for group in range(4)
            for block in range(4)
            for side in range(2)
        ]
        return lax.ppermute(values, ALL_AXES, moves)


def by_role(values, order=SLAB_OF):
    values = values.reshape((4, 2, -1) + values.shape[1:])
    values = jnp.stack([values[at] for at in order])
    return values.reshape((8,) + values.shape[2:])


def after(values, *others):
    return lax.optimization_barrier((values,) + others)[0]


def exchange(values, axes):
    return lax.all_to_all(values, axes, split_axis=0, concat_axis=0, tiled=True)


def columns_kernel(pieces_ref, out_ref):
    part = pieces_ref.shape[2] // 4
    for role in range(8):
        for block in range(4):
            order = (block * 2 + role % 2) * 4 + role // 2
            out_ref[:, order * part : (order + 1) * part] = pieces_ref[
                role, :, block * part : (block + 1) * part
            ].astype(jnp.float32)


def settle_columns(pieces):
    roles, rows, columns = pieces.shape
    return pl.pallas_call(
        columns_kernel,
        out_shape=jax.ShapeDtypeStruct((rows, roles * columns), jnp.float32),
        in_specs=in_vmem(1),
        out_specs=pl.BlockSpec(memory_space=pltpu.VMEM),
        compiler_params=pltpu.CompilerParams(vmem_limit_bytes=VMEM_BYTES),
        cost_estimate=cost(4),
        name="settle_columns",
    )(pieces)


def heads_kernel(pieces_ref, *outs):
    for role in range(8):
        for place, out_ref in enumerate(outs):
            out_ref[:, role * PAIR : (role + 1) * PAIR] = pieces_ref[
                role, :, place * PAIR : (place + 1) * PAIR
            ].astype(jnp.float32)


def settle_heads(pieces):
    roles, rows, columns = pieces.shape
    count = columns // PAIR
    return pl.pallas_call(
        heads_kernel,
        out_shape=(jax.ShapeDtypeStruct((rows, roles * PAIR), jnp.float32),) * count,
        in_specs=in_vmem(1),
        out_specs=tuple(in_vmem(count)),
        compiler_params=pltpu.CompilerParams(vmem_limit_bytes=VMEM_BYTES),
        cost_estimate=cost(3),
        name="settle_heads",
    )(pieces)


def head_body(
    prompt,
    continued,
    encoded,
    cont_lengths,
    self_gain,
    self_shift,
    query_weight,
    query_bias,
    key_weight,
    value_weight,
    value_bias,
    output_weight,
    output_bias,
    cross_gain,
    cross_shift,
    probe_weight,
    probe_bias,
    lookup_weight,
    content_weight,
    content_bias,
    merged_weight,
    merged_bias,
    feed_gain,
    feed_shift,
    up_weight,
    up_bias,
    down_weight,
    down_bias,
    cot_prompt,
    cot_cont,
):
    slab = Slab()
    low = jnp.bfloat16
    width = prompt.shape[1]
    shard = width // 8
    piece = shard // 4
    prompt_rows = prompt.shape[0]
    local_rows = prompt_rows + continued.shape[0]
    prompt_all = 8 * prompt_rows
    memory_rows = encoded.shape[0]
    quarter, side = slab.group, slab.side
    role = 2 * quarter + side

    swapped = [
        (joined(group, block), joined(block, SLAB_OF[group]))
        for group in range(4)
        for block in range(4)
    ]
    lengths = lax.ppermute(cont_lengths, (GRP, BLK), swapped)
    bounds = jnp.cumsum(lengths).astype(jnp.int32)

    own_all = slab.enter(jnp.concatenate([prompt, continued, encoded], axis=0))

    def head_columns(weight):
        mine = lax.dynamic_slice_in_dim(weight.reshape(shard, 4, 2 * shard), quarter, 1, axis=1)
        return mine.reshape(shard, 2, shard).transpose(1, 0, 2)

    small = (
        self_gain,
        self_shift,
        output_bias,
        cross_gain,
        cross_shift,
        probe_bias,
        merged_bias,
        feed_gain,
        feed_shift,
        down_bias,
        content_bias,
        query_bias,
        value_bias,
    )
    vectors = jnp.concatenate(small + (up_bias,) + (self_gain,) * 3).reshape(1, 8, 3 * shard)
    mixed_in = jnp.concatenate(
        [
            jnp.concatenate(
                [head_columns(query_weight), head_columns(key_weight), head_columns(value_weight)],
                axis=2,
            ),
            jnp.broadcast_to(vectors, (2, 8, 3 * shard)),
        ],
        axis=1,
    )
    mixed_in = jnp.broadcast_to(mixed_in[None], (4,) + mixed_in.shape)
    mixed_in = exchange(mixed_in.reshape(8, shard + 8, 3 * shard), ROW_AXES)
    own_all, mixed_in = lax.optimization_barrier((own_all, mixed_in))
    head_weights = mixed_in[:, :shard].reshape(width, 3 * shard)
    vectors = mixed_in[:, shard:].reshape(8, 24, shard)
    packed = vectors[:, : len(small)].transpose(1, 0, 2).reshape(len(small), width)
    (
        self_gain_full,
        self_shift_full,
        output_bias_full,
        cross_gain_full,
        cross_shift_full,
        probe_bias_full,
        merged_bias_full,
        feed_gain_full,
        feed_shift_full,
        down_bias_full,
        content_bias_full,
        query_bias_full,
        value_bias_full,
    ) = [packed[at].astype(jnp.float32) for at in range(len(small))]
    ups = vectors[:, len(small) : len(small) + 8].reshape(4, 2, 4, -1)
    ups = lax.dynamic_index_in_dim(ups, side, 1, keepdims=False)
    up_bias_own = lax.dynamic_index_in_dim(ups, quarter, 1, keepdims=False).reshape(width)
    up_bias_own = up_bias_own.astype(jnp.float32)

    row_groups = slab.gather(own_all)
    up_mine = lax.dynamic_index_in_dim(
        up_weight.reshape(shard, 4, 2, 4, -1), quarter, 3, keepdims=False
    )
    up_mine = up_mine.transpose(2, 0, 1, 3).reshape(2, shard, width)
    up_mine = exchange(after(up_mine, own_all), HEAD).reshape(2 * shard, width)
    down_mine = lax.dynamic_slice_in_dim(down_weight, quarter * 2 * shard, 2 * shard, axis=0)

    squares = (output_weight, probe_weight, merged_weight, lookup_weight, content_weight)
    shared = jnp.concatenate(
        [lax.dynamic_slice_in_dim(weight, quarter * piece, piece, axis=0) for weight in squares],
        axis=0,
    )
    shared = after(shared, own_all)
    shared = lax.all_gather(shared, (BLK, HEAD, GRP), axis=0, tiled=False)
    shared = shared.reshape(32, len(squares), piece, width)
    output_full, probe_full, merged_full, lookup_full, content_full = [
        shared[:, at].reshape(width, width) for at in range(len(squares))
    ]

    rows = own_all[:local_rows].astype(jnp.float32)

    def own_columns(vector):
        return lax.dynamic_slice_in_dim(vector, role * shard, shard, axis=0)

    head_bias = jnp.concatenate(
        [
            own_columns(query_bias_full),
            jnp.zeros((shard,), jnp.float32),
            own_columns(value_bias_full),
        ]
    )
    projected = [
        project(group, local_rows, self_gain_full, self_shift_full, head_weights, head_bias)
        for group in row_groups
    ]
    upstream = slab.enter(
        after(jnp.concatenate([cot_prompt, cot_cont], axis=0), own_all)
    )
    feed_weights = jnp.concatenate([up_mine, down_mine], axis=0)
    feed_weights = lax.all_gather(feed_weights, BLK, axis=0, tiled=False)
    head_groups = [pair[1] for pair in projected]
    attended, attended_low, logsum = self_forward(slab.lines, bounds, head_groups, prompt_all)
    upstream_groups = slab.gather(
        after(upstream, row_groups[2]), (head_groups[2], attended_low)
    )
    mixed = exchange(attended_low, ROLE_AXES).transpose(1, 0, 2).reshape(local_rows, width)
    first = rows + matmul(mixed, output_full) + output_bias_full
    first_unit, first_rate = norm_parts(first)
    normed_cross = (first_unit * cross_gain_full + cross_shift_full).astype(low)
    probes = (matmul(normed_cross, probe_full) + probe_bias_full).astype(low)

    memory = jnp.zeros((8 * memory_rows, width), low)
    chunks = [chunk for group in row_groups for chunk in group]
    for at, chunk in enumerate(chunks):
        memory = lax.dynamic_update_slice_in_dim(
            memory, chunk[local_rows:], slab.lines[at] * memory_rows, axis=0
        )
    lookups = matmul(memory, lookup_full).astype(low)
    contents = (matmul(memory, content_full) + content_bias_full).astype(low)
    recalled, cross_logsum = cross_forward(probes, lookups, contents)
    recalled_low = recalled.astype(low)
    second = first + matmul(recalled_low, merged_full) + merged_bias_full
    second_unit, second_rate = norm_parts(second)
    normed_feed = (second_unit * feed_gain_full + feed_shift_full).astype(low)

    fed = [
        feed(group, upstream_group, feed_weights, up_bias_own)
        for group, upstream_group in zip(slab.gather(normed_feed), upstream_groups)
    ]
    dnormed_feed = slab.scatter(*[parts[0] for parts in fed])
    output = second + dnormed_feed[local_rows:] + down_bias_full
    dnormed_feed = dnormed_feed[:local_rows]

    kept = after([parts[1:] for parts in fed], slab.mark)

    def summed(left, right):
        return sum(
            left_product(parts[left].reshape(-1, width), parts[right].reshape(-1, width))
            for parts in kept
        ).astype(low)

    down_gradient = summed(2, 1).reshape(4, 2 * shard, width)
    up_sum = sum(column_sum(parts[3].reshape(-1, width)) for parts in kept).astype(low)
    up_sum = jnp.broadcast_to(
        jnp.pad(up_sum.reshape(4, 1, 2 * shard), ((0, 0), (0, 0), (0, width - 2 * shard))),
        (4, 16, width),
    )
    down_gradient = jnp.concatenate([down_gradient, up_sum], axis=1)
    down_gradient = after(down_gradient, dnormed_feed)
    down_gradient = slab.leave_quarters(
        [
            lax.dynamic_index_in_dim(down_gradient, quarter ^ at, 0, keepdims=False)
            for at in range(4)
        ]
    )
    up_gradient = after(by_role(summed(0, 3), COLUMN_OF), dnormed_feed)
    up_gradient = exchange(up_gradient, ROLE_AXES)

    part, feed_gain_sum, feed_shift_sum = norm_backward(
        dnormed_feed, second_unit, second_rate, feed_gain_full
    )
    dsecond = upstream.astype(jnp.float32) + part
    dsecond_low = dsecond.astype(low)
    drecalled = right_product(dsecond_low, merged_full).astype(low)
    dprobes, dmemory, dlookups, dcontents = cross_backward(
        probes, lookups, contents, drecalled, recalled, cross_logsum
    )
    encoded_gradient = right_product(dlookups, lookup_full) + right_product(
        dcontents, content_full
    )
    encoded_gradient = encoded_gradient.astype(low)
    dnormed_cross = right_product(after(dprobes, (up_gradient, down_gradient)), probe_full)
    part, cross_gain_sum, cross_shift_sum = norm_backward(
        dnormed_cross, first_unit, first_rate, cross_gain_full
    )
    dfirst = dsecond + part
    dfirst_low = dfirst.astype(low)
    dmixed = right_product(dfirst_low, output_full).astype(low)
    dmixed = dmixed.reshape(local_rows, 8, shard).transpose(1, 0, 2)
    dmixed = exchange(dmixed, ROLE_AXES)
    up_gradient = slab.leave_columns(after(up_gradient, dmixed))

    sums = jnp.stack(
        (
            column_sum(dfirst_low),
            cross_gain_sum,
            cross_shift_sum,
            column_sum(dprobes),
            column_sum(dsecond_low),
            feed_gain_sum,
            feed_shift_sum,
            column_sum(upstream),
        )
    )
    sums = by_role(sums.T).transpose(0, 2, 1).reshape(8, 1, width)
    sums = jnp.broadcast_to(sums, (8, 16, width))
    scattered = jnp.concatenate(
        [
            by_role(left_product(recalled_low, dsecond_low).astype(low)),
            by_role(left_product(normed_cross, dprobes).astype(low)),
            encoded_gradient.reshape(8, memory_rows, width),
            by_role(left_product(mixed, dfirst_low).astype(low)),
            sums.astype(low),
            dmemory,
        ],
        axis=1,
    )
    scattered = lax.psum_scatter(scattered, ROLE_AXES, scatter_dimension=0, tiled=False)

    dhead_groups = self_backward(
        slab.lines, bounds, head_groups, dmixed, attended, logsum, prompt_all
    )
    done = dhead_groups[0]
    output = slab.leave(after(output.astype(low), done))

    dnormed = slab.scatter(
        *[
            right_product(group.reshape(-1, 3 * shard), head_weights)
            .astype(low)
            .reshape(group.shape[0], local_rows, width)
            for group in dhead_groups
        ]
    )

    up_gradient, down_gradient, scattered = after(
        (up_gradient, down_gradient, scattered), done
    )
    up_weight_gradient = settle_columns(up_gradient)
    down_weight_gradient = slab.settle(
        [part[: 2 * shard] for part in down_gradient], jnp.zeros((4, 2 * shard, width), jnp.float32)
    ).reshape(width, width)
    up_bias_gradient = slab.settle(
        [part[2 * shard, : 2 * shard] for part in down_gradient],
        jnp.zeros((4, 2 * shard), jnp.float32),
    ).reshape(width)

    encoded_end = 2 * shard + memory_rows
    squares_end = encoded_end + shard + 16
    mine_dmemory = scattered[squares_end:].reshape(2, memory_rows, 8, shard)
    mine_dmemory = mine_dmemory.transpose(0, 2, 1, 3)
    mine_dmemory = mine_dmemory.reshape(2, 8 * memory_rows, shard)

    head_gradient = [
        sum(
            left_product(normed.reshape(-1, width), group.reshape(-1, 3 * shard))
            for (normed, unused), group in zip(projected, dhead_groups)
        ),
        left_product(memory, mine_dmemory[0]),
        left_product(memory, mine_dmemory[1]),
    ]
    head_gradient = jnp.concatenate([part.astype(low) for part in head_gradient], axis=1)
    head_gradient = exchange(by_role(head_gradient, COLUMN_OF), ROLE_AXES)
    (
        query_weight_gradient,
        key_weight_gradient,
        value_weight_gradient,
        lookup_weight_gradient,
        content_weight_gradient,
    ) = settle_heads(slab.leave_columns(head_gradient))
    head_sums = sum(column_sum(group.reshape(-1, 3 * shard)) for group in dhead_groups)
    head_sums = slab.leave_own(
        jnp.stack([head_sums[:shard], head_sums[2 * shard :], column_sum(mine_dmemory[1])])
    )
    unit, rate = norm_parts(rows)
    part, self_gain_sum, self_shift_sum = norm_backward(dnormed, unit, rate, self_gain_full)
    row_gradient = jnp.concatenate([(dfirst + part).astype(low), scattered[:squares_end]], axis=0)
    row_gradient = slab.leave(row_gradient).astype(jnp.float32)
    square_gradient = row_gradient[local_rows:]
    merged_weight_gradient = square_gradient[:shard]
    probe_weight_gradient = square_gradient[shard : 2 * shard]
    encoded_gradient = square_gradient[2 * shard : encoded_end]
    output_weight_gradient = square_gradient[encoded_end : encoded_end + shard]
    small_sums = square_gradient[encoded_end + shard].reshape(8, shard)
    (
        output_bias_gradient,
        cross_gain_gradient,
        cross_shift_gradient,
        probe_bias_gradient,
        merged_bias_gradient,
        feed_gain_gradient,
        feed_shift_gradient,
        down_bias_gradient,
    ) = [small_sums[at] for at in range(8)]

    sums = after(jnp.stack((self_gain_sum, self_shift_sum), axis=1), head_gradient)
    sums = by_role(sums)
    sums = jnp.sum(exchange(sums.transpose(0, 2, 1), ROLE_AXES), axis=0)
    sums = slab.leave(sums)
    up_bias_gradient = up_bias_gradient.reshape(-1)
    query_bias_gradient, value_bias_gradient, content_bias_gradient = [
        head_sums[at] for at in range(3)
    ]
    self_gain_gradient, self_shift_gradient = sums[0], sums[1]

    return (
        (
            output[:prompt_rows],
            output[prompt_rows:],
            row_gradient[:prompt_rows],
            row_gradient[prompt_rows:local_rows],
            encoded_gradient,
            self_gain_gradient,
            self_shift_gradient,
            query_weight_gradient,
            query_bias_gradient,
            key_weight_gradient,
            value_weight_gradient,
            value_bias_gradient,
            output_weight_gradient,
            output_bias_gradient,
            cross_gain_gradient,
            cross_shift_gradient,
            probe_weight_gradient,
            probe_bias_gradient,
            lookup_weight_gradient,
            content_weight_gradient,
            content_bias_gradient,
            merged_weight_gradient,
            merged_bias_gradient,
            feed_gain_gradient,
            feed_shift_gradient,
            up_weight_gradient,
            up_bias_gradient,
            down_weight_gradient,
            down_bias_gradient,
        )
    )


def solution(mesh):
    rows, group = P(ALL_AXES, None), P(ALL_AXES)
    weight, vector = P(ROW_AXES, None), P(ROW_AXES)
    ranks = [2 if "weight" in name else 1 for name in PARAM_NAMES]
    sizes = tuple(mesh.shape[axis] for axis in ALL_AXES)
    return jax.shard_map(
        head_body if sizes == (4, 4, 2) and HEADS * HD == 8 * PAIR else token_body,
        mesh=mesh,
        in_specs=(rows, rows, rows, P(GRP))
        + tuple(weight if rank == 2 else vector for rank in ranks)
        + (rows, rows),
        out_specs=(rows,) * 5 + tuple(rows if rank == 2 else group for rank in ranks),
        check_vma=False,
    )
```

```python
import functools
import math
import types

import jax
import jax.numpy as jnp
from jax import lax
from jax.experimental import pallas as pl
from jax.experimental.pallas import tpu as pltpu
from jax.sharding import PartitionSpec as P

HEADS = 16
HD = 64


floor_value = -1e30
BLK = "blk"
HEAD = "head"
GRP = "grp"
ROW_AXES = (BLK, HEAD)
ROLE_AXES = (GRP, HEAD)
ALL_AXES = (GRP, BLK, HEAD)
PARAM_NAMES = (
    "self_gain",
    "self_shift",
    "query_weight",
    "query_bias",
    "key_weight",
    "value_weight",
    "value_bias",
    "output_weight",
    "output_bias",
    "cross_gain",
    "cross_shift",
    "probe_weight",
    "probe_bias",
    "lookup_weight",
    "content_weight",
    "content_bias",
    "merged_weight",
    "merged_bias",
    "feed_gain",
    "feed_shift",
    "up_weight",
    "up_bias",
    "down_weight",
    "down_bias",
)


def layer_norm(rows, gain, shift):
    center = jnp.mean(rows, axis=-1, keepdims=True)
    centred = rows - center
    spread = jnp.mean(centred * centred, axis=-1, keepdims=True)
    return centred * lax.rsqrt(spread + 1e-05) * gain + shift


def matmul(left, right):
    return jnp.dot(left, right, preferred_element_type=jnp.float32)


def left_product(left, right):
    return jnp.einsum("rd,re->de", left, right, preferred_element_type=jnp.float32)


def right_product(left, right):
    return jnp.einsum("re,de->rd", left, right, preferred_element_type=jnp.float32)


def column_sum(values):
    return jnp.sum(values.astype(jnp.float32), axis=0)


def exact_gelu(values):
    return jax.nn.gelu(values, approximate=False)


def row_meta(global_rows, bounds, prompt_rows, cont_rows, heads_here):
    local_rows = prompt_rows + cont_rows
    span = heads_here * local_rows
    owner = global_rows // span
    inner = global_rows % span
    device = owner * heads_here + inner // local_rows
    offset = inner % local_rows
    in_prompt = offset < prompt_rows
    places = jnp.where(
        in_prompt, device * prompt_rows + offset, device * cont_rows + offset - prompt_rows
    )
    later = jnp.sum((places[:, None] >= bounds[None, :]).astype(jnp.int32), axis=1)
    segment = jnp.where(in_prompt, 0, 1 + later)
    return (segment, places)


def allowed_pairs(query_seg, query_place, key_seg, key_place):
    from_prompt = (key_seg[None, :] == 0) & (query_seg[:, None] > 0)
    causal = (key_seg[None, :] == query_seg[:, None]) & (key_place[None, :] <= query_place[:, None])
    return from_prompt | causal


def token_body(
    prompt,
    continued,
    encoded,
    cont_lengths,
    self_gain,
    self_shift,
    query_weight,
    query_bias,
    key_weight,
    value_weight,
    value_bias,
    output_weight,
    output_bias,
    cross_gain,
    cross_shift,
    probe_weight,
    probe_bias,
    lookup_weight,
    content_weight,
    content_bias,
    merged_weight,
    merged_bias,
    feed_gain,
    feed_shift,
    up_weight,
    up_bias,
    down_weight,
    down_bias,
    cot_prompt,
    cot_cont,
):
    gathered = (
        lax.all_gather(self_gain, ROW_AXES, axis=0, tiled=True),
        lax.all_gather(self_shift, ROW_AXES, axis=0, tiled=True),
        lax.all_gather(query_weight, ROW_AXES, axis=0, tiled=True),
        lax.all_gather(query_bias, ROW_AXES, axis=0, tiled=True),
        lax.all_gather(key_weight, ROW_AXES, axis=0, tiled=True),
        lax.all_gather(value_weight, ROW_AXES, axis=0, tiled=True),
        lax.all_gather(value_bias, ROW_AXES, axis=0, tiled=True),
        lax.all_gather(output_weight, ROW_AXES, axis=0, tiled=True),
        lax.all_gather(output_bias, ROW_AXES, axis=0, tiled=True),
        lax.all_gather(cross_gain, ROW_AXES, axis=0, tiled=True),
        lax.all_gather(cross_shift, ROW_AXES, axis=0, tiled=True),
        lax.all_gather(probe_weight, ROW_AXES, axis=0, tiled=True),
        lax.all_gather(probe_bias, ROW_AXES, axis=0, tiled=True),
        lax.all_gather(lookup_weight, ROW_AXES, axis=0, tiled=True),
        lax.all_gather(content_weight, ROW_AXES, axis=0, tiled=True),
        lax.all_gather(content_bias, ROW_AXES, axis=0, tiled=True),
        lax.all_gather(merged_weight, ROW_AXES, axis=0, tiled=True),
        lax.all_gather(merged_bias, ROW_AXES, axis=0, tiled=True),
        lax.all_gather(feed_gain, ROW_AXES, axis=0, tiled=True),
        lax.all_gather(feed_shift, ROW_AXES, axis=0, tiled=True),
        lax.all_gather(up_weight, ROW_AXES, axis=0, tiled=True),
        lax.all_gather(up_bias, ROW_AXES, axis=0, tiled=True),
        lax.all_gather(down_weight, ROW_AXES, axis=0, tiled=True),
        lax.all_gather(down_bias, ROW_AXES, axis=0, tiled=True),
    )
    full = types.SimpleNamespace(**dict(zip(PARAM_NAMES, gathered)))
    heads_here = lax.axis_size(HEAD)
    prompt_rows = prompt.shape[0]
    cont_rows = continued.shape[0]
    local_rows = prompt_rows + cont_rows
    span = heads_here * local_rows
    width = prompt.shape[1]
    local_heads = HEADS // heads_here
    half = local_heads * HD
    scale = HD ** (-0.5)
    bounds = jnp.cumsum(cont_lengths)
    rows = jnp.concatenate([prompt, continued], axis=0).astype(jnp.float32)
    self_gain_full = full.self_gain.astype(jnp.float32)
    self_shift_full = full.self_shift.astype(jnp.float32)
    cross_gain_full = full.cross_gain.astype(jnp.float32)
    cross_shift_full = full.cross_shift.astype(jnp.float32)
    feed_gain_full = full.feed_gain.astype(jnp.float32)
    feed_shift_full = full.feed_shift.astype(jnp.float32)
    normed = layer_norm(rows, self_gain_full, self_shift_full).astype(jnp.bfloat16)
    queries = (matmul(normed, full.query_weight) + full.query_bias).astype(jnp.bfloat16)
    keys_rows = matmul(normed, full.key_weight).astype(jnp.bfloat16)
    values_rows = (matmul(normed, full.value_weight) + full.value_bias).astype(jnp.bfloat16)
    head_queries, head_keys, head_values = (
        lax.all_to_all(queries, HEAD, split_axis=1, concat_axis=0, tiled=True),
        lax.all_to_all(keys_rows, HEAD, split_axis=1, concat_axis=0, tiled=True),
        lax.all_to_all(values_rows, HEAD, split_axis=1, concat_axis=0, tiled=True),
    )
    query_block = math.gcd(span, 512)
    query_count = span // query_block
    own_rows = lax.axis_index(BLK) * span + jnp.arange(span, dtype=jnp.int32)
    own_seg, own_place = row_meta(own_rows, bounds, prompt_rows, cont_rows, heads_here)
    query_tiles = head_queries.reshape(query_count, query_block, local_heads, HD)
    seg_tiles = own_seg.reshape(query_count, query_block)
    place_tiles = own_place.reshape(query_count, query_block)

    def key_tiles(piece_keys, piece_values):
        count = piece_keys.shape[0]
        key_block = math.gcd(count, span)
        key_count = count // key_block
        key_rows = jnp.arange(count, dtype=jnp.int32)
        key_seg, key_place = row_meta(key_rows, bounds, prompt_rows, cont_rows, heads_here)
        return (
            piece_keys.reshape(key_count, key_block, local_heads, HD),
            piece_values.reshape(key_count, key_block, local_heads, HD),
            key_seg.reshape(key_count, key_block),
            key_place.reshape(key_count, key_block),
        )

    def scores_of(query_tile, query_seg, query_place, key_tile, key_seg, key_place):
        raw = (
            jnp.einsum("qhd,khd->qhk", query_tile, key_tile, preferred_element_type=jnp.float32)
            * scale
        )
        allowed = allowed_pairs(query_seg, query_place, key_seg, key_place)[:, None, :]
        return (jnp.where(allowed, raw, floor_value), allowed)

    start_top = jnp.full((query_count, query_block, local_heads), floor_value, jnp.float32)
    start_total = jnp.zeros((query_count, query_block, local_heads), jnp.float32)
    start_sum = jnp.zeros((query_count, query_block, local_heads, HD), jnp.float32)
    piece = (
        lax.all_gather(head_keys, BLK, axis=0, tiled=True),
        lax.all_gather(head_values, BLK, axis=0, tiled=True),
    )
    tiles = key_tiles(piece[0], piece[1])

    def fold_per_query(args):
        query_tile, query_seg, query_place, running_top, running_total, running_sum = args

        def fold_per_key(state, key_args):
            key_tile, value_tile, key_seg, key_place = key_args
            top_old, total_old, sum_old = state
            scores, allowed = scores_of(
                query_tile, query_seg, query_place, key_tile, key_seg, key_place
            )
            top_new = jnp.maximum(top_old, jnp.max(scores, axis=-1))
            weights = jnp.where(allowed, jnp.exp(scores - top_new[..., None]), 0.0)
            fade = jnp.exp(top_old - top_new)
            total_new = total_old * fade + jnp.sum(weights, axis=-1)
            sum_new = sum_old * fade[..., None] + jnp.einsum(
                "qhk,khd->qhd",
                weights.astype(jnp.bfloat16),
                value_tile,
                preferred_element_type=jnp.float32,
            )
            return ((top_new, total_new, sum_new), None)

        state, unused = lax.scan(fold_per_key, (running_top, running_total, running_sum), tiles)
        return state

    top, total, summed = lax.map(
        fold_per_query, (query_tiles, seg_tiles, place_tiles, start_top, start_total, start_sum)
    )
    attended = summed / total[..., None]
    logsum = top + jnp.log(total)
    attended_low = attended.reshape(span, half).astype(jnp.bfloat16)
    mixed = lax.all_to_all(attended_low, HEAD, split_axis=0, concat_axis=1, tiled=True)
    first = rows + matmul(mixed, full.output_weight) + full.output_bias
    normed_cross = layer_norm(first, cross_gain_full, cross_shift_full).astype(jnp.bfloat16)
    probes = (matmul(normed_cross, full.probe_weight) + full.probe_bias).astype(jnp.bfloat16)
    lookups_own = matmul(encoded, full.lookup_weight).astype(jnp.bfloat16)
    contents_own = (matmul(encoded, full.content_weight) + full.content_bias).astype(
        jnp.bfloat16
    )
    lookups, contents = (
        lax.all_gather(lookups_own, ROW_AXES, axis=0, tiled=True),
        lax.all_gather(contents_own, ROW_AXES, axis=0, tiled=True),
    )
    memory_rows = lookups.shape[0]
    memory_keys = lookups.reshape(memory_rows, HEADS, HD)
    memory_values = contents.reshape(memory_rows, HEADS, HD)
    cross_block = math.gcd(local_rows, 256)
    cross_count = local_rows // cross_block
    probe_tiles = probes.reshape(cross_count, cross_block, HEADS, HD)

    def cross_scores(probe_tile):
        return (
            jnp.einsum("qhd,khd->qhk", probe_tile, memory_keys, preferred_element_type=jnp.float32)
            * scale
        )

    def cross_forward(probe_tile):
        scores = cross_scores(probe_tile)
        peak = jnp.max(scores, axis=-1, keepdims=True)
        weights = jnp.exp(scores - peak)
        weight_sum = jnp.sum(weights, axis=-1, keepdims=True)
        probs = (weights / weight_sum).astype(jnp.bfloat16)
        recalled_tile = jnp.einsum(
            "qhk,khd->qhd", probs, memory_values, preferred_element_type=jnp.float32
        )
        return (recalled_tile, (peak + jnp.log(weight_sum))[..., 0])

    recalled, cross_logsum = lax.map(cross_forward, probe_tiles)
    recalled_low = recalled.reshape(local_rows, width).astype(jnp.bfloat16)
    second = first + matmul(recalled_low, full.merged_weight) + full.merged_bias
    normed_feed = layer_norm(second, feed_gain_full, feed_shift_full).astype(jnp.bfloat16)
    hidden = matmul(normed_feed, full.up_weight) + full.up_bias
    active = exact_gelu(hidden).astype(jnp.bfloat16)
    output = second + matmul(active, full.down_weight) + full.down_bias
    output_low = output.astype(jnp.bfloat16)
    grads = types.SimpleNamespace()
    upstream = jnp.concatenate([cot_prompt, cot_cont], axis=0)
    grads.down_weight = left_product(active, upstream)
    grads.down_bias = column_sum(upstream)
    dactive = right_product(upstream, full.down_weight)
    unused, gelu_pull = jax.vjp(exact_gelu, hidden)
    dhidden = gelu_pull(dactive)[0].astype(jnp.bfloat16)
    grads.up_weight = left_product(normed_feed, dhidden)
    grads.up_bias = column_sum(dhidden)
    dnormed_feed = right_product(dhidden, full.up_weight)
    unused, feed_pull = jax.vjp(layer_norm, second, feed_gain_full, feed_shift_full)
    dsecond_part, grads.feed_gain, grads.feed_shift = feed_pull(dnormed_feed)
    dsecond = upstream.astype(jnp.float32) + dsecond_part
    dsecond_low = dsecond.astype(jnp.bfloat16)
    grads.merged_weight = left_product(recalled_low, dsecond_low)
    grads.merged_bias = column_sum(dsecond_low)
    drecalled = right_product(dsecond_low, full.merged_weight).astype(jnp.bfloat16)
    drecalled_tiles = drecalled.reshape(cross_count, cross_block, HEADS, HD)
    cross_delta = jnp.sum(drecalled_tiles.astype(jnp.float32) * recalled, axis=-1)

    def cross_backward(state, args):
        probe_tile, drecalled_tile, logsum_tile, delta_tile = args
        dlookups_acc, dcontents_acc = state
        scores = cross_scores(probe_tile)
        probs = jnp.exp(scores - logsum_tile[..., None])
        dprobs = jnp.einsum(
            "qhd,khd->qhk", drecalled_tile, memory_values, preferred_element_type=jnp.float32
        )
        dscores = (probs * (dprobs - delta_tile[..., None])).astype(jnp.bfloat16)
        dprobe_tile = (
            jnp.einsum("qhk,khd->qhd", dscores, memory_keys, preferred_element_type=jnp.float32)
            * scale
        )
        dlookups_acc = (
            dlookups_acc
            + jnp.einsum("qhk,qhd->khd", dscores, probe_tile, preferred_element_type=jnp.float32)
            * scale
        )
        dcontents_acc = dcontents_acc + jnp.einsum(
            "qhk,qhd->khd",
            probs.astype(jnp.bfloat16),
            drecalled_tile,
            preferred_element_type=jnp.float32,
        )
        return ((dlookups_acc, dcontents_acc), dprobe_tile)

    zero_memory = jnp.zeros((memory_rows, HEADS, HD), jnp.float32)
    (dlookups, dcontents), dprobes = lax.scan(
        cross_backward,
        (zero_memory, zero_memory),
        (probe_tiles, drecalled_tiles, cross_logsum, cross_delta),
    )
    mine_lookups, mine_contents = (
        lax.psum_scatter(
            dlookups.reshape(memory_rows, width).astype(jnp.bfloat16),
            ROW_AXES,
            scatter_dimension=0,
            tiled=True,
        ).astype(jnp.float32),
        lax.psum_scatter(
            dcontents.reshape(memory_rows, width).astype(jnp.bfloat16),
            ROW_AXES,
            scatter_dimension=0,
            tiled=True,
        ).astype(jnp.float32),
    )
    mine_lookups = mine_lookups.astype(jnp.bfloat16)
    mine_contents = mine_contents.astype(jnp.bfloat16)
    grads.lookup_weight = left_product(encoded, mine_lookups)
    grads.content_weight = left_product(encoded, mine_contents)
    grads.content_bias = column_sum(mine_contents)
    encoded_gradient = right_product(mine_lookups, full.lookup_weight) + right_product(
        mine_contents, full.content_weight
    )
    dprobes_low = dprobes.reshape(local_rows, width).astype(jnp.bfloat16)
    grads.probe_weight = left_product(normed_cross, dprobes_low)
    grads.probe_bias = column_sum(dprobes_low)
    dnormed_cross = right_product(dprobes_low, full.probe_weight)
    unused, cross_pull = jax.vjp(layer_norm, first, cross_gain_full, cross_shift_full)
    dfirst_part, grads.cross_gain, grads.cross_shift = cross_pull(dnormed_cross)
    dfirst = dsecond + dfirst_part
    dfirst_low = dfirst.astype(jnp.bfloat16)
    grads.output_weight = left_product(mixed, dfirst_low)
    grads.output_bias = column_sum(dfirst_low)
    dmixed = right_product(dfirst_low, full.output_weight).astype(jnp.bfloat16)
    head_dmixed = lax.all_to_all(dmixed, HEAD, split_axis=1, concat_axis=0, tiled=True)
    dmixed_tiles = head_dmixed.reshape(query_count, query_block, local_heads, HD)
    delta_tiles = jnp.sum(dmixed_tiles.astype(jnp.float32) * attended, axis=-1)
    start_dquery = jnp.zeros((query_count, query_block, local_heads, HD), jnp.float32)
    piece = (
        lax.all_gather(head_keys, BLK, axis=0, tiled=True),
        lax.all_gather(head_values, BLK, axis=0, tiled=True),
    )
    dquery_tiles = start_dquery
    count = piece[0].shape[0]
    block_dquery_tiles = dquery_tiles
    piece_keys = piece[0]
    block_tiles = key_tiles(piece_keys, piece[1])
    count = piece_keys.shape[0]

    def block_per_query(state, args):
        dkey_part, dvalue_part = state
        query_tile, query_seg, query_place, logsum_tile, delta_tile, dmixed_tile, dquery_tile = args

        def block_per_key(dquery_acc, key_args):
            key_tile, value_tile, key_seg, key_place = key_args
            scores, allowed = scores_of(
                query_tile, query_seg, query_place, key_tile, key_seg, key_place
            )
            probs = jnp.where(allowed, jnp.exp(scores - logsum_tile[..., None]), 0.0)
            dprobs = jnp.einsum(
                "qhd,khd->qhk", dmixed_tile, value_tile, preferred_element_type=jnp.float32
            )
            dscores = (probs * (dprobs - delta_tile[..., None])).astype(jnp.bfloat16)
            dquery_acc = (
                dquery_acc
                + jnp.einsum("qhk,khd->qhd", dscores, key_tile, preferred_element_type=jnp.float32)
                * scale
            )
            dkey_tile = (
                jnp.einsum("qhk,qhd->khd", dscores, query_tile, preferred_element_type=jnp.float32)
                * scale
            )
            dvalue_tile = jnp.einsum(
                "qhk,qhd->khd",
                probs.astype(jnp.bfloat16),
                dmixed_tile,
                preferred_element_type=jnp.float32,
            )
            return (dquery_acc, (dkey_tile, dvalue_tile))

        dquery_new, key_terms = lax.scan(block_per_key, dquery_tile, block_tiles)
        return ((dkey_part + key_terms[0], dvalue_part + key_terms[1]), dquery_new)

    zero_part = jnp.zeros(block_tiles[0].shape, jnp.float32)
    parts, block_dquery_tiles = lax.scan(
        block_per_query,
        (zero_part, zero_part),
        (
            query_tiles,
            seg_tiles,
            place_tiles,
            logsum,
            delta_tiles,
            dmixed_tiles,
            block_dquery_tiles,
        ),
    )
    dquery_tiles = block_dquery_tiles
    dkey_part = parts[0].reshape(count, half)
    dvalue_part = parts[1].reshape(count, half)
    dkey_rows = dkey_part
    dvalue_rows = dvalue_part
    dquery_tiles, dkey_rows, dvalue_rows = (dquery_tiles, dkey_rows, dvalue_rows)
    own_dkeys, own_dvalues = (
        lax.psum_scatter(
            dkey_rows.astype(jnp.bfloat16), BLK, scatter_dimension=0, tiled=True
        ).astype(jnp.float32),
        lax.psum_scatter(
            dvalue_rows.astype(jnp.bfloat16), BLK, scatter_dimension=0, tiled=True
        ).astype(jnp.float32),
    )
    row_dqueries, row_dkeys, row_dvalues = (
        lax.all_to_all(
            dquery_tiles.reshape(span, half).astype(jnp.bfloat16),
            HEAD,
            split_axis=0,
            concat_axis=1,
            tiled=True,
        ),
        lax.all_to_all(
            own_dkeys.astype(jnp.bfloat16), HEAD, split_axis=0, concat_axis=1, tiled=True
        ),
        lax.all_to_all(
            own_dvalues.astype(jnp.bfloat16), HEAD, split_axis=0, concat_axis=1, tiled=True
        ),
    )
    grads.query_weight = left_product(normed, row_dqueries)
    grads.query_bias = column_sum(row_dqueries)
    grads.key_weight = left_product(normed, row_dkeys)
    grads.value_weight = left_product(normed, row_dvalues)
    grads.value_bias = column_sum(row_dvalues)
    dnormed = (
        right_product(row_dqueries, full.query_weight)
        + right_product(row_dkeys, full.key_weight)
        + right_product(row_dvalues, full.value_weight)
    )
    unused, self_pull = jax.vjp(layer_norm, rows, self_gain_full, self_shift_full)
    drows_part, grads.self_gain, grads.self_shift = self_pull(dnormed)
    row_gradient = dfirst + drows_part
    shards = tuple(
        (
            lax.psum_scatter(
                grads.self_gain.astype(jnp.bfloat16),
                ROW_AXES,
                scatter_dimension=0,
                tiled=True,
            ).astype(jnp.float32),
            lax.psum_scatter(
                grads.self_shift.astype(jnp.bfloat16),
                ROW_AXES,
                scatter_dimension=0,
                tiled=True,
            ).astype(jnp.float32),
            lax.psum_scatter(
                grads.query_weight.astype(jnp.bfloat16),
                ROW_AXES,
                scatter_dimension=0,
                tiled=True,
            ).astype(jnp.float32),
            lax.psum_scatter(
                grads.query_bias.astype(jnp.bfloat16),
                ROW_AXES,
                scatter_dimension=0,
                tiled=True,
            ).astype(jnp.float32),
            lax.psum_scatter(
                grads.key_weight.astype(jnp.bfloat16),
                ROW_AXES,
                scatter_dimension=0,
                tiled=True,
            ).astype(jnp.float32),
            lax.psum_scatter(
                grads.value_weight.astype(jnp.bfloat16),
                ROW_AXES,
                scatter_dimension=0,
                tiled=True,
            ).astype(jnp.float32),
            lax.psum_scatter(
                grads.value_bias.astype(jnp.bfloat16),
                ROW_AXES,
                scatter_dimension=0,
                tiled=True,
            ).astype(jnp.float32),
            lax.psum_scatter(
                grads.output_weight.astype(jnp.bfloat16),
                ROW_AXES,
                scatter_dimension=0,
                tiled=True,
            ).astype(jnp.float32),
            lax.psum_scatter(
                grads.output_bias.astype(jnp.bfloat16),
                ROW_AXES,
                scatter_dimension=0,
                tiled=True,
            ).astype(jnp.float32),
            lax.psum_scatter(
                grads.cross_gain.astype(jnp.bfloat16),
                ROW_AXES,
                scatter_dimension=0,
                tiled=True,
            ).astype(jnp.float32),
            lax.psum_scatter(
                grads.cross_shift.astype(jnp.bfloat16),
                ROW_AXES,
                scatter_dimension=0,
                tiled=True,
            ).astype(jnp.float32),
            lax.psum_scatter(
                grads.probe_weight.astype(jnp.bfloat16),
                ROW_AXES,
                scatter_dimension=0,
                tiled=True,
            ).astype(jnp.float32),
            lax.psum_scatter(
                grads.probe_bias.astype(jnp.bfloat16),
                ROW_AXES,
                scatter_dimension=0,
                tiled=True,
            ).astype(jnp.float32),
            lax.psum_scatter(
                grads.lookup_weight.astype(jnp.bfloat16),
                ROW_AXES,
                scatter_dimension=0,
                tiled=True,
            ).astype(jnp.float32),
            lax.psum_scatter(
                grads.content_weight.astype(jnp.bfloat16),
                ROW_AXES,
                scatter_dimension=0,
                tiled=True,
            ).astype(jnp.float32),
            lax.psum_scatter(
                grads.content_bias.astype(jnp.bfloat16),
                ROW_AXES,
                scatter_dimension=0,
                tiled=True,
            ).astype(jnp.float32),
            lax.psum_scatter(
                grads.merged_weight.astype(jnp.bfloat16),
                ROW_AXES,
                scatter_dimension=0,
                tiled=True,
            ).astype(jnp.float32),
            lax.psum_scatter(
                grads.merged_bias.astype(jnp.bfloat16),
                ROW_AXES,
                scatter_dimension=0,
                tiled=True,
            ).astype(jnp.float32),
            lax.psum_scatter(
                grads.feed_gain.astype(jnp.bfloat16),
                ROW_AXES,
                scatter_dimension=0,
                tiled=True,
            ).astype(jnp.float32),
            lax.psum_scatter(
                grads.feed_shift.astype(jnp.bfloat16),
                ROW_AXES,
                scatter_dimension=0,
                tiled=True,
            ).astype(jnp.float32),
            lax.psum_scatter(
                grads.up_weight.astype(jnp.bfloat16),
                ROW_AXES,
                scatter_dimension=0,
                tiled=True,
            ).astype(jnp.float32),
            lax.psum_scatter(
                grads.up_bias.astype(jnp.bfloat16),
                ROW_AXES,
                scatter_dimension=0,
                tiled=True,
            ).astype(jnp.float32),
            lax.psum_scatter(
                grads.down_weight.astype(jnp.bfloat16),
                ROW_AXES,
                scatter_dimension=0,
                tiled=True,
            ).astype(jnp.float32),
            lax.psum_scatter(
                grads.down_bias.astype(jnp.bfloat16),
                ROW_AXES,
                scatter_dimension=0,
                tiled=True,
            ).astype(jnp.float32),
        )
    )
    return (
        output_low[:prompt_rows],
        output_low[prompt_rows:],
        row_gradient[:prompt_rows],
        row_gradient[prompt_rows:],
        encoded_gradient,
    ) + shards


NT = (((1,), (1,)), ((), ()))
TN = (((0,), (0,)), ((), ()))
PAIR = 2 * HD
TILE = 512
VMEM_BYTES = 56 * 1024 * 1024


def dot(left, right, dims=(((1,), (0,)), ((), ()))):
    return lax.dot_general(left, right, dims, preferred_element_type=jnp.float32)


def first_lanes(shape):
    return lax.broadcasted_iota(jnp.int32, shape, len(shape) - 1) < HD


def split_heads(values, fill=0.0):
    mine = first_lanes(values.shape)
    other = jnp.full(values.shape, fill, values.dtype)
    return jnp.where(mine, values, other), jnp.where(mine, other, values)


def fold(state, query, key, value, allowed=None):
    top, acc = state
    scores = dot(query, key, NT)
    if allowed is not None:
        scores = jnp.where(allowed, scores, floor_value)
    top_new = jnp.maximum(top, jnp.max(scores, axis=1, keepdims=True))
    weights = jnp.exp(scores - top_new).astype(jnp.bfloat16)
    acc_new = acc * jnp.exp(top - top_new) + dot(weights, value)
    return top_new, acc_new


def close(state0, state1):
    top0, acc0 = state0
    top1, acc1 = state1
    mine = first_lanes(acc0.shape)
    total = jnp.where(mine, pltpu.roll(acc0, HD, 1), pltpu.roll(acc1, HD, 1))
    result = jnp.where(mine, acc0, acc1) / total
    logsum = jnp.where(mine, top0, top1) + jnp.log(total)
    turned = jnp.transpose(logsum)
    return result, turned[0:1], turned[HD : HD + 1]


def segment_start(place, bounds_ref):
    start = jnp.zeros_like(place)
    for at in range(bounds_ref.shape[0] - 1):
        start = jnp.where(place >= bounds_ref[at], bounds_ref[at], start)
    return start


SLAB_OF = (0, 2, 1, 3)
COLUMN_OF = (1, 3, 0, 2)


def shard_of(role):
    quarter, side = role >> 1, role & 1
    return (((quarter & 1) << 1) | (quarter >> 1)) * 2 + side


def natural_rows(role, total, prompt_all):
    local_rows, prompt_rows = total // 8, prompt_all // 8
    order = shard_of(role)
    pieces = []
    for low, high, base in (
        (0, prompt_rows, order * prompt_rows),
        (prompt_rows, local_rows, prompt_all + order * (local_rows - prompt_rows)),
    ):
        if not isinstance(base, int):
            base = pl.multiple_of(base, prompt_rows)
        pieces.append((low, high, pl.ds(base, high - low)))
    return pieces


def group_pieces(groups, lines_ref, total, prompt_all):
    pieces = []
    at = 0
    for group in groups:
        for place in range(group.shape[0]):
            for low, high, where in natural_rows(lines_ref[at], total, prompt_all):
                pieces.append((group, place, low, high, where))
            at += 1
    return pieces


def self_forward_kernel(
    prompt_all,
    lines_ref,
    bounds_ref,
    near_ref,
    next_ref,
    far_ref,
    att_ref,
    low_ref,
    lse_ref,
    qn,
    kn,
    v0n,
    v1n,
):
    groups = (near_ref, next_ref, far_ref)
    total = qn.shape[0]
    for group, place, low, high, where in group_pieces(groups, lines_ref, total, prompt_all):
        qn[where] = group[place, low:high, 0:PAIR] * jnp.bfloat16(HD**-0.5)
        kn[where] = group[place, low:high, PAIR : 2 * PAIR]
        v0n[where], v1n[where] = split_heads(group[place, low:high, 2 * PAIR : 3 * PAIR], 1.0)

    prompt_tiles = prompt_all // TILE
    tiles = qn.shape[0] // TILE
    start = (
        jnp.full((TILE, 1), floor_value, jnp.float32),
        jnp.zeros((TILE, PAIR), jnp.float32),
    )

    def both(state, query, base, size, allowed=None):
        key = kn[pl.ds(base, size)]
        return (
            fold(state[0], query[0], key, v0n[pl.ds(base, size)], allowed),
            fold(state[1], query[1], key, v1n[pl.ds(base, size)], allowed),
        )

    def finish(tile, state):
        result, lse0, lse1 = close(*state)
        att_ref[pl.ds(tile * TILE, TILE)] = result
        lse_ref[tile, 0:1, :] = lse0
        lse_ref[tile, 1:2, :] = lse1

    query_at = lax.broadcasted_iota(jnp.int32, (TILE, TILE), 0)
    key_at = lax.broadcasted_iota(jnp.int32, (TILE, TILE), 1)

    def prompt_tile(tile, carry):
        query = split_heads(qn[pl.ds(tile * TILE, TILE)])
        state = lax.fori_loop(
            0, tile, lambda at, now: both(now, query, at * TILE, TILE), (start, start)
        )
        state = both(state, query, tile * TILE, TILE, key_at <= query_at)
        finish(tile, state)
        return carry

    lax.fori_loop(0, prompt_tiles, prompt_tile, 0)

    def cont_tile(tile, carry):
        query = split_heads(qn[pl.ds(tile * TILE, TILE)])
        state = (start, start)
        for at in range(0, prompt_all, 2 * TILE):
            state = both(state, query, at, 2 * TILE)
        first_place = tile * TILE - prompt_all
        place = first_place + query_at
        begin = segment_start(place, bounds_ref)

        def cont_step(at, now):
            key_place = at * TILE - prompt_all + key_at
            return both(now, query, at * TILE, TILE, (key_place <= place) & (key_place >= begin))

        first_key = prompt_tiles + segment_start(first_place, bounds_ref) // TILE
        state = lax.fori_loop(first_key, tile + 1, cont_step, state)
        finish(tile, state)
        return carry

    lax.fori_loop(prompt_tiles, tiles, cont_tile, 0)
    for role in range(8):
        for low, high, where in natural_rows(role, total, prompt_all):
            low_ref[role, low:high] = att_ref[where].astype(jnp.bfloat16)


def unfold(query, key, value, grad, lse, delta, allowed=None):
    probs = jnp.exp(dot(key, query, NT) - lse)
    if allowed is not None:
        probs = jnp.where(allowed, probs, 0.0)
    dscores = (probs * (dot(value, grad, NT) - delta)).astype(jnp.bfloat16)
    return probs.astype(jnp.bfloat16), dscores


def head_inner(left, right):
    turned = jnp.transpose(left * right)
    return (
        jnp.sum(turned[:HD], axis=0, keepdims=True),
        jnp.sum(turned[HD:], axis=0, keepdims=True),
    )


def self_backward_kernel(
    prompt_all,
    lines_ref,
    bounds_ref,
    near_ref,
    next_ref,
    far_ref,
    grad_ref,
    att_ref,
    lse_ref,
    near_out,
    next_out,
    far_out,
    qn,
    kn,
    vn,
    gn,
    dqn,
    dkn,
    dvn,
):
    total = qn.shape[0]
    groups = (near_ref, next_ref, far_ref)
    for group, place, low, high, where in group_pieces(groups, lines_ref, total, prompt_all):
        qn[where] = group[place, low:high, 0:PAIR] * jnp.bfloat16(HD**-0.5)
        kn[where] = group[place, low:high, PAIR : 2 * PAIR]
        vn[where] = group[place, low:high, 2 * PAIR : 3 * PAIR]
    for role in range(8):
        for low, high, where in natural_rows(role, total, prompt_all):
            gn[where] = grad_ref[role, low:high]
    dkn[...] = jnp.zeros_like(dkn)
    dvn[...] = jnp.zeros_like(dvn)
    prompt_tiles = prompt_all // TILE
    tiles = qn.shape[0] // TILE
    key_at = lax.broadcasted_iota(jnp.int32, (TILE, TILE), 0)
    query_at = lax.broadcasted_iota(jnp.int32, (TILE, TILE), 1)

    def load(tile):
        query = split_heads(qn[pl.ds(tile * TILE, TILE)])
        whole = gn[pl.ds(tile * TILE, TILE)]
        grad = split_heads(whole)
        delta = head_inner(whole.astype(jnp.float32), att_ref[pl.ds(tile * TILE, TILE)])
        lse = (lse_ref[tile, 0:1, :], lse_ref[tile, 1:2, :])
        return query, grad, lse, delta

    def step(acc, query, grad, lse, delta, base, allowed=None):
        where = pl.ds(base, TILE)
        key, value = kn[where], vn[where]
        keys = split_heads(key)
        dkey, dvalue = dkn[where], dvn[where]
        for side in range(2):
            probs, dscores = unfold(
                query[side], key, value, grad[side], lse[side], delta[side], allowed
            )
            dvalue = dvalue + dot(probs, grad[side])
            dkey = dkey + dot(dscores, query[side])
            acc = acc + dot(dscores, keys[side], TN)
        dkn[where] = dkey
        dvn[where] = dvalue
        return acc

    def finish(tile, acc):
        dqn[pl.ds(tile * TILE, TILE)] = (acc * HD**-0.5).astype(jnp.bfloat16)

    start = jnp.zeros((TILE, PAIR), jnp.float32)

    def prompt_tile(tile, carry):
        given = load(tile)
        acc = lax.fori_loop(0, tile, lambda at, now: step(now, *given, at * TILE), start)
        acc = step(acc, *given, tile * TILE, key_at <= query_at)
        finish(tile, acc)
        return carry

    lax.fori_loop(0, prompt_tiles, prompt_tile, 0)

    def cont_tile(tile, carry):
        given = load(tile)
        acc = lax.fori_loop(0, prompt_tiles, lambda at, now: step(now, *given, at * TILE), start)
        first_place = tile * TILE - prompt_all
        place = first_place + query_at
        begin = segment_start(place, bounds_ref)

        def cont_step(at, now):
            key_place = at * TILE - prompt_all + key_at
            return step(now, *given, at * TILE, (key_place <= place) & (key_place >= begin))

        first_key = prompt_tiles + segment_start(first_place, bounds_ref) // TILE
        acc = lax.fori_loop(first_key, tile + 1, cont_step, acc)
        finish(tile, acc)
        return carry

    lax.fori_loop(prompt_tiles, tiles, cont_tile, 0)
    outs = (near_out, next_out, far_out)
    for group, place, low, high, where in group_pieces(outs, lines_ref, total, prompt_all):
        group[place, low:high, 0:PAIR] = dqn[where]
        group[place, low:high, PAIR : 2 * PAIR] = dkn[where].astype(jnp.bfloat16)
        group[place, low:high, 2 * PAIR : 3 * PAIR] = dvn[where].astype(jnp.bfloat16)


def cost(micros):
    return pl.CostEstimate(
        flops=int(micros * 9e8), bytes_accessed=int(micros * 2e6), transcendentals=0
    )


def in_vmem(count):
    return [pl.BlockSpec(memory_space=pltpu.VMEM)] * count


def in_smem(count):
    return [pl.BlockSpec(memory_space=pltpu.SMEM)] * count


def self_forward(lines, bounds, groups, prompt_all):
    local_rows = groups[0].shape[1]
    total = 8 * local_rows
    natural = pltpu.VMEM((total, PAIR), jnp.bfloat16)
    return pl.pallas_call(
        functools.partial(self_forward_kernel, prompt_all),
        out_shape=(
            jax.ShapeDtypeStruct((total, PAIR), jnp.float32),
            jax.ShapeDtypeStruct((8, local_rows, PAIR), jnp.bfloat16),
            jax.ShapeDtypeStruct((total // TILE, 2, TILE), jnp.float32),
        ),
        in_specs=in_smem(2) + in_vmem(3),
        out_specs=tuple(in_vmem(3)),
        scratch_shapes=[natural] * 4,
        compiler_params=pltpu.CompilerParams(vmem_limit_bytes=VMEM_BYTES),
        cost_estimate=cost(25),
        name="self_forward",
    )(lines, bounds, *groups)


def self_backward(lines, bounds, groups, grad, att, lse, prompt_all):
    total = 8 * groups[0].shape[1]
    natural = pltpu.VMEM((total, PAIR), jnp.bfloat16)
    wide = pltpu.VMEM((total, PAIR), jnp.float32)
    return pl.pallas_call(
        functools.partial(self_backward_kernel, prompt_all),
        out_shape=tuple(jax.ShapeDtypeStruct(group.shape, jnp.bfloat16) for group in groups),
        in_specs=in_smem(2) + in_vmem(6),
        out_specs=tuple(in_vmem(3)),
        scratch_shapes=[natural] * 5 + [wide] * 2,
        compiler_params=pltpu.CompilerParams(vmem_limit_bytes=VMEM_BYTES),
        cost_estimate=cost(37),
        name="self_backward",
    )(lines, bounds, *groups, grad, att, lse)


def pick(refs, target):
    at = pl.program_id(0)
    for place, ref in enumerate(refs):

        @pl.when(at == place)
        def unused(ref=ref):
            target[...] = ref[0 : target.shape[0]]


def project_kernel(count, *refs):
    gain_ref, shift_ref, weight_ref, bias_ref = refs[count : count + 4]
    normed_ref, rows_ref, chunk = refs[count + 4 :]
    pick(refs[:count], chunk)
    unit, unused = norm_parts(chunk[...].astype(jnp.float32))
    normed = (unit * gain_ref[...] + shift_ref[...]).astype(jnp.bfloat16)
    normed_ref[0] = normed
    rows_ref[0] = (dot(normed, weight_ref[...]) + bias_ref[...]).astype(jnp.bfloat16)


def fixed(shape):
    return pl.BlockSpec(shape, lambda at, *unused: (0,) * len(shape), pipeline_mode=pl.Buffered(1))


def stepped(shape):
    return pl.BlockSpec((1,) + shape, lambda at, *unused: (at,) + (0,) * len(shape))


def project(chunks, rows, gain, shift, weight, bias):
    count = len(chunks)
    width, columns = weight.shape
    return pl.pallas_call(
        functools.partial(project_kernel, count),
        grid=(count,),
        out_shape=(
            jax.ShapeDtypeStruct((count, rows, width), jnp.bfloat16),
            jax.ShapeDtypeStruct((count, rows, columns), jnp.bfloat16),
        ),
        in_specs=[fixed(chunk.shape) for chunk in chunks]
        + [fixed((1, width)), fixed((1, width)), fixed(weight.shape), fixed((1, columns))],
        out_specs=(stepped((rows, width)), stepped((rows, columns))),
        scratch_shapes=[pltpu.VMEM((rows, width), jnp.bfloat16)],
        compiler_params=pltpu.CompilerParams(vmem_limit_bytes=VMEM_BYTES),
        cost_estimate=cost(2.3 * count),
        name="project",
    )(*chunks, gain[None], shift[None], weight, bias[None])


def feed_kernel(count, *refs):
    chunks, upstreams = refs[:count], refs[count : 2 * count]
    weights_ref, bias_ref = refs[2 * count : 2 * count + 2]
    sums_ref, feed_ref, upstream_ref, active_ref, dhidden_ref = refs[2 * count + 2 :]
    pick(chunks, feed_ref.at[0])
    pick(upstreams, upstream_ref.at[0])
    feed = feed_ref[0]
    upstream = upstream_ref[0]
    blocks, both, width = weights_ref.shape
    step = both // 2
    out = None
    for low in range(0, blocks * step, step):
        where = slice(low, low + step)
        up = weights_ref[:, :step, where].reshape(blocks * step, step)
        down = weights_ref[low // step, step:]
        hidden = dot(feed, up) + bias_ref[:, where]
        tail = 0.5 + 0.5 * lax.erf(hidden * math.sqrt(0.5))
        active = (hidden * tail).astype(jnp.bfloat16)
        slope = tail + hidden * jnp.exp(-0.5 * hidden * hidden) * (1.0 / math.sqrt(2.0 * math.pi))
        dhidden = (dot(upstream, down, NT) * slope).astype(jnp.bfloat16)
        active_ref[0, :, where] = active
        dhidden_ref[0, :, where] = dhidden
        term, dterm = dot(active, down), dot(dhidden, up, NT)
        out, dnormed = (term, dterm) if out is None else (out + term, dnormed + dterm)
    rows = feed.shape[0]
    sums_ref[0, :rows] = dnormed.astype(jnp.bfloat16)
    sums_ref[0, rows:] = out.astype(jnp.bfloat16)


def feed(chunks, upstreams, weights, bias):
    count = len(chunks)
    rows, width = chunks[0].shape
    columns = bias.shape[0]
    return pl.pallas_call(
        functools.partial(feed_kernel, count),
        grid=(count,),
        in_specs=[fixed((rows, width))] * (2 * count)
        + [fixed(weights.shape), fixed((1, columns))],
        out_specs=[stepped((2 * rows, width))]
        + [stepped((rows, width))] * 2
        + [stepped((rows, columns))] * 2,
        out_shape=[jax.ShapeDtypeStruct((count, 2 * rows, width), jnp.bfloat16)]
        + [jax.ShapeDtypeStruct((count, rows, width), jnp.bfloat16)] * 2
        + [jax.ShapeDtypeStruct((count, rows, columns), jnp.bfloat16)] * 2,
        compiler_params=pltpu.CompilerParams(vmem_limit_bytes=VMEM_BYTES),
        cost_estimate=cost(6.5 * count),
        name="feed",
    )(*chunks, *upstreams, weights, bias[None])


def cross_forward_kernel(probe_ref, lookup_ref, content_ref, out_ref, lse_ref):
    rows = probe_ref.shape[0]
    start = (jnp.full((rows, 1), floor_value, jnp.float32), jnp.zeros((rows, PAIR), jnp.float32))
    for pair in range(lse_ref.shape[0]):
        columns = slice(pair * PAIR, (pair + 1) * PAIR)
        query = split_heads(probe_ref[:, columns] * jnp.bfloat16(HD**-0.5))
        key = lookup_ref[:, columns]
        values = split_heads(content_ref[:, columns], 1.0)
        states = [fold(start, query[side], key, values[side]) for side in range(2)]
        result, lse0, lse1 = close(*states)
        out_ref[:, columns] = result
        lse_ref[pair, 0:1, :] = lse0
        lse_ref[pair, 1:2, :] = lse1


def cross_backward_kernel(
    probe_ref,
    lookup_ref,
    content_ref,
    grad_ref,
    out_ref,
    lse_ref,
    dprobe_ref,
    dmemory_ref,
    dlookup_ref,
    dcontent_ref,
):
    query = split_heads(probe_ref[...] * jnp.bfloat16(HD**-0.5))
    key = lookup_ref[...]
    keys = split_heads(key)
    value = content_ref[...]
    whole = grad_ref[...]
    grad = split_heads(whole)
    delta = head_inner(whole.astype(jnp.float32), out_ref[...])
    terms = []
    for side in range(2):
        probs, dscores = unfold(
            query[side], key, value, grad[side], lse_ref[0, side : side + 1, :], delta[side]
        )
        terms.append(
            (
                dot(dscores, keys[side], TN),
                dot(dscores, query[side]),
                dot(probs, grad[side]),
            )
        )
    dprobe_ref[...] = ((terms[0][0] + terms[1][0]) * HD**-0.5).astype(jnp.bfloat16)
    dlookup = (terms[0][1] + terms[1][1]).astype(jnp.bfloat16)
    dcontent = (terms[0][2] + terms[1][2]).astype(jnp.bfloat16)
    rows = dmemory_ref.shape[1] // 2
    for block in range(8):
        columns = slice(block * PAIR, (block + 1) * PAIR)
        dmemory_ref[0, :rows, columns] = dlookup[block * rows : (block + 1) * rows]
        dmemory_ref[0, rows:, columns] = dcontent[block * rows : (block + 1) * rows]
    dlookup_ref[...] = dlookup
    dcontent_ref[...] = dcontent


def pair_block(rows, pairs=1):
    return pl.BlockSpec((rows, pairs * PAIR), lambda at: (0, at))


def cross_forward(probes, lookups, contents):
    rows, width = probes.shape
    memory = lookups.shape[0]
    pairs = width // PAIR
    return pl.pallas_call(
        cross_forward_kernel,
        grid=(pairs // 2,),
        out_shape=(
            jax.ShapeDtypeStruct((rows, width), jnp.float32),
            jax.ShapeDtypeStruct((pairs, 2, rows), jnp.float32),
        ),
        in_specs=[pair_block(rows, 2), pair_block(memory, 2), pair_block(memory, 2)],
        out_specs=(pair_block(rows, 2), pl.BlockSpec((2, 2, rows), lambda at: (at, 0, 0))),
        compiler_params=pltpu.CompilerParams(vmem_limit_bytes=VMEM_BYTES),
        cost_estimate=cost(10),
        name="cross_forward",
    )(probes, lookups, contents)


def cross_backward(probes, lookups, contents, grad, recalled, lse):
    rows, width = probes.shape
    memory = lookups.shape[0]
    pairs = width // PAIR
    return pl.pallas_call(
        cross_backward_kernel,
        grid=(pairs,),
        out_shape=(
            jax.ShapeDtypeStruct((rows, width), jnp.bfloat16),
            jax.ShapeDtypeStruct((pairs, 2 * memory // 8, width), jnp.bfloat16),
            jax.ShapeDtypeStruct((memory, width), jnp.bfloat16),
            jax.ShapeDtypeStruct((memory, width), jnp.bfloat16),
        ),
        in_specs=[
            pair_block(rows),
            pair_block(memory),
            pair_block(memory),
            pair_block(rows),
            pair_block(rows),
            pl.BlockSpec((1, 2, rows), lambda at: (at, 0, 0)),
        ],
        out_specs=(
            pair_block(rows),
            pl.BlockSpec((1, 2 * memory // 8, width), lambda at: (at, 0, 0)),
            pair_block(memory),
            pair_block(memory),
        ),
        compiler_params=pltpu.CompilerParams(vmem_limit_bytes=VMEM_BYTES),
        cost_estimate=cost(13),
        name="cross_backward",
    )(probes, lookups, contents, grad, recalled, lse)


def norm_parts(values):
    center = jnp.mean(values, axis=-1, keepdims=True)
    centred = values - center
    spread = jnp.mean(centred * centred, axis=-1, keepdims=True)
    rate = lax.rsqrt(spread + 1e-05)
    return centred * rate, rate


def norm_backward(grad, unit, rate, gain):
    scaled = grad * gain
    along = jnp.mean(scaled, axis=-1, keepdims=True)
    across = jnp.mean(scaled * unit, axis=-1, keepdims=True)
    return (
        rate * (scaled - along - unit * across),
        jnp.sum(grad * unit, axis=0),
        jnp.sum(grad, axis=0),
    )


def joined(group, block, side=0, sides=1):
    return (group * 4 + block) * sides + side


class Slab:
    def __init__(self):
        group, side = lax.axis_index(GRP), lax.axis_index(HEAD)
        self.group, self.side, self.block = group, side, lax.axis_index(BLK)
        column, core = group // 2, group % 2
        chips = ((0, 0), (1, 0), (1, 1), (0, 1))
        lines = [[4 * left + 2 * own + right for left, right in chips] for own in range(2)]
        self.forward = [(line[at], line[(at + 1) % 4]) for line in lines for at in range(4)]
        self.reverse = [(right, left) for left, right in self.forward]
        self.cores = [(role, role ^ 2) for role in range(8)]
        place = jnp.where(column == 0, 3 * side, 1 + side)
        owners = []
        for step, other in ((0, 0), (0, 1), (-1, 0), (1, 0), (-1, 1), (1, 1), (2, 0), (2, 1)):
            there = (place + step) % 4
            far = ((there == 1) | (there == 2)).astype(jnp.int32)
            owners.append(4 * far + 2 * ((core + other) % 2) + (there >= 2).astype(jnp.int32))
        self.lines = jnp.stack(owners).astype(jnp.int32)

    def up(self, values):
        return lax.ppermute(values, ROLE_AXES, self.forward)

    def down(self, values):
        return lax.ppermute(values, ROLE_AXES, self.reverse)

    def swap(self, values):
        return lax.ppermute(values, ROLE_AXES, self.cores)

    def gather(self, values, gates=(None, None)):
        half = values.shape[0] // 2
        left, right, other = self.up(values), self.down(values), self.swap(values)
        if gates[0] is not None:
            left, right, other = after((left, right, other), gates[0])
        pair = (self.up(left[:half]), self.down(right[half:]))
        near, far = self.swap(left), self.swap(right)
        if gates[1] is not None:
            pair, near, far = after((pair, near, far), gates[1])
        last = jnp.concatenate(pair, axis=0)
        return ((values, other), (left, right, near, far), (last, self.swap(last)))

    def scatter(self, near, after_parts, far, gates=(None, None, None)):
        low, wide = jnp.bfloat16, jnp.float32
        swaps = [self.swap(far[1]), self.swap(after_parts[2:4]), self.swap(near[1])]
        if gates[0] is not None:
            swaps = after(swaps, gates[0])
        last = far[0].astype(wide) + swaps[0]
        half = last.shape[0] // 2
        sent = (self.up(last[:half].astype(low)), self.down(last[half:].astype(low)))
        if gates[1] is not None:
            sent = after(sent, gates[1])
        self.mark = left, right = sent
        pair = after_parts[0:2].astype(wide) + swaps[1]
        behind, ahead = pair[0], pair[1]
        left = jnp.concatenate([left + ahead[:half], ahead[half:]], axis=0).astype(low)
        right = jnp.concatenate([behind[:half], right + behind[half:]], axis=0).astype(low)
        sent = (self.up(left), self.down(right))
        if gates[2] is not None:
            sent = after(sent, gates[2])
        return near[0].astype(wide) + swaps[2] + sent[0] + sent[1]

    def enter(self, values):
        moves = [
            (joined(group, block), joined(SLAB_OF[block], SLAB_OF[group]))
            for group in range(4)
            for block in range(4)
        ]
        return lax.ppermute(values, (GRP, BLK), moves)

    def leave(self, values):
        moves = [
            (joined(group, block), joined(SLAB_OF[block], SLAB_OF[group]))
            for group in range(4)
            for block in range(4)
        ]
        return lax.ppermute(values, (GRP, BLK), moves)

    def leave_columns(self, values):
        moves = [
            (joined(group, block), joined(SLAB_OF[block], COLUMN_OF[group]))
            for group in range(4)
            for block in range(4)
        ]
        return lax.ppermute(values, (GRP, BLK), moves)

    def leave_quarters(self, pieces):
        result = []
        for at, piece in enumerate(pieces):
            moves = [
                (joined(group, block), joined(SLAB_OF[block], group ^ at))
                for group in range(4)
                for block in range(4)
            ]
            result.append(lax.ppermute(piece, (GRP, BLK), moves))
        return result

    def settle(self, parts, blank):
        for at, part in enumerate(parts):
            start = (self.block ^ at,) + (0,) * part.ndim
            blank = lax.dynamic_update_slice(blank, part[None].astype(blank.dtype), start)
        return blank

    def leave_own(self, values):
        moves = [
            (joined(group, block, side, 2), joined(SLAB_OF[block], group, side, 2))
            for group in range(4)
            for block in range(4)
            for side in range(2)
        ]
        return lax.ppermute(values, ALL_AXES, moves)


def by_role(values, order=SLAB_OF):
    values = values.reshape((4, 2, -1) + values.shape[1:])
    values = jnp.stack([values[at] for at in order])
    return values.reshape((8,) + values.shape[2:])


def after(values, *others):
    return lax.optimization_barrier((values,) + others)[0]


def exchange(values, axes):
    return lax.all_to_all(values, axes, split_axis=0, concat_axis=0, tiled=True)


def columns_kernel(pieces_ref, out_ref):
    part = pieces_ref.shape[2] // 4
    for role in range(8):
        for block in range(4):
            order = (block * 2 + role % 2) * 4 + role // 2
            out_ref[:, order * part : (order + 1) * part] = pieces_ref[
                role, :, block * part : (block + 1) * part
            ].astype(jnp.float32)


def settle_columns(pieces):
    roles, rows, columns = pieces.shape
    return pl.pallas_call(
        columns_kernel,
        out_shape=jax.ShapeDtypeStruct((rows, roles * columns), jnp.float32),
        in_specs=in_vmem(1),
        out_specs=pl.BlockSpec(memory_space=pltpu.VMEM),
        compiler_params=pltpu.CompilerParams(vmem_limit_bytes=VMEM_BYTES),
        cost_estimate=cost(4),
        name="settle_columns",
    )(pieces)


def heads_kernel(pieces_ref, *outs):
    for role in range(8):
        for place, out_ref in enumerate(outs):
            out_ref[:, role * PAIR : (role + 1) * PAIR] = pieces_ref[
                role, :, place * PAIR : (place + 1) * PAIR
            ].astype(jnp.float32)


def settle_heads(pieces):
    roles, rows, columns = pieces.shape
    count = columns // PAIR
    return pl.pallas_call(
        heads_kernel,
        out_shape=(jax.ShapeDtypeStruct((rows, roles * PAIR), jnp.float32),) * count,
        in_specs=in_vmem(1),
        out_specs=tuple(in_vmem(count)),
        compiler_params=pltpu.CompilerParams(vmem_limit_bytes=VMEM_BYTES),
        cost_estimate=cost(3),
        name="settle_heads",
    )(pieces)


def head_body(
    prompt,
    continued,
    encoded,
    cont_lengths,
    self_gain,
    self_shift,
    query_weight,
    query_bias,
    key_weight,
    value_weight,
    value_bias,
    output_weight,
    output_bias,
    cross_gain,
    cross_shift,
    probe_weight,
    probe_bias,
    lookup_weight,
    content_weight,
    content_bias,
    merged_weight,
    merged_bias,
    feed_gain,
    feed_shift,
    up_weight,
    up_bias,
    down_weight,
    down_bias,
    cot_prompt,
    cot_cont,
):
    slab = Slab()
    low = jnp.bfloat16
    width = prompt.shape[1]
    shard = width // 8
    piece = shard // 4
    prompt_rows = prompt.shape[0]
    local_rows = prompt_rows + continued.shape[0]
    prompt_all = 8 * prompt_rows
    memory_rows = encoded.shape[0]
    quarter, side = slab.group, slab.side
    role = 2 * quarter + side

    swapped = [
        (joined(group, block), joined(block, SLAB_OF[group]))
        for group in range(4)
        for block in range(4)
    ]
    lengths = lax.ppermute(cont_lengths, (GRP, BLK), swapped)
    bounds = jnp.cumsum(lengths).astype(jnp.int32)

    own_all = slab.enter(jnp.concatenate([prompt, continued, encoded], axis=0))

    def head_columns(weight):
        mine = lax.dynamic_slice_in_dim(weight.reshape(shard, 4, 2 * shard), quarter, 1, axis=1)
        return mine.reshape(shard, 2, shard).transpose(1, 0, 2)

    small = (
        self_gain,
        self_shift,
        output_bias,
        cross_gain,
        cross_shift,
        probe_bias,
        merged_bias,
        feed_gain,
        feed_shift,
        down_bias,
        content_bias,
        query_bias,
        value_bias,
    )
    vectors = jnp.concatenate(small + (up_bias,) + (self_gain,) * 3).reshape(1, 8, 3 * shard)
    mixed_in = jnp.concatenate(
        [
            jnp.concatenate(
                [head_columns(query_weight), head_columns(key_weight), head_columns(value_weight)],
                axis=2,
            ),
            jnp.broadcast_to(vectors, (2, 8, 3 * shard)),
        ],
        axis=1,
    )
    mixed_in = jnp.broadcast_to(mixed_in[None], (4,) + mixed_in.shape)
    mixed_in = exchange(mixed_in.reshape(8, shard + 8, 3 * shard), ROW_AXES)
    own_all, mixed_in = lax.optimization_barrier((own_all, mixed_in))
    head_weights = mixed_in[:, :shard].reshape(width, 3 * shard)
    vectors = mixed_in[:, shard:].reshape(8, 24, shard)
    packed = vectors[:, : len(small)].transpose(1, 0, 2).reshape(len(small), width)
    (
        self_gain_full,
        self_shift_full,
        output_bias_full,
        cross_gain_full,
        cross_shift_full,
        probe_bias_full,
        merged_bias_full,
        feed_gain_full,
        feed_shift_full,
        down_bias_full,
        content_bias_full,
        query_bias_full,
        value_bias_full,
    ) = [packed[at].astype(jnp.float32) for at in range(len(small))]
    ups = vectors[:, len(small) : len(small) + 8].reshape(4, 2, 4, -1)
    ups = lax.dynamic_index_in_dim(ups, side, 1, keepdims=False)
    up_bias_own = lax.dynamic_index_in_dim(ups, quarter, 1, keepdims=False).reshape(width)
    up_bias_own = up_bias_own.astype(jnp.float32)

    row_groups = slab.gather(own_all)
    up_mine = lax.dynamic_index_in_dim(
        up_weight.reshape(shard, 4, 2, 4, -1), quarter, 3, keepdims=False
    )
    up_mine = up_mine.transpose(2, 0, 1, 3).reshape(2, shard, width)
    up_mine = exchange(after(up_mine, own_all), HEAD).reshape(2 * shard, width)
    down_mine = lax.dynamic_slice_in_dim(down_weight, quarter * 2 * shard, 2 * shard, axis=0)

    squares = (output_weight, probe_weight, merged_weight, lookup_weight, content_weight)
    shared = jnp.concatenate(
        [lax.dynamic_slice_in_dim(weight, quarter * piece, piece, axis=0) for weight in squares],
        axis=0,
    )
    shared = after(shared, own_all)
    shared = lax.all_gather(shared, (BLK, HEAD, GRP), axis=0, tiled=False)
    shared = shared.reshape(32, len(squares), piece, width)
    output_full, probe_full, merged_full, lookup_full, content_full = [
        shared[:, at].reshape(width, width) for at in range(len(squares))
    ]

    rows = own_all[:local_rows].astype(jnp.float32)

    def own_columns(vector):
        return lax.dynamic_slice_in_dim(vector, role * shard, shard, axis=0)

    head_bias = jnp.concatenate(
        [
            own_columns(query_bias_full),
            jnp.zeros((shard,), jnp.float32),
            own_columns(value_bias_full),
        ]
    )
    projected = [
        project(group, local_rows, self_gain_full, self_shift_full, head_weights, head_bias)
        for group in row_groups
    ]
    upstream = slab.enter(
        after(jnp.concatenate([cot_prompt, cot_cont], axis=0), own_all)
    )
    feed_weights = jnp.concatenate([up_mine, down_mine], axis=0)
    feed_weights = lax.all_gather(feed_weights, BLK, axis=0, tiled=False)
    head_groups = [pair[1] for pair in projected]
    attended, attended_low, logsum = self_forward(slab.lines, bounds, head_groups, prompt_all)
    upstream_groups = slab.gather(
        after(upstream, row_groups[2]), (head_groups[2], attended_low)
    )
    mixed = exchange(attended_low, ROLE_AXES).transpose(1, 0, 2).reshape(local_rows, width)
    first = rows + matmul(mixed, output_full) + output_bias_full
    first_unit, first_rate = norm_parts(first)
    normed_cross = (first_unit * cross_gain_full + cross_shift_full).astype(low)
    probes = (matmul(normed_cross, probe_full) + probe_bias_full).astype(low)

    memory = jnp.zeros((8 * memory_rows, width), low)
    chunks = [chunk for group in row_groups for chunk in group]
    for at, chunk in enumerate(chunks):
        memory = lax.dynamic_update_slice_in_dim(
            memory, chunk[local_rows:], slab.lines[at] * memory_rows, axis=0
        )
    lookups = matmul(memory, lookup_full).astype(low)
    contents = (matmul(memory, content_full) + content_bias_full).astype(low)
    recalled, cross_logsum = cross_forward(probes, lookups, contents)
    recalled_low = recalled.astype(low)
    second = first + matmul(recalled_low, merged_full) + merged_bias_full
    second_unit, second_rate = norm_parts(second)
    normed_feed = (second_unit * feed_gain_full + feed_shift_full).astype(low)

    fed = [
        feed(group, upstream_group, feed_weights, up_bias_own)
        for group, upstream_group in zip(slab.gather(normed_feed), upstream_groups)
    ]
    dnormed_feed = slab.scatter(*[parts[0] for parts in fed])
    output = second + dnormed_feed[local_rows:] + down_bias_full
    dnormed_feed = dnormed_feed[:local_rows]

    kept = after([parts[1:] for parts in fed], slab.mark)

    def summed(left, right):
        return sum(
            left_product(parts[left].reshape(-1, width), parts[right].reshape(-1, width))
            for parts in kept
        ).astype(low)

    down_gradient = summed(2, 1).reshape(4, 2 * shard, width)
    up_sum = sum(column_sum(parts[3].reshape(-1, width)) for parts in kept).astype(low)
    up_sum = jnp.broadcast_to(
        jnp.pad(up_sum.reshape(4, 1, 2 * shard), ((0, 0), (0, 0), (0, width - 2 * shard))),
        (4, 16, width),
    )
    down_gradient = jnp.concatenate([down_gradient, up_sum], axis=1)
    down_gradient = after(down_gradient, dnormed_feed)
    down_gradient = slab.leave_quarters(
        [
            lax.dynamic_index_in_dim(down_gradient, quarter ^ at, 0, keepdims=False)
            for at in range(4)
        ]
    )
    up_gradient = after(by_role(summed(0, 3), COLUMN_OF), dnormed_feed)
    up_gradient = exchange(up_gradient, ROLE_AXES)

    part, feed_gain_sum, feed_shift_sum = norm_backward(
        dnormed_feed, second_unit, second_rate, feed_gain_full
    )
    dsecond = upstream.astype(jnp.float32) + part
    dsecond_low = dsecond.astype(low)
    drecalled = right_product(dsecond_low, merged_full).astype(low)
    dprobes, dmemory, dlookups, dcontents = cross_backward(
        probes, lookups, contents, drecalled, recalled, cross_logsum
    )
    encoded_gradient = right_product(dlookups, lookup_full) + right_product(
        dcontents, content_full
    )
    encoded_gradient = encoded_gradient.astype(low)
    dnormed_cross = right_product(after(dprobes, (up_gradient, down_gradient)), probe_full)
    part, cross_gain_sum, cross_shift_sum = norm_backward(
        dnormed_cross, first_unit, first_rate, cross_gain_full
    )
    dfirst = dsecond + part
    dfirst_low = dfirst.astype(low)
    dmixed = right_product(dfirst_low, output_full).astype(low)
    dmixed = dmixed.reshape(local_rows, 8, shard).transpose(1, 0, 2)
    dmixed = exchange(dmixed, ROLE_AXES)
    up_gradient = slab.leave_columns(after(up_gradient, dmixed))

    sums = jnp.stack(
        (
            column_sum(dfirst_low),
            cross_gain_sum,
            cross_shift_sum,
            column_sum(dprobes),
            column_sum(dsecond_low),
            feed_gain_sum,
            feed_shift_sum,
            column_sum(upstream),
        )
    )
    sums = by_role(sums.T).transpose(0, 2, 1).reshape(8, 1, width)
    sums = jnp.broadcast_to(sums, (8, 16, width))
    scattered = jnp.concatenate(
        [
            by_role(left_product(recalled_low, dsecond_low).astype(low)),
            by_role(left_product(normed_cross, dprobes).astype(low)),
            encoded_gradient.reshape(8, memory_rows, width),
            by_role(left_product(mixed, dfirst_low).astype(low)),
            sums.astype(low),
            dmemory,
        ],
        axis=1,
    )
    scattered = lax.psum_scatter(scattered, ROLE_AXES, scatter_dimension=0, tiled=False)

    dhead_groups = self_backward(
        slab.lines, bounds, head_groups, dmixed, attended, logsum, prompt_all
    )
    done = dhead_groups[0]
    output = slab.leave(after(output.astype(low), done))

    dnormed = slab.scatter(
        *[
            right_product(group.reshape(-1, 3 * shard), head_weights)
            .astype(low)
            .reshape(group.shape[0], local_rows, width)
            for group in dhead_groups
        ]
    )

    up_gradient, down_gradient, scattered = after(
        (up_gradient, down_gradient, scattered), done
    )
    up_weight_gradient = settle_columns(up_gradient)
    down_weight_gradient = slab.settle(
        [part[: 2 * shard] for part in down_gradient], jnp.zeros((4, 2 * shard, width), jnp.float32)
    ).reshape(width, width)
    up_bias_gradient = slab.settle(
        [part[2 * shard, : 2 * shard] for part in down_gradient],
        jnp.zeros((4, 2 * shard), jnp.float32),
    ).reshape(width)

    encoded_end = 2 * shard + memory_rows
    squares_end = encoded_end + shard + 16
    mine_dmemory = scattered[squares_end:].reshape(2, memory_rows, 8, shard)
    mine_dmemory = mine_dmemory.transpose(0, 2, 1, 3)
    mine_dmemory = mine_dmemory.reshape(2, 8 * memory_rows, shard)

    head_gradient = [
        sum(
            left_product(normed.reshape(-1, width), group.reshape(-1, 3 * shard))
            for (normed, unused), group in zip(projected, dhead_groups)
        ),
        left_product(memory, mine_dmemory[0]),
        left_product(memory, mine_dmemory[1]),
    ]
    head_gradient = jnp.concatenate([part.astype(low) for part in head_gradient], axis=1)
    head_gradient = exchange(by_role(head_gradient, COLUMN_OF), ROLE_AXES)
    (
        query_weight_gradient,
        key_weight_gradient,
        value_weight_gradient,
        lookup_weight_gradient,
        content_weight_gradient,
    ) = settle_heads(slab.leave_columns(head_gradient))
    head_sums = sum(column_sum(group.reshape(-1, 3 * shard)) for group in dhead_groups)
    head_sums = slab.leave_own(
        jnp.stack([head_sums[:shard], head_sums[2 * shard :], column_sum(mine_dmemory[1])])
    )
    unit, rate = norm_parts(rows)
    part, self_gain_sum, self_shift_sum = norm_backward(dnormed, unit, rate, self_gain_full)
    row_gradient = jnp.concatenate([(dfirst + part).astype(low), scattered[:squares_end]], axis=0)
    row_gradient = slab.leave(row_gradient).astype(jnp.float32)
    square_gradient = row_gradient[local_rows:]
    merged_weight_gradient = square_gradient[:shard]
    probe_weight_gradient = square_gradient[shard : 2 * shard]
    encoded_gradient = square_gradient[2 * shard : encoded_end]
    output_weight_gradient = square_gradient[encoded_end : encoded_end + shard]
    small_sums = square_gradient[encoded_end + shard].reshape(8, shard)
    (
        output_bias_gradient,
        cross_gain_gradient,
        cross_shift_gradient,
        probe_bias_gradient,
        merged_bias_gradient,
        feed_gain_gradient,
        feed_shift_gradient,
        down_bias_gradient,
    ) = [small_sums[at] for at in range(8)]

    sums = after(jnp.stack((self_gain_sum, self_shift_sum), axis=1), head_gradient)
    sums = by_role(sums)
    sums = jnp.sum(exchange(sums.transpose(0, 2, 1), ROLE_AXES), axis=0)
    sums = slab.leave(sums)
    up_bias_gradient = up_bias_gradient.reshape(-1)
    query_bias_gradient, value_bias_gradient, content_bias_gradient = [
        head_sums[at] for at in range(3)
    ]
    self_gain_gradient, self_shift_gradient = sums[0], sums[1]

    return (
        (
            output[:prompt_rows],
            output[prompt_rows:],
            row_gradient[:prompt_rows],
            row_gradient[prompt_rows:local_rows],
            encoded_gradient,
            self_gain_gradient,
            self_shift_gradient,
            query_weight_gradient,
            query_bias_gradient,
            key_weight_gradient,
            value_weight_gradient,
            value_bias_gradient,
            output_weight_gradient,
            output_bias_gradient,
            cross_gain_gradient,
            cross_shift_gradient,
            probe_weight_gradient,
            probe_bias_gradient,
            lookup_weight_gradient,
            content_weight_gradient,
            content_bias_gradient,
            merged_weight_gradient,
            merged_bias_gradient,
            feed_gain_gradient,
            feed_shift_gradient,
            up_weight_gradient,
            up_bias_gradient,
            down_weight_gradient,
            down_bias_gradient,
        )
    )


def solution(mesh):
    rows, group = P(ALL_AXES, None), P(ALL_AXES)
    weight, vector = P(ROW_AXES, None), P(ROW_AXES)
    ranks = [2 if "weight" in name else 1 for name in PARAM_NAMES]
    sizes = tuple(mesh.shape[axis] for axis in ALL_AXES)
    return jax.shard_map(
        head_body if sizes == (4, 4, 2) and HEADS * HD == 8 * PAIR else token_body,
        mesh=mesh,
        in_specs=(rows, rows, rows, P(GRP))
        + tuple(weight if rank == 2 else vector for rank in ranks)
        + (rows, rows),
        out_specs=(rows,) * 5 + tuple(rows if rank == 2 else group for rank in ranks),
        check_vma=False,
    )
```
